32 devices in a mesh: mp: 4 (over x, core), fsdp: 2 (over y), dp: 4 (over z).
Axes of the slice: x: 2, y: 2, z: 4, core: 2. Of those that a mesh axis runs over, the one named last changes fastest.
Arguments:
- gen_noise: float32 [4, 512, 128], P('dp', 'fsdp'), may hold values from -6 to 6
- renoise: float32 [4, 512, 128], P('dp', 'fsdp'), may hold values from -120 to 120
- gen_step: int32 [4], P('dp'), may hold values from 250 to 999
- renoise_step: int32 [4], P('dp'), may hold values from 20 to 979
- text_pooled: bfloat16 [4, 768], P('dp'), may hold values from -6 to 6
- embed: bfloat16 [3, 64, 3072], replicated, may hold values from -0.75 to 0.75
- mod_weight: bfloat16 [3, 1024, 6144], P(None, None, 'fsdp'), may hold values from -0.1875 to 0.1875
- proj_weight: bfloat16 [3, 3072, 3072], P(None, 'fsdp', 'mp'), may hold values from -0.109375 to 0.109375
- unembed: bfloat16 [3, 64, 3072], P(None, None, 'mp'), may hold values from -0.109375 to 0.109375
Outputs:
- gen_grad: float32 [3072, 3072], P('fsdp', 'mp')
- score_gap: float32 [4, 512, 128], P('dp', 'fsdp')
The draws below stay inside these ranges and needn't reach their ends.
All inputs are finite; a program needn't handle non-finite values. Where the reference program divides by a largest or mean magnitude, that divisor is 1e-20 or more.
Results may differ from the reference program's by a relative error of at most 0.03.
Values may be sent and summed in bfloat16 or wider, within the bound.
No kernel may reach another device: no remote copies, remote signals or barrier semaphores. Data moves between devices by JAX's collectives and lax.ppermute only.
A program may use at most 128 MiB of HBM per device.

```python
import math
import jax
import jax.numpy as jnp
from jax import lax

D = 3072
CH = 64
TXT = 768
TEMB = 256
SEQ = 1024
BATCH = 4
TOKENS = 4096


def draw_renoise(key, part):
    row_key, col_key, base_key = jax.random.split(key, 3)
    pair_rows = SEQ // 2
    position = jnp.arange(pair_rows, dtype=jnp.float32) / pair_rows
    row_factor = jnp.exp(jax.random.uniform(row_key, (BATCH, pair_rows, 1), minval=0.0, maxval=math.log(3.3)))
    col_factor = jnp.exp(jax.random.uniform(col_key, (1, 1, 2 * CH), minval=0.0, maxval=math.log(10.0)))
    rising = jnp.exp(math.log(3.0) * position)[None, :, None]
    base_vals = jnp.clip(jax.random.normal(base_key, (BATCH, pair_rows, 2 * CH)), -6.0, 6.0)
    return (0.2 * base_vals * rising * row_factor * col_factor).astype(jnp.float32)


def set_ends(values, rng, low, top_value):
    dims = values.shape
    place = [jax.random.randint(jax.random.fold_in(rng, axis), (), 0, dims[axis]) for axis in range(len(dims))]
    values = values.at[tuple(place)].set(low)
    longest = dims.index(max(dims))
    place[longest] = (place[longest] + 1) % dims[longest]
    return values.at[tuple(place)].set(top_value)


def level_of(stream_key, extent, cuts, smallest, largest):
    level, own = 1.0, jax.random.fold_in(stream_key, 6)
    for axis_at, shards_of in cuts:
        steps = jnp.exp(jax.random.uniform(jax.random.fold_in(own, axis_at), (shards_of,), jnp.float32, smallest / len(cuts), largest / len(cuts)))
        level = level * jnp.repeat(steps, extent[axis_at] // shards_of).reshape([-1 if axis == axis_at else 1 for axis in range(len(extent))])
    return level


def gaussian(stream_key, dims, width, reach, cuts=(), held_as=jnp.bfloat16):
    loudness = level_of(stream_key, dims, cuts, -0.22, 0.18) if cuts else 1.0
    drawn = jax.random.normal(stream_key, dims, jnp.float32) * width * loudness
    return jnp.minimum(jnp.maximum(drawn, -reach), reach).astype(held_as)


def setup_inputs(seed: int = 0) -> dict:
    seeds = jax.random.split(jax.random.key(seed), 10)
    gen_noise = gaussian(seeds[0], (BATCH, SEQ // 2, 2 * CH), 1.0, 6.0, ((0, 4), (1, 2)), jnp.float32)
    renoise = draw_renoise(jax.random.fold_in(seeds[9], 71), 0)
    gen_step = set_ends(jax.random.randint(seeds[2], (BATCH,), 250, 1000), jax.random.fold_in(seeds[2], 1), 250, 999).astype(jnp.int32)
    renoise_step = set_ends(jax.random.randint(seeds[3], (BATCH,), 20, 980), jax.random.fold_in(seeds[3], 1), 20, 979).astype(jnp.int32)
    text_pooled = gaussian(seeds[4], (BATCH, TXT), 1.0, 6.0, ((0, 4),))
    embed = gaussian(seeds[5], (3, CH, D), CH ** -0.5, 0.75)
    mod_weight = gaussian(seeds[6], (3, TEMB + TXT, 2 * D), (TEMB + TXT) ** -0.5, 0.1875, ((2, 2),))
    proj_weight = gaussian(seeds[7], (3, D, D), D ** -0.5, 0.109375, ((1, 2), (2, 4)))
    unembed = gaussian(seeds[8], (3, CH, D), D ** -0.5, 0.109375, ((2, 4),))
    return {"gen_noise": gen_noise, "renoise": renoise, "gen_step": gen_step, "renoise_step": renoise_step, "text_pooled": text_pooled, "embed": embed, "mod_weight": mod_weight, "proj_weight": proj_weight, "unembed": unembed}


GUIDANCE = 3.5
EPS_NORM = 1e-06
EPS_GAP = 1e-05

def sinusoid(timesteps):
    half_size = TEMB // 2
    frequency = jnp.exp(-math.log(10000.0) * jnp.arange(half_size, dtype=jnp.float32) / half_size)
    angles = timesteps.astype(jnp.float32)[:, None] * frequency[None, :]
    return jnp.concatenate([jnp.cos(angles), jnp.sin(angles)], axis=1)

def condition(timesteps, pooled):
    joined = jnp.concatenate([sinusoid(timesteps), pooled.astype(jnp.float32)], axis=1)
    return jax.nn.silu(joined).astype(jnp.bfloat16)

def normalize(values):
    average = lax.optimization_barrier(jnp.mean(values, axis=1, keepdims=True))
    centred = values - average
    variance = lax.optimization_barrier(jnp.mean(centred * centred, axis=1, keepdims=True))
    return centred * lax.rsqrt(variance + EPS_NORM)

def modulate(normed, modulation):
    return (normed * (1.0 + modulation[D:]) + modulation[:D]).astype(jnp.bfloat16)

def finish(embedded, hidden, weight, out_weight):
    summed = embedded + jnp.dot(hidden, weight, preferred_element_type=jnp.float32)
    return jnp.dot(summed.astype(jnp.bfloat16), out_weight.T, preferred_element_type=jnp.float32)

def reference(gen_noise, renoise, gen_step, renoise_step, text_pooled, embed, mod_weight, proj_weight, unembed):
    blank_text = jnp.zeros_like(text_pooled)
    noisy_vec = condition(renoise_step, text_pooled)
    gen_mod = jnp.dot(condition(gen_step, text_pooled), mod_weight[0], preferred_element_type=jnp.float32)
    cond_mod = jnp.dot(noisy_vec, mod_weight[1], preferred_element_type=jnp.float32)
    blank_mod = jnp.dot(condition(renoise_step, blank_text), mod_weight[1], preferred_element_type=jnp.float32)
    fake_mod = jnp.dot(noisy_vec, mod_weight[2], preferred_element_type=jnp.float32)
    levels = renoise_step.astype(jnp.float32) / 1000.0

    def one_sample(grad_sum, sample_items):
        noise_in, noise_out, gen_row, cond_row, blank_row, fake_row, noise_level = sample_items
        latent = noise_in.reshape(SEQ, CH)
        embedded = jnp.dot(latent.astype(jnp.bfloat16), embed[0], preferred_element_type=jnp.float32)
        gen_hidden = modulate(normalize(embedded), gen_row)
        clean_lat = finish(embedded, gen_hidden, proj_weight[0], unembed[0])
        noisy_lat = (1.0 - noise_level) * clean_lat + noise_level * noise_out.reshape(SEQ, CH)
        noisy_bf = noisy_lat.astype(jnp.bfloat16)
        teacher_in = jnp.dot(noisy_bf, embed[1], preferred_element_type=jnp.float32)
        teacher_norm = normalize(teacher_in)
        cond_out = finish(teacher_in, modulate(teacher_norm, cond_row), proj_weight[1], unembed[1])
        blank_out = finish(teacher_in, modulate(teacher_norm, blank_row), proj_weight[1], unembed[1])
        fake_in = jnp.dot(noisy_bf, embed[2], preferred_element_type=jnp.float32)
        fake_out = finish(fake_in, modulate(normalize(fake_in), fake_row), proj_weight[2], unembed[2])
        real_pred = noisy_lat - noise_level * (blank_out + GUIDANCE * (cond_out - blank_out))
        fake_pred = noisy_lat - noise_level * fake_out
        gap_scale = jnp.mean(jnp.abs(clean_lat - real_pred)) + EPS_GAP
        score_rows = (fake_pred - real_pred) / gap_scale
        cotangent = (score_rows / math.sqrt(TOKENS)).astype(jnp.bfloat16)
        upstream = jnp.dot(cotangent, unembed[0], preferred_element_type=jnp.float32).astype(jnp.bfloat16)
        grad_sum = grad_sum + lax.dot_general(gen_hidden, upstream, (((0,), (0,)), ((), ())), preferred_element_type=jnp.float32)
        return (grad_sum, score_rows.reshape(SEQ // 2, 2 * CH))
    grad_start = jnp.zeros((D, D), jnp.float32)
    gen_grad, score_gap = lax.scan(one_sample, grad_start, (gen_noise, renoise, gen_mod, cond_mod, blank_mod, fake_mod, levels))
    return (gen_grad, score_gap)
```

```python
import math

import jax
import jax.numpy as jnp
from jax import lax
from jax.sharding import PartitionSpec as P

D = 3072
CH = 64
TEMB = 256

GUIDANCE = 3.5
EPS_NORM = 1e-06
EPS_GAP = 1e-05
HI = lax.Precision.HIGHEST


def sinusoid(timesteps):
    half_size = TEMB // 2
    frequency = jnp.exp(-math.log(10000.0) * jnp.arange(half_size, dtype=jnp.float32) / half_size)
    angles = timesteps.astype(jnp.float32)[:, None] * frequency[None, :]
    return jnp.concatenate([jnp.cos(angles), jnp.sin(angles)], axis=1)


def condition(timesteps, pooled):
    joined = jnp.concatenate([sinusoid(timesteps), pooled.astype(jnp.float32)], axis=1)
    return jax.nn.silu(joined).astype(jnp.bfloat16)


def swap(x, axes, mask):
    count = lax.axis_size(axes)
    return lax.ppermute(x, axes, [(i, i ^ mask) for i in range(count)])


def plane_sum(x):
    if lax.axis_size("mp") != 4 or lax.axis_size("fsdp") != 2:
        return lax.psum(x, ("mp", "fsdp"))
    x = x + swap(x, "mp", 1)
    plane = ("mp", "fsdp")
    parts = [swap(x, plane, mask) for mask in (4, 1, 5)]
    return (x + parts[0]) + (parts[1] + parts[2])


def gather_samples(x):
    count = lax.axis_size("dp")
    if lax.axis_size("mp") != 4 or count != 4:
        blocks = lax.all_gather(x, "dp")
        return [blocks[i] for i in range(count)]
    pairs = []
    for m in range(4):
        for s in range(4):
            pairs.append((m * 4 + s, m * 4 + (s ^ (1 if m % 2 == 0 else 2))))
    near = lax.ppermute(x, ("mp", "dp"), pairs)
    far = swap(x, "dp", 3)
    return [x, near, swap(near, "mp", 1), far]


def exchange_modulation(local_mod, rows):
    if lax.axis_size("fsdp") == 2:
        f = lax.axis_index("fsdp")
        mine = lax.dynamic_slice_in_dim(local_mod, f * rows, rows, 1)
        theirs = swap(lax.dynamic_slice_in_dim(local_mod, (1 - f) * rows, rows, 1), "fsdp", 1)
        return jnp.where(f == 0, mine, theirs), jnp.where(f == 0, theirs, mine)
    whole = lax.all_gather(local_mod, "fsdp", axis=1, tiled=True)
    start = lax.axis_index("fsdp") * rows
    return (
        lax.dynamic_slice_in_dim(whole[:, :D], start, rows, 1),
        lax.dynamic_slice_in_dim(whole[:, D:], start, rows, 1),
    )


def dot(a, b, precision=HI):
    return jnp.dot(a, b, precision=precision, preferred_element_type=jnp.float32)


def both(x):
    zero = jnp.zeros_like(x)
    return jnp.concatenate(
        [jnp.concatenate([x, zero], 1), jnp.concatenate([zero, x], 1)], 0
    )


def body(
    gen_noise, renoise, gen_step, renoise_step, text_pooled, embed, mod_weight, proj_weight, unembed
):
    rows, cols = proj_weight.shape[1], proj_weight.shape[2]
    f = lax.axis_index("fsdp")
    noise_all = lax.all_gather(gen_noise[0], "fsdp", axis=0, tiled=True)
    renoise_all = lax.all_gather(renoise[0], "fsdp", axis=0, tiled=True)

    blank_text = jnp.zeros_like(text_pooled)
    gen_vec = condition(gen_step, text_pooled)
    real_vec = jnp.concatenate(
        [condition(renoise_step, text_pooled), condition(renoise_step, blank_text)], 0
    )
    teacher_mod = jnp.dot(real_vec, mod_weight[1], preferred_element_type=jnp.float32)
    local_mod = jnp.concatenate(
        [
            jnp.dot(gen_vec, mod_weight[0], preferred_element_type=jnp.float32),
            GUIDANCE * teacher_mod[0:1] + (1.0 - GUIDANCE) * teacher_mod[1:2],
            jnp.dot(real_vec[0:1], mod_weight[2], preferred_element_type=jnp.float32),
        ],
        axis=0,
    )
    shift, scale = exchange_modulation(local_mod, rows)

    centred = embed.astype(jnp.float32)
    centred = centred - jnp.mean(centred, axis=2, keepdims=True)
    gram = [dot(centred[m], centred[m].T) / D for m in range(3)]
    centred_rows = lax.dynamic_slice_in_dim(centred, f * rows, rows, 2)
    embed_cols = lax.dynamic_slice_in_dim(embed, lax.axis_index("mp") * cols, cols, 2)

    pieces = []
    for m in range(3):
        through = lax.dot_general(
            proj_weight[m], unembed[m], (((1,), (1,)), ((), ())), preferred_element_type=jnp.float32
        )
        direct = lax.dot_general(
            embed_cols[m], unembed[m], (((1,), (1,)), ((), ())), preferred_element_type=jnp.float32
        )
        direct = jnp.where(f == 0, direct, 0.0)
        modulated = dot(centred_rows[m] * (1.0 + scale[m : m + 1]), through)
        offset = dot(shift[m : m + 1], through)
        offset = jnp.concatenate([offset, jnp.zeros((7, CH), jnp.float32)], 0)
        pieces.append(
            jnp.concatenate(
                [
                    jnp.concatenate([direct, modulated], 1),
                    jnp.concatenate([offset, jnp.zeros_like(offset)], 1),
                ],
                0,
            )
        )
    maps = plane_sum(jnp.concatenate(pieces, 0)).reshape(3, CH + 8, 2 * CH)
    direct = [both(maps[m, :CH, :CH]) for m in range(3)]
    modulated = [both(maps[m, :CH, CH:]) for m in range(3)]
    offset = [jnp.concatenate([maps[m, CH : CH + 1, :CH]] * 2, 1) for m in range(3)]

    ones = both(jnp.ones((CH, CH), jnp.float32))

    def normalized(u, m):
        spread = dot(dot(u, both(gram[m])) * u, ones)
        return u * lax.rsqrt(jnp.maximum(spread, 0.0) + EPS_NORM)

    def model(u, u_norm, m):
        return dot(u, direct[m]) + dot(u_norm, modulated[m]) + offset[m]

    noise = noise_all.astype(jnp.bfloat16).astype(jnp.float32)
    noise_norm = normalized(noise, 0)
    clean = model(noise, noise_norm, 0)
    level = renoise_step[0].astype(jnp.float32) / 1000.0
    noisy = (1.0 - level) * clean + level * renoise_all
    noisy = noisy.astype(jnp.bfloat16).astype(jnp.float32)
    real_v = model(noisy, normalized(noisy, 1), 1)
    fake_v = model(noisy, normalized(noisy, 2), 2)
    total = jnp.sum(jnp.abs(clean - renoise_all + real_v))
    gap_scale = level * total / (noise_all.shape[0] * 2 * CH) + EPS_GAP
    score = level * (real_v - fake_v) / gap_scale
    local_rows = gen_noise.shape[1]
    score_gap = lax.dynamic_slice_in_dim(score, f * local_rows, local_rows, 0)

    all_tokens = noise_all.shape[0] * 2 * lax.axis_size("dp")
    cotangent = (score / math.sqrt(all_tokens)).astype(jnp.bfloat16).astype(jnp.float32)
    pairs = dot(noise_norm.T, cotangent)
    outer = pairs[:CH, :CH] + pairs[CH:, CH:]
    sums = jnp.sum(cotangent, axis=0)
    sums = sums[:CH] + sums[CH:]
    payload = jnp.concatenate(
        [
            jnp.pad(outer, ((0, 0), (0, CH))),
            jnp.pad(sums[None], ((0, 7), (0, CH))),
            jnp.concatenate([shift[0], scale[0]]).reshape(-1, 2 * CH),
        ],
        0,
    )
    blocks = gather_samples(payload)
    grad_map = jnp.zeros((CH, rows), jnp.float32)
    for block in blocks:
        block_mod = block[CH + 8 :].reshape(2, rows)
        grad_map += dot(block[:CH, :CH].T, centred_rows[0]) * (1.0 + block_mod[1:2])
        grad_map += block[CH, :CH][:, None] * block_mod[0:1]
    gen_grad = lax.dot_general(
        grad_map.astype(jnp.bfloat16),
        unembed[0],
        (((0,), (0,)), ((), ())),
        preferred_element_type=jnp.float32,
    )
    return (gen_grad, score_gap[None])


def solution(mesh):
    return jax.shard_map(
        body,
        mesh=mesh,
        in_specs=(
            P("dp", "fsdp", None),
            P("dp", "fsdp", None),
            P("dp"),
            P("dp"),
            P("dp", None),
            P(),
            P(None, None, "fsdp"),
            P(None, "fsdp", "mp"),
            P(None, None, "mp"),
        ),
        out_specs=(P("fsdp", "mp"), P("dp", "fsdp", None)),
        check_vma=False,
    )
```

```python
import math

import jax
import jax.numpy as jnp
from jax import lax
from jax.experimental import pallas as pl
from jax.experimental.pallas import tpu as pltpu
from jax.sharding import PartitionSpec as P

D = 3072
CH = 64
TEMB = 256

GUIDANCE = 3.5
EPS_NORM = 1e-06
EPS_GAP = 1e-05
HI = lax.Precision.HIGHEST


def sinusoid(timesteps):
    half_size = TEMB // 2
    frequency = jnp.exp(-math.log(10000.0) * jnp.arange(half_size, dtype=jnp.float32) / half_size)
    angles = timesteps.astype(jnp.float32)[:, None] * frequency[None, :]
    return jnp.concatenate([jnp.cos(angles), jnp.sin(angles)], axis=1)


def condition(timesteps, pooled):
    joined = jnp.concatenate([sinusoid(timesteps), pooled.astype(jnp.float32)], axis=1)
    return jax.nn.silu(joined).astype(jnp.bfloat16)


def swap(x, axes, mask):
    count = lax.axis_size(axes)
    return lax.ppermute(x, axes, [(i, i ^ mask) for i in range(count)])


def plane_sum(x):
    if lax.axis_size("mp") != 4 or lax.axis_size("fsdp") != 2:
        return lax.psum(x, ("mp", "fsdp"))
    x = x + swap(x, "mp", 1)
    plane = ("mp", "fsdp")
    parts = [swap(x, plane, mask) for mask in (4, 1, 5)]
    return (x + parts[0]) + (parts[1] + parts[2])


def gather_samples(x):
    count = lax.axis_size("dp")
    if lax.axis_size("mp") != 4 or count != 4:
        blocks = lax.all_gather(x, "dp")
        return [blocks[i] for i in range(count)]
    pairs = []
    for m in range(4):
        for s in range(4):
            pairs.append((m * 4 + s, m * 4 + (s ^ (1 if m % 2 == 0 else 2))))
    near = lax.ppermute(x, ("mp", "dp"), pairs)
    far = swap(x, "dp", 3)
    return [x, near, swap(near, "mp", 1), far]


def exchange_modulation(local_mod, rows):
    if lax.axis_size("fsdp") == 2:
        f = lax.axis_index("fsdp")
        mine = lax.dynamic_slice_in_dim(local_mod, f * rows, rows, 1)
        theirs = swap(lax.dynamic_slice_in_dim(local_mod, (1 - f) * rows, rows, 1), "fsdp", 1)
        return jnp.where(f == 0, mine, theirs), jnp.where(f == 0, theirs, mine)
    whole = lax.all_gather(local_mod, "fsdp", axis=1, tiled=True)
    start = lax.axis_index("fsdp") * rows
    return (
        lax.dynamic_slice_in_dim(whole[:, :D], start, rows, 1),
        lax.dynamic_slice_in_dim(whole[:, D:], start, rows, 1),
    )


def dot(a, b, precision=HI):
    return jnp.dot(a, b, precision=precision, preferred_element_type=jnp.float32)


def both(x):
    zero = jnp.zeros_like(x)
    return jnp.concatenate(
        [jnp.concatenate([x, zero], 1), jnp.concatenate([zero, x], 1)], 0
    )


def plain_body(
    gen_noise, renoise, gen_step, renoise_step, text_pooled, embed, mod_weight, proj_weight, unembed
):
    rows, cols = proj_weight.shape[1], proj_weight.shape[2]
    f = lax.axis_index("fsdp")
    noise_all = lax.all_gather(gen_noise[0], "fsdp", axis=0, tiled=True)
    renoise_all = lax.all_gather(renoise[0], "fsdp", axis=0, tiled=True)

    blank_text = jnp.zeros_like(text_pooled)
    gen_vec = condition(gen_step, text_pooled)
    real_vec = jnp.concatenate(
        [condition(renoise_step, text_pooled), condition(renoise_step, blank_text)], 0
    )
    teacher_mod = jnp.dot(real_vec, mod_weight[1], preferred_element_type=jnp.float32)
    local_mod = jnp.concatenate(
        [
            jnp.dot(gen_vec, mod_weight[0], preferred_element_type=jnp.float32),
            GUIDANCE * teacher_mod[0:1] + (1.0 - GUIDANCE) * teacher_mod[1:2],
            jnp.dot(real_vec[0:1], mod_weight[2], preferred_element_type=jnp.float32),
        ],
        axis=0,
    )
    shift, scale = exchange_modulation(local_mod, rows)

    centred = embed.astype(jnp.float32)
    centred = centred - jnp.mean(centred, axis=2, keepdims=True)
    gram = [dot(centred[m], centred[m].T) / D for m in range(3)]
    centred_rows = lax.dynamic_slice_in_dim(centred, f * rows, rows, 2)
    embed_cols = lax.dynamic_slice_in_dim(embed, lax.axis_index("mp") * cols, cols, 2)

    pieces = []
    for m in range(3):
        through = lax.dot_general(
            proj_weight[m], unembed[m], (((1,), (1,)), ((), ())), preferred_element_type=jnp.float32
        )
        direct = lax.dot_general(
            embed_cols[m], unembed[m], (((1,), (1,)), ((), ())), preferred_element_type=jnp.float32
        )
        direct = jnp.where(f == 0, direct, 0.0)
        modulated = dot(centred_rows[m] * (1.0 + scale[m : m + 1]), through)
        offset = dot(shift[m : m + 1], through)
        offset = jnp.concatenate([offset, jnp.zeros((7, CH), jnp.float32)], 0)
        pieces.append(
            jnp.concatenate(
                [
                    jnp.concatenate([direct, modulated], 1),
                    jnp.concatenate([offset, jnp.zeros_like(offset)], 1),
                ],
                0,
            )
        )
    maps = plane_sum(jnp.concatenate(pieces, 0)).reshape(3, CH + 8, 2 * CH)
    direct = [both(maps[m, :CH, :CH]) for m in range(3)]
    modulated = [both(maps[m, :CH, CH:]) for m in range(3)]
    offset = [jnp.concatenate([maps[m, CH : CH + 1, :CH]] * 2, 1) for m in range(3)]

    ones = both(jnp.ones((CH, CH), jnp.float32))

    def normalized(u, m):
        spread = dot(dot(u, both(gram[m])) * u, ones)
        return u * lax.rsqrt(jnp.maximum(spread, 0.0) + EPS_NORM)

    def model(u, u_norm, m):
        return dot(u, direct[m]) + dot(u_norm, modulated[m]) + offset[m]

    noise = noise_all.astype(jnp.bfloat16).astype(jnp.float32)
    noise_norm = normalized(noise, 0)
    clean = model(noise, noise_norm, 0)
    level = renoise_step[0].astype(jnp.float32) / 1000.0
    noisy = (1.0 - level) * clean + level * renoise_all
    noisy = noisy.astype(jnp.bfloat16).astype(jnp.float32)
    real_v = model(noisy, normalized(noisy, 1), 1)
    fake_v = model(noisy, normalized(noisy, 2), 2)
    total = jnp.sum(jnp.abs(clean - renoise_all + real_v))
    gap_scale = level * total / (noise_all.shape[0] * 2 * CH) + EPS_GAP
    score = level * (real_v - fake_v) / gap_scale
    local_rows = gen_noise.shape[1]
    score_gap = lax.dynamic_slice_in_dim(score, f * local_rows, local_rows, 0)

    all_tokens = noise_all.shape[0] * 2 * lax.axis_size("dp")
    cotangent = (score / math.sqrt(all_tokens)).astype(jnp.bfloat16).astype(jnp.float32)
    pairs = dot(noise_norm.T, cotangent)
    outer = pairs[:CH, :CH] + pairs[CH:, CH:]
    sums = jnp.sum(cotangent, axis=0)
    sums = sums[:CH] + sums[CH:]
    payload = jnp.concatenate(
        [
            jnp.pad(outer, ((0, 0), (0, CH))),
            jnp.pad(sums[None], ((0, 7), (0, CH))),
            jnp.concatenate([shift[0], scale[0]]).reshape(-1, 2 * CH),
        ],
        0,
    )
    blocks = gather_samples(payload)
    grad_map = jnp.zeros((CH, rows), jnp.float32)
    for block in blocks:
        block_mod = block[CH + 8 :].reshape(2, rows)
        grad_map += dot(block[:CH, :CH].T, centred_rows[0]) * (1.0 + block_mod[1:2])
        grad_map += block[CH, :CH][:, None] * block_mod[0:1]
    gen_grad = lax.dot_general(
        grad_map.astype(jnp.bfloat16),
        unembed[0],
        (((0,), (0,)), ((), ())),
        preferred_element_type=jnp.float32,
    )
    return (gen_grad, score_gap[None])


def vmem_params():
    return pltpu.CompilerParams(vmem_limit_bytes=48 * 1024 * 1024)


def whole_specs(count):
    return [pl.BlockSpec(memory_space=pltpu.VMEM)] * count


def split_two(x):
    high = x.astype(jnp.bfloat16)
    return high, (x - high.astype(jnp.float32)).astype(jnp.bfloat16)


def split_three(x):
    high = x.astype(jnp.bfloat16)
    rest = x - high.astype(jnp.float32)
    middle = rest.astype(jnp.bfloat16)
    return high, middle, (rest - middle.astype(jnp.float32)).astype(jnp.bfloat16)


def lane_index(shape):
    return lax.broadcasted_iota(jnp.int32, shape, len(shape) - 1)


def block_diagonal(left_copy, right_copy):
    lanes = lane_index(left_copy.shape)
    top = jnp.where(lanes < CH, left_copy, 0.0)
    bottom = jnp.where(lanes >= CH, right_copy, 0.0)
    return jnp.concatenate([top, bottom], 0)


MOD_PIECES = 4


def mod_kernel(vec_ref, weight_ref, out_ref, buffer, sems):
    width = buffer.shape[2]
    depth = buffer.shape[1] // MOD_PIECES
    start = pl.multiple_of((lax.axis_index("mp") % 2) * width, 128)

    def piece(m, k):
        part = pl.ds(k * depth, depth)
        return pltpu.make_async_copy(
            weight_ref.at[m, part, pl.ds(start, width)], buffer.at[m, part], sems.at[m, k]
        )

    for m in range(3):
        for k in range(MOD_PIECES):
            piece(m, k).start()
    rows = []
    for m in range(3):
        total = jnp.zeros((8, width), jnp.float32)
        for k in range(MOD_PIECES):
            piece(m, k).wait()
            part = slice(k * depth, (k + 1) * depth)
            total += jnp.dot(
                vec_ref[:, part], buffer[m, part], preferred_element_type=jnp.float32
            )
        rows.append(total)
    out_ref[...] = jnp.zeros_like(out_ref)
    out_ref[0:1] = rows[0][0:1]
    out_ref[1:2] = GUIDANCE * rows[1][1:2] + (1.0 - GUIDANCE) * rows[1][2:3]
    out_ref[2:3] = rows[2][1:2]


def local_modulation(vectors, mod_weight, width):
    depth = mod_weight.shape[1]
    return pl.pallas_call(
        mod_kernel,
        out_shape=jax.ShapeDtypeStruct((8, width), jnp.float32),
        in_specs=[pl.BlockSpec(memory_space=pltpu.VMEM), pl.BlockSpec(memory_space=pl.ANY)],
        out_specs=pl.BlockSpec(memory_space=pltpu.VMEM),
        scratch_shapes=[
            pltpu.VMEM((3, depth, width), jnp.bfloat16),
            pltpu.SemaphoreType.DMA((3, MOD_PIECES)),
        ],
        compiler_params=vmem_params(),
        cost_estimate=pl.CostEstimate(
            flops=48 * depth * width, bytes_accessed=6 * depth * width, transcendentals=0
        ),
        name="modulation",
    )(vectors, mod_weight)


PROJ_PIECES = 2


def weights_kernel(
    embed_ref, unembed_ref, proj_ref, through_ref, direct_ref, gram_ref, rows_ref, buffer, sems
):
    rows, cols = buffer.shape[1:]
    depth = rows // PROJ_PIECES

    def piece(m, k):
        part = pl.ds(k * depth, depth)
        return pltpu.make_async_copy(proj_ref.at[m, part], buffer.at[m, part], sems.at[m, k])

    for m in range(3):
        for k in range(PROJ_PIECES):
            piece(m, k).start()
    f = lax.axis_index("fsdp")
    row_start = pl.multiple_of(f * rows, 128)
    col_start = pl.multiple_of(lax.axis_index("mp") * cols, 128)
    contract = (((1,), (1,)), ((), ()))
    for m in range(3):
        whole = embed_ref[m].astype(jnp.float32)
        average = jnp.sum(whole, axis=1, keepdims=True) * (1.0 / D)
        centred = whole - average
        high, low = split_two(centred)
        high_high = lax.dot_general(high, high, contract, preferred_element_type=jnp.float32)
        high_low = lax.dot_general(high, low, contract, preferred_element_type=jnp.float32)
        low_low = lax.dot_general(low, low, contract, preferred_element_type=jnp.float32)
        gram = (high_high + (high_low + high_low.T) + low_low) * (1.0 / D)
        gram = jnp.concatenate([gram, gram], 1)
        gram_ref[m] = jnp.concatenate(split_three(block_diagonal(gram, gram)), 1)
        rows_ref[m] = embed_ref[m, :, pl.ds(row_start, rows)].astype(jnp.float32) - average
        nothing = jnp.zeros((CH, cols), jnp.bfloat16)
        left = jnp.concatenate([unembed_ref[m], nothing], 0)
        direct = lax.dot_general(
            embed_ref[m, :, pl.ds(col_start, cols)],
            left,
            contract,
            preferred_element_type=jnp.float32,
        )
        direct_ref[m] = jnp.where(f == 0, direct, 0.0)
    for m in range(3):
        right = jnp.concatenate([jnp.zeros((CH, cols), jnp.bfloat16), unembed_ref[m]], 0)
        for k in range(PROJ_PIECES):
            piece(m, k).wait()
            part = slice(k * depth, (k + 1) * depth)
            through_ref[m, part] = lax.dot_general(
                buffer[m, part], right, contract, preferred_element_type=jnp.float32
            ).astype(jnp.bfloat16)


def weight_products(embed, unembed, proj_weight):
    rows, cols = proj_weight.shape[1:]
    return pl.pallas_call(
        weights_kernel,
        out_shape=[
            jax.ShapeDtypeStruct((3, rows, 2 * CH), jnp.bfloat16),
            jax.ShapeDtypeStruct((3, CH, 2 * CH), jnp.float32),
            jax.ShapeDtypeStruct((3, 2 * CH, 6 * CH), jnp.bfloat16),
            jax.ShapeDtypeStruct((3, CH, rows), jnp.float32),
        ],
        in_specs=whole_specs(2) + [pl.BlockSpec(memory_space=pl.ANY)],
        out_specs=whole_specs(4),
        scratch_shapes=[
            pltpu.VMEM((3, rows, cols), jnp.bfloat16),
            pltpu.SemaphoreType.DMA((3, PROJ_PIECES)),
        ],
        compiler_params=vmem_params(),
        cost_estimate=pl.CostEstimate(
            flops=12 * CH * rows * cols, bytes_accessed=6 * rows * cols, transcendentals=0
        ),
        name="weight_products",
    )(embed, unembed, proj_weight)


def maps_kernel(mine_ref, first_ref, second_ref, rows_ref, through_ref, direct_ref, maps_ref, mod_ref):
    rows = rows_ref.shape[2]
    f = lax.axis_index("fsdp")
    core = lax.axis_index("mp") % 2
    mine, first, second = mine_ref[...], first_ref[...], second_ref[...]
    shift = jnp.where(f == 0, jnp.where(core == 0, mine, first), jnp.where(core == 0, second, first))
    scale = jnp.where(f == 0, jnp.where(core == 0, first, second), jnp.where(core == 0, first, mine))
    for m in range(3):
        left = jnp.concatenate(
            [
                rows_ref[m] * (1.0 + scale[m : m + 1]),
                shift[m : m + 1],
                jnp.zeros((7, rows), jnp.float32),
            ],
            0,
        )
        product = jnp.dot(
            left.astype(jnp.bfloat16), through_ref[m], preferred_element_type=jnp.float32
        )
        base = m * (CH + 8)
        maps_ref[base : base + CH] = product[:CH] + direct_ref[m]
        maps_ref[base + CH : base + CH + 8] = product[CH:]
    for j in range(rows // 128):
        part = slice(j * 128, (j + 1) * 128)
        mod_ref[j : j + 1] = shift[0:1, part]
        mod_ref[rows // 128 + j : rows // 128 + j + 1] = scale[0:1, part]


def modulated_maps(mine, first, second, rows_part, through, direct):
    rows = rows_part.shape[2]
    return pl.pallas_call(
        maps_kernel,
        out_shape=[
            jax.ShapeDtypeStruct((3 * (CH + 8), 2 * CH), jnp.float32),
            jax.ShapeDtypeStruct((2 * rows // 128, 128), jnp.float32),
        ],
        in_specs=whole_specs(6),
        out_specs=whole_specs(2),
        compiler_params=vmem_params(),
        name="modulated_maps",
    )(mine, first, second, rows_part, through, direct)


def token_kernel(
    level_ref,
    noise_ref,
    noise_other_ref,
    renoise_ref,
    renoise_other_ref,
    gram_ref,
    maps_a,
    maps_b,
    maps_c,
    maps_d,
    mod_ref,
    score_ref,
    payload_ref,
):
    half = noise_ref.shape[0]
    level = level_ref[0]
    maps = (maps_a[...] + maps_b[...]) + (maps_c[...] + maps_d[...])
    width = 2 * CH
    lanes = lane_index((width, width))
    subs = lax.broadcasted_iota(jnp.int32, (width, width), 0)
    ones = jnp.where((lanes < CH) == (subs < CH), 1.0, 0.0).astype(jnp.bfloat16)
    ones = jnp.concatenate([ones, ones], 0)

    def model_matrix(m):
        base = m * (CH + 8)
        pair = maps[base : base + CH]
        turned = pltpu.roll(pair, CH, 1)
        direct = split_two(block_diagonal(pair, turned))
        modulated = split_two(block_diagonal(turned, pair))
        offset = maps[base + CH : base + CH + 1]
        offset = offset + pltpu.roll(offset, CH, 1)
        return jnp.concatenate(direct + modulated + (gram_ref[m],), 1), offset

    def inverse_deviation(u, by_gram):
        squares = jnp.concatenate(split_two(by_gram * u), 1)
        spread = jnp.dot(squares, ones, preferred_element_type=jnp.float32)
        return lax.rsqrt(jnp.maximum(spread, 0.0) + EPS_NORM)

    def model(u, product, offset):
        part = [product[:, i * width : (i + 1) * width] for i in range(7)]
        inverse = inverse_deviation(u.astype(jnp.float32), part[4] + part[5] + part[6])
        return (part[0] + part[1]) + inverse * (part[2] + part[3]) + offset, inverse

    matrices = [model_matrix(m) for m in range(3)]
    noise = jnp.concatenate([noise_ref[...], noise_other_ref[...]], 0).astype(jnp.bfloat16)
    renoise = jnp.concatenate([renoise_ref[...], renoise_other_ref[...]], 0)
    product = jnp.dot(noise, matrices[0][0], preferred_element_type=jnp.float32)
    clean, inverse = model(noise, product, matrices[0][1])
    noise_norm = noise.astype(jnp.float32) * inverse
    noisy = ((1.0 - level) * clean + level * renoise).astype(jnp.bfloat16)
    product = jnp.dot(noisy, matrices[1][0], preferred_element_type=jnp.float32)
    real_v, _ = model(noisy, product, matrices[1][1])
    product = jnp.dot(noisy, matrices[2][0], preferred_element_type=jnp.float32)
    fake_v, _ = model(noisy, product, matrices[2][1])
    total = jnp.sum(jnp.abs(clean - renoise + real_v))
    gap_scale = level * total * (1.0 / (2 * half * width)) + EPS_GAP
    score = level * (real_v - fake_v) / gap_scale
    score_ref[...] = score[:half]
    tokens = 4 * half * lax.axis_size("dp")
    cotangent = (score * (1.0 / math.sqrt(tokens))).astype(jnp.bfloat16)
    pairs = lax.dot_general(
        noise_norm.astype(jnp.bfloat16),
        cotangent,
        (((0,), (0,)), ((), ())),
        preferred_element_type=jnp.float32,
    )
    payload_ref[:CH] = pairs[:CH] + pltpu.roll(pairs[CH:], CH, 1)
    sums = jnp.sum(cotangent.astype(jnp.float32), axis=0, keepdims=True)
    payload_ref[CH : CH + 8] = jnp.concatenate(
        [sums + pltpu.roll(sums, CH, 1), jnp.zeros((7, width), jnp.float32)], 0
    )
    payload_ref[CH + 8 :] = mod_ref[...]


def token_phase(level, noise, noise_other, renoise, renoise_other, gram, maps, mod):
    half = noise.shape[0]
    return pl.pallas_call(
        token_kernel,
        out_shape=[
            jax.ShapeDtypeStruct((half, 2 * CH), jnp.float32),
            jax.ShapeDtypeStruct((CH + 8 + mod.shape[0], 2 * CH), jnp.float32),
        ],
        in_specs=[pl.BlockSpec(memory_space=pltpu.SMEM)] + whole_specs(10),
        out_specs=whole_specs(2),
        compiler_params=vmem_params(),
        name="tokens",
    )(level, noise, noise_other, renoise, renoise_other, gram, *maps, mod)


GRAD_TILE = 256


def grad_kernel(block_a, block_b, block_c, block_d, rows_ref, unembed_ref, grad_ref):
    tile = grad_ref.shape[0]
    step = pl.program_id(0)
    count = (block_a.shape[0] - CH - 8) // 2
    per_tile = tile // 128
    lefts, rights = [], []
    embed_rows = rows_ref[0]
    for block in (block_a, block_b, block_c, block_d):
        lefts.append(block[: CH + 8])
        shift, scale = [], []
        for j in range(per_tile):
            shift.append(block[pl.ds(CH + 8 + step * per_tile + j, 1)])
            scale.append(block[pl.ds(CH + 8 + count + step * per_tile + j, 1)])
        rights += [
            embed_rows * (1.0 + jnp.concatenate(scale, 1)),
            jnp.concatenate(shift, 1),
            jnp.zeros((7, tile), jnp.float32),
        ]
    left = jnp.concatenate(lefts, 0)[:, :CH].astype(jnp.bfloat16)
    right = jnp.concatenate(rights, 0).astype(jnp.bfloat16)
    grad_map = lax.dot_general(
        right, left, (((0,), (0,)), ((), ())), preferred_element_type=jnp.float32
    )
    grad_ref[...] = jnp.dot(
        grad_map.astype(jnp.bfloat16), unembed_ref[0], preferred_element_type=jnp.float32
    )


def gradient(blocks, rows_part, unembed):
    rows = rows_part.shape[2]
    cols = unembed.shape[2]
    block_spec = pl.BlockSpec(blocks[0].shape, lambda i: (0, 0))
    return pl.pallas_call(
        grad_kernel,
        grid=(rows // GRAD_TILE,),
        out_shape=jax.ShapeDtypeStruct((rows, cols), jnp.float32),
        in_specs=[block_spec] * 4
        + [
            pl.BlockSpec((1, CH, GRAD_TILE), lambda i: (0, 0, i)),
            pl.BlockSpec((1, CH, cols), lambda i: (0, 0, 0)),
        ],
        out_specs=pl.BlockSpec((GRAD_TILE, cols), lambda i: (i, 0)),
        compiler_params=vmem_params(),
        name="gradient",
    )(*blocks, rows_part, unembed)


def exchange_halves(x):
    pairs_first, pairs_second = [], []
    for chip in range(2):
        for y, core, to_y, to_core in ((1, 0, 0, 0), (0, 0, 0, 1), (0, 1, 1, 1), (1, 1, 1, 0)):
            pairs_first.append((chip * 4 + core * 2 + y, chip * 4 + to_core * 2 + to_y))
        for y, core, to_y, to_core in ((1, 0, 0, 1), (0, 1, 1, 0)):
            pairs_second.append((chip * 4 + core * 2 + y, chip * 4 + to_core * 2 + to_y))
    axes = ("mp", "fsdp")
    return lax.ppermute(x, axes, pairs_first), lax.ppermute(x, axes, pairs_second)


def body(
    gen_noise, renoise, gen_step, renoise_step, text_pooled, embed, mod_weight, proj_weight, unembed
):
    blank_text = jnp.zeros_like(text_pooled)
    vectors = jnp.concatenate(
        [
            condition(gen_step, text_pooled),
            condition(renoise_step, text_pooled),
            condition(renoise_step, blank_text),
            jnp.zeros((5, TEMB + text_pooled.shape[1]), jnp.bfloat16),
        ],
        axis=0,
    )
    mine = local_modulation(vectors, mod_weight, mod_weight.shape[2] // 2)
    first, second = exchange_halves(mine)
    noise_other = swap(gen_noise[0], "fsdp", 1)
    renoise_other = swap(renoise[0], "fsdp", 1)
    through, direct, gram, rows_part = weight_products(embed, unembed, proj_weight)
    maps, mod = modulated_maps(mine, first, second, rows_part, through, direct)
    maps = maps + swap(maps, "mp", 1)
    plane = ("mp", "fsdp")
    maps = [maps] + [swap(maps, plane, mask) for mask in (4, 1, 5)]
    level = renoise_step.astype(jnp.float32) / 1000.0
    score_gap, payload = token_phase(
        level, gen_noise[0], noise_other, renoise[0], renoise_other, gram, maps, mod
    )
    blocks = gather_samples(payload)
    return (gradient(blocks, rows_part, unembed), score_gap[None])


def fits_kernels(mesh):
    return mesh.shape["mp"] == 4 and mesh.shape["fsdp"] == 2 and mesh.shape["dp"] == 4


def solution(mesh):
    return jax.shard_map(
        body if fits_kernels(mesh) else plain_body,
        mesh=mesh,
        in_specs=(
            P("dp", "fsdp", None),
            P("dp", "fsdp", None),
            P("dp"),
            P("dp"),
            P("dp", None),
            P(),
            P(None, None, "fsdp"),
            P(None, "fsdp", "mp"),
            P(None, None, "mp"),
        ),
        out_specs=(P("fsdp", "mp"), P("dp", "fsdp", None)),
        check_vma=False,
    )
```

```python
import math

import jax
import jax.numpy as jnp
from jax import lax
from jax.experimental import pallas as pl
from jax.experimental.pallas import tpu as pltpu
from jax.sharding import PartitionSpec as P

D = 3072
CH = 64
TEMB = 256

GUIDANCE = 3.5
EPS_NORM = 1e-06
EPS_GAP = 1e-05
HI = lax.Precision.HIGHEST


def sinusoid(timesteps):
    half_size = TEMB // 2
    frequency = jnp.exp(-math.log(10000.0) * jnp.arange(half_size, dtype=jnp.float32) / half_size)
    angles = timesteps.astype(jnp.float32)[:, None] * frequency[None, :]
    return jnp.concatenate([jnp.cos(angles), jnp.sin(angles)], axis=1)


def condition(timesteps, pooled):
    joined = jnp.concatenate([sinusoid(timesteps), pooled.astype(jnp.float32)], axis=1)
    return jax.nn.silu(joined).astype(jnp.bfloat16)


def swap(x, axes, mask):
    count = lax.axis_size(axes)
    return lax.ppermute(x, axes, [(i, i ^ mask) for i in range(count)])


def plane_sum(x):
    if lax.axis_size("mp") != 4 or lax.axis_size("fsdp") != 2:
        return lax.psum(x, ("mp", "fsdp"))
    x = x + swap(x, "mp", 1)
    plane = ("mp", "fsdp")
    parts = [swap(x, plane, mask) for mask in (4, 1, 5)]
    return (x + parts[0]) + (parts[1] + parts[2])


def gather_samples(x):
    count = lax.axis_size("dp")
    if lax.axis_size("mp") != 4 or count != 4:
        blocks = lax.all_gather(x, "dp")
        return [blocks[i] for i in range(count)]
    pairs = []
    for m in range(4):
        for s in range(4):
            pairs.append((m * 4 + s, m * 4 + (s ^ (1 if m % 2 == 0 else 2))))
    near = lax.ppermute(x, ("mp", "dp"), pairs)
    far = swap(x, "dp", 3)
    return [x, near, swap(near, "mp", 1), far]


def exchange_modulation(local_mod, rows):
    if lax.axis_size("fsdp") == 2:
        f = lax.axis_index("fsdp")
        mine = lax.dynamic_slice_in_dim(local_mod, f * rows, rows, 1)
        theirs = swap(lax.dynamic_slice_in_dim(local_mod, (1 - f) * rows, rows, 1), "fsdp", 1)
        return jnp.where(f == 0, mine, theirs), jnp.where(f == 0, theirs, mine)
    whole = lax.all_gather(local_mod, "fsdp", axis=1, tiled=True)
    start = lax.axis_index("fsdp") * rows
    return (
        lax.dynamic_slice_in_dim(whole[:, :D], start, rows, 1),
        lax.dynamic_slice_in_dim(whole[:, D:], start, rows, 1),
    )


def dot(a, b, precision=HI):
    return jnp.dot(a, b, precision=precision, preferred_element_type=jnp.float32)


def both(x):
    zero = jnp.zeros_like(x)
    return jnp.concatenate(
        [jnp.concatenate([x, zero], 1), jnp.concatenate([zero, x], 1)], 0
    )


def plain_body(
    gen_noise, renoise, gen_step, renoise_step, text_pooled, embed, mod_weight, proj_weight, unembed
):
    rows, cols = proj_weight.shape[1], proj_weight.shape[2]
    f = lax.axis_index("fsdp")
    noise_all = lax.all_gather(gen_noise[0], "fsdp", axis=0, tiled=True)
    renoise_all = lax.all_gather(renoise[0], "fsdp", axis=0, tiled=True)

    blank_text = jnp.zeros_like(text_pooled)
    gen_vec = condition(gen_step, text_pooled)
    real_vec = jnp.concatenate(
        [condition(renoise_step, text_pooled), condition(renoise_step, blank_text)], 0
    )
    teacher_mod = jnp.dot(real_vec, mod_weight[1], preferred_element_type=jnp.float32)
    local_mod = jnp.concatenate(
        [
            jnp.dot(gen_vec, mod_weight[0], preferred_element_type=jnp.float32),
            GUIDANCE * teacher_mod[0:1] + (1.0 - GUIDANCE) * teacher_mod[1:2],
            jnp.dot(real_vec[0:1], mod_weight[2], preferred_element_type=jnp.float32),
        ],
        axis=0,
    )
    shift, scale = exchange_modulation(local_mod, rows)

    centred = embed.astype(jnp.float32)
    centred = centred - jnp.mean(centred, axis=2, keepdims=True)
    gram = [dot(centred[m], centred[m].T) / D for m in range(3)]
    centred_rows = lax.dynamic_slice_in_dim(centred, f * rows, rows, 2)
    embed_cols = lax.dynamic_slice_in_dim(embed, lax.axis_index("mp") * cols, cols, 2)

    pieces = []
    for m in range(3):
        through = lax.dot_general(
            proj_weight[m], unembed[m], (((1,), (1,)), ((), ())), preferred_element_type=jnp.float32
        )
        direct = lax.dot_general(
            embed_cols[m], unembed[m], (((1,), (1,)), ((), ())), preferred_element_type=jnp.float32
        )
        direct = jnp.where(f == 0, direct, 0.0)
        modulated = dot(centred_rows[m] * (1.0 + scale[m : m + 1]), through)
        offset = dot(shift[m : m + 1], through)
        offset = jnp.concatenate([offset, jnp.zeros((7, CH), jnp.float32)], 0)
        pieces.append(
            jnp.concatenate(
                [
                    jnp.concatenate([direct, modulated], 1),
                    jnp.concatenate([offset, jnp.zeros_like(offset)], 1),
                ],
                0,
            )
        )
    maps = plane_sum(jnp.concatenate(pieces, 0)).reshape(3, CH + 8, 2 * CH)
    direct = [both(maps[m, :CH, :CH]) for m in range(3)]
    modulated = [both(maps[m, :CH, CH:]) for m in range(3)]
    offset = [jnp.concatenate([maps[m, CH : CH + 1, :CH]] * 2, 1) for m in range(3)]

    ones = both(jnp.ones((CH, CH), jnp.float32))

    def normalized(u, m):
        spread = dot(dot(u, both(gram[m])) * u, ones)
        return u * lax.rsqrt(jnp.maximum(spread, 0.0) + EPS_NORM)

    def model(u, u_norm, m):
        return dot(u, direct[m]) + dot(u_norm, modulated[m]) + offset[m]

    noise = noise_all.astype(jnp.bfloat16).astype(jnp.float32)
    noise_norm = normalized(noise, 0)
    clean = model(noise, noise_norm, 0)
    level = renoise_step[0].astype(jnp.float32) / 1000.0
    noisy = (1.0 - level) * clean + level * renoise_all
    noisy = noisy.astype(jnp.bfloat16).astype(jnp.float32)
    real_v = model(noisy, normalized(noisy, 1), 1)
    fake_v = model(noisy, normalized(noisy, 2), 2)
    total = jnp.sum(jnp.abs(clean - renoise_all + real_v))
    gap_scale = level * total / (noise_all.shape[0] * 2 * CH) + EPS_GAP
    score = level * (real_v - fake_v) / gap_scale
    local_rows = gen_noise.shape[1]
    score_gap = lax.dynamic_slice_in_dim(score, f * local_rows, local_rows, 0)

    all_tokens = noise_all.shape[0] * 2 * lax.axis_size("dp")
    cotangent = (score / math.sqrt(all_tokens)).astype(jnp.bfloat16).astype(jnp.float32)
    pairs = dot(noise_norm.T, cotangent)
    outer = pairs[:CH, :CH] + pairs[CH:, CH:]
    sums = jnp.sum(cotangent, axis=0)
    sums = sums[:CH] + sums[CH:]
    payload = jnp.concatenate(
        [
            jnp.pad(outer, ((0, 0), (0, CH))),
            jnp.pad(sums[None], ((0, 7), (0, CH))),
            jnp.concatenate([shift[0], scale[0]]).reshape(-1, 2 * CH),
        ],
        0,
    )
    blocks = gather_samples(payload)
    grad_map = jnp.zeros((CH, rows), jnp.float32)
    for block in blocks:
        block_mod = block[CH + 8 :].reshape(2, rows)
        grad_map += dot(block[:CH, :CH].T, centred_rows[0]) * (1.0 + block_mod[1:2])
        grad_map += block[CH, :CH][:, None] * block_mod[0:1]
    gen_grad = lax.dot_general(
        grad_map.astype(jnp.bfloat16),
        unembed[0],
        (((0,), (0,)), ((), ())),
        preferred_element_type=jnp.float32,
    )
    return (gen_grad, score_gap[None])


def vmem_params():
    return pltpu.CompilerParams(vmem_limit_bytes=48 * 1024 * 1024)


def whole_specs(count):
    return [pl.BlockSpec(memory_space=pltpu.VMEM)] * count


def split_two(x):
    high = x.astype(jnp.bfloat16)
    return high, (x - high.astype(jnp.float32)).astype(jnp.bfloat16)


def split_three(x):
    high = x.astype(jnp.bfloat16)
    rest = x - high.astype(jnp.float32)
    middle = rest.astype(jnp.bfloat16)
    return high, middle, (rest - middle.astype(jnp.float32)).astype(jnp.bfloat16)


def lane_index(shape):
    return lax.broadcasted_iota(jnp.int32, shape, len(shape) - 1)


def block_diagonal(left_copy, right_copy):
    lanes = lane_index(left_copy.shape)
    top = jnp.where(lanes < CH, left_copy, 0.0)
    bottom = jnp.where(lanes >= CH, right_copy, 0.0)
    return jnp.concatenate([top, bottom], 0)


MOD_PIECES = 4
PROJ_PIECES = 2
IN_FLIGHT = 6
PACK = 128
CONTRACT_LAST = (((1,), (1,)), ((), ()))
CONTRACT_FIRST = (((0,), (0,)), ((), ()))


def stream_kernel(
    gen_step_ref,
    renoise_step_ref,
    text_hbm,
    noise_hbm,
    renoise_hbm,
    mod_hbm,
    proj_hbm,
    unembed_hbm,
    mod_ref,
    latents_ref,
    through_ref,
    text_ref,
    noise_ref,
    renoise_ref,
    unembed_ref,
    mod_buffer,
    proj_buffer,
    mod_sems,
    proj_sems,
    small_sems,
):
    width = mod_buffer.shape[2]
    rows, cols = proj_buffer.shape[1:]
    mod_depth = mod_buffer.shape[1] // MOD_PIECES
    proj_depth = rows // PROJ_PIECES
    mod_start = pl.multiple_of((lax.axis_index("mp") % 2) * width, 128)

    def mod_piece(m, k):
        part = pl.ds(k * mod_depth, mod_depth)
        return pltpu.make_async_copy(
            mod_hbm.at[m, part, pl.ds(mod_start, width)], mod_buffer.at[m, part], mod_sems.at[m, k]
        )

    def proj_piece(m, k):
        part = pl.ds(k * proj_depth, proj_depth)
        return pltpu.make_async_copy(
            proj_hbm.at[m, part], proj_buffer.at[m, part], proj_sems.at[m, k]
        )

    small = [
        pltpu.make_async_copy(source, target, small_sems.at[k])
        for k, (source, target) in enumerate(
            (
                (text_hbm, text_ref),
                (unembed_hbm, unembed_ref),
                (noise_hbm, noise_ref),
                (renoise_hbm, renoise_ref),
            )
        )
    ]
    order = []
    for m in range(3):
        order += [proj_piece(m, k) for k in range(PROJ_PIECES)]
        order += [mod_piece(m, k) for k in range(MOD_PIECES)]
    order = small[:2] + order[:IN_FLIGHT] + small[2:] + order[IN_FLIGHT:]
    ahead = IN_FLIGHT + 4
    for copy in order[:ahead]:
        copy.start()

    def take(position):
        order[position].wait()
        if position + ahead < len(order):
            order[position + ahead].start()

    take(0)
    half_size = TEMB // 2
    place = lane_index((8, half_size)).astype(jnp.float32)
    frequency = jnp.exp(place * (-math.log(10000.0) / half_size))
    level = lax.broadcasted_iota(jnp.int32, (8, half_size), 0)
    steps = jnp.where(level == 0, gen_step_ref[0], renoise_step_ref[0]).astype(jnp.float32)
    angles = steps * frequency
    text = jnp.broadcast_to(text_ref[...].astype(jnp.float32), (8, text_ref.shape[1]))
    text = jnp.where(lax.broadcasted_iota(jnp.int32, text.shape, 0) < 2, text, 0.0)
    joined = jnp.concatenate([jnp.cos(angles), jnp.sin(angles), text], 1)
    vectors = (joined / (1.0 + jnp.exp(-joined))).astype(jnp.bfloat16)
    packs = width // PACK
    mod_ref[...] = jnp.zeros_like(mod_ref)
    take(1)
    place = 2
    for m in range(3):
        total = jnp.zeros((8, width), jnp.float32)
        for k in range(PROJ_PIECES + MOD_PIECES):
            if place == IN_FLIGHT + 2:
                take(place)
                take(place + 1)
                latents = jnp.where(lax.axis_index("mp") % 2 == 0, noise_ref[...], renoise_ref[...])
                latents_ref[...] = latents.astype(jnp.bfloat16)
                place += 2
            take(place)
            place += 1
            if k < PROJ_PIECES:
                part = slice(k * proj_depth, (k + 1) * proj_depth)
                through_ref[m, :, part] = lax.dot_general(
                    unembed_ref[m],
                    proj_buffer[m, part],
                    CONTRACT_LAST,
                    preferred_element_type=jnp.float32,
                ).astype(jnp.bfloat16)
            else:
                part = slice((k - PROJ_PIECES) * mod_depth, (k - PROJ_PIECES + 1) * mod_depth)
                total += jnp.dot(
                    vectors[:, part], mod_buffer[m, part], preferred_element_type=jnp.float32
                )
        if m == 0:
            line = total[0:1]
        elif m == 1:
            line = GUIDANCE * total[1:2] + (1.0 - GUIDANCE) * total[2:3]
        else:
            line = total[1:2]
        for j in range(packs):
            mod_ref[m * packs + j : m * packs + j + 1] = line[:, j * PACK : (j + 1) * PACK]


def streamed_weights(
    gen_step, renoise_step, text, noise, renoise, mod_weight, proj_weight, unembed
):
    depth, width = mod_weight.shape[1], mod_weight.shape[2] // 2
    rows, cols = proj_weight.shape[1:]
    pack_rows = -(-3 * width // PACK // 8) * 8
    return pl.pallas_call(
        stream_kernel,
        out_shape=[
            jax.ShapeDtypeStruct((pack_rows, PACK), jnp.float32),
            jax.ShapeDtypeStruct(noise.shape, jnp.bfloat16),
            jax.ShapeDtypeStruct((3, CH, rows), jnp.bfloat16),
        ],
        in_specs=[pl.BlockSpec(memory_space=pltpu.SMEM)] * 2
        + [pl.BlockSpec(memory_space=pltpu.HBM)] * 6,
        out_specs=whole_specs(3),
        scratch_shapes=[
            pltpu.VMEM(text.shape, text.dtype),
            pltpu.VMEM(noise.shape, noise.dtype),
            pltpu.VMEM(renoise.shape, renoise.dtype),
            pltpu.VMEM(unembed.shape, unembed.dtype),
            pltpu.VMEM((3, depth, width), jnp.bfloat16),
            pltpu.VMEM((3, rows, cols), jnp.bfloat16),
            pltpu.SemaphoreType.DMA((3, MOD_PIECES)),
            pltpu.SemaphoreType.DMA((3, PROJ_PIECES)),
            pltpu.SemaphoreType.DMA((4,)),
        ],
        compiler_params=vmem_params(),
        name="stream_weights",
    )(
        gen_step,
        renoise_step,
        *(
            pltpu.with_memory_space_constraint(x, pltpu.HBM)
            for x in (text, noise, renoise, mod_weight, proj_weight, unembed)
        ),
    )


def embed_kernel(embed_ref, unembed_ref, gram_ref, rows_ref, direct_ref):
    rows, cols = rows_ref.shape[2], unembed_ref.shape[2]
    f = lax.axis_index("fsdp")
    row_start = pl.multiple_of(f * rows, 128)
    col_start = pl.multiple_of(lax.axis_index("mp") * cols, 128)
    nothing = jnp.zeros((CH, cols), jnp.bfloat16)
    for m in range(3):
        whole = embed_ref[m].astype(jnp.float32)
        average = jnp.sum(whole, axis=1, keepdims=True) * (1.0 / D)
        rows_ref[m] = embed_ref[m, :, pl.ds(row_start, rows)].astype(jnp.float32) - average
        direct = lax.dot_general(
            embed_ref[m, :, pl.ds(col_start, cols)],
            jnp.concatenate([unembed_ref[m], nothing], 0),
            CONTRACT_LAST,
            preferred_element_type=jnp.float32,
        )
        direct_ref[m] = jnp.where(f == 0, direct, 0.0)
        pair = jnp.concatenate(split_two(whole - average), 0)
        product = lax.dot_general(pair, pair, CONTRACT_LAST, preferred_element_type=jnp.float32)
        product = product[:CH] + product[CH:]
        gram = (product + pltpu.roll(product, CH, 1)) * (1.0 / D)
        gram_ref[m] = jnp.concatenate(split_three(block_diagonal(gram, gram)), 1)


def embed_products(embed, unembed, rows):
    return pl.pallas_call(
        embed_kernel,
        out_shape=[
            jax.ShapeDtypeStruct((3, 2 * CH, 6 * CH), jnp.bfloat16),
            jax.ShapeDtypeStruct((3, CH, rows), jnp.float32),
            jax.ShapeDtypeStruct((3, CH, 2 * CH), jnp.float32),
        ],
        in_specs=whole_specs(2),
        out_specs=whole_specs(3),
        compiler_params=vmem_params(),
        cost_estimate=pl.CostEstimate(
            flops=6 * 128 * 128 * D, bytes_accessed=6 * CH * D, transcendentals=0
        ),
        name="embed_products",
    )(embed, unembed)


def pair_ones():
    shape = (2 * CH, 2 * CH)
    lanes = lane_index(shape)
    subs = lax.broadcasted_iota(jnp.int32, shape, 0)
    ones = jnp.where((lanes < CH) == (subs < CH), 1.0, 0.0).astype(jnp.bfloat16)
    return jnp.concatenate([ones, ones], 0)


def inverse_deviation(u, by_gram, ones):
    squares = jnp.concatenate(split_two(by_gram * u), 1)
    spread = jnp.dot(squares, ones, preferred_element_type=jnp.float32)
    return lax.rsqrt(jnp.maximum(spread, 0.0) + EPS_NORM)


def columns(product, i):
    return product[:, i * 2 * CH : (i + 1) * 2 * CH]


def sample_latents(noise_ref, first_ref, second_ref):
    first, second = first_ref[...], second_ref[...]
    core = lax.axis_index("mp") % 2
    other = jnp.where(core == 0, first, second)
    other_renoise = jnp.where(core == 0, second, first)
    return jnp.concatenate([noise_ref[...].astype(jnp.bfloat16), other], 0), other_renoise


def noise_kernel(noise_ref, first_ref, second_ref, gram_ref, inverse_ref, normal_ref):
    noise, _ = sample_latents(noise_ref, first_ref, second_ref)
    product = jnp.dot(noise, gram_ref[0], preferred_element_type=jnp.float32)
    noise = noise.astype(jnp.float32)
    by_gram = columns(product, 0) + columns(product, 1) + columns(product, 2)
    inverse = inverse_deviation(noise, by_gram, pair_ones())
    inverse_ref[...] = inverse
    normal_ref[...] = (noise * inverse).astype(jnp.bfloat16)


def noise_statistics(noise, first, second, gram):
    shape = (2 * noise.shape[0], noise.shape[1])
    return pl.pallas_call(
        noise_kernel,
        out_shape=[
            jax.ShapeDtypeStruct(shape, jnp.float32),
            jax.ShapeDtypeStruct(shape, jnp.bfloat16),
        ],
        in_specs=whole_specs(4),
        out_specs=whole_specs(2),
        compiler_params=vmem_params(),
        name="noise_statistics",
    )(noise, first, second, gram)


def maps_kernel(kept_ref, got_ref, rows_ref, through_ref, direct_ref, maps_ref, mod_ref):
    rows = rows_ref.shape[2]
    packs = rows // PACK
    f = lax.axis_index("fsdp")
    kept, got = kept_ref[...], got_ref[...]
    shift = jnp.where(f == 0, kept, got)
    scale = jnp.where(f == 0, got, kept)
    for m in range(3):
        pieces = []
        for j in range(packs):
            line = slice(m * packs + j, m * packs + j + 1)
            pieces.append(
                jnp.concatenate(
                    [
                        rows_ref[m, :, j * PACK : (j + 1) * PACK] * (1.0 + scale[line]),
                        shift[line],
                        jnp.zeros((7, PACK), jnp.float32),
                    ],
                    0,
                )
            )
        left = jnp.concatenate(pieces, 1).astype(jnp.bfloat16)
        through = jnp.concatenate([jnp.zeros((CH, rows), jnp.bfloat16), through_ref[m]], 0)
        product = lax.dot_general(
            left, through, CONTRACT_LAST, preferred_element_type=jnp.float32
        )
        base = m * (CH + 8)
        maps_ref[base : base + CH] = product[:CH] + direct_ref[m]
        maps_ref[base + CH : base + CH + 8] = product[CH:]
    rest = jnp.zeros((mod_ref.shape[0] - 2 * packs, PACK), jnp.float32)
    mod_ref[...] = jnp.concatenate([shift[:packs], scale[:packs], rest], 0).astype(jnp.bfloat16)


def modulated_maps(kept, got, rows_part, through, direct):
    packs = rows_part.shape[2] // PACK
    return pl.pallas_call(
        maps_kernel,
        out_shape=[
            jax.ShapeDtypeStruct((3 * (CH + 8), 2 * CH), jnp.float32),
            jax.ShapeDtypeStruct((-(-2 * packs // 16) * 16, PACK), jnp.bfloat16),
        ],
        in_specs=whole_specs(5),
        out_specs=whole_specs(2),
        compiler_params=vmem_params(),
        name="modulated_maps",
    )(kept, got, rows_part, through, direct)


MAP_ROWS = CH + 16


def token_kernel(
    level_ref,
    noise_ref,
    first_ref,
    second_ref,
    renoise_ref,
    inverse_ref,
    normal_ref,
    gram_ref,
    maps_a,
    maps_b,
    maps_c,
    maps_d,
    mod_ref,
    score_ref,
    payload_ref,
):
    half = renoise_ref.shape[0]
    level = level_ref[0]
    maps = [part[...].astype(jnp.float32) for part in (maps_a, maps_b, maps_c, maps_d)]
    maps = (maps[0] + maps[1]) + (maps[2] + maps[3])
    width = 2 * CH
    ones = pair_ones()

    def model_matrix(m):
        base = m * (CH + 8)
        pair = maps[base : base + CH]
        turned = pltpu.roll(pair, CH, 1)
        direct = split_two(block_diagonal(pair, turned))
        modulated = split_two(block_diagonal(turned, pair))
        offset = maps[base + CH : base + CH + 1]
        return jnp.concatenate(direct + modulated, 1), offset + pltpu.roll(offset, CH, 1)

    def combine(product, inverse, offset):
        direct = columns(product, 0) + columns(product, 1)
        return direct + inverse * (columns(product, 2) + columns(product, 3)) + offset

    noise, other_renoise = sample_latents(noise_ref, first_ref, second_ref)
    renoise = jnp.concatenate([renoise_ref[...], other_renoise.astype(jnp.float32)], 0)
    matrix, offset = model_matrix(0)
    product = jnp.dot(noise, matrix, preferred_element_type=jnp.float32)
    clean = combine(product, inverse_ref[...], offset)
    noisy = ((1.0 - level) * clean + level * renoise).astype(jnp.bfloat16)
    noisy_wide = noisy.astype(jnp.float32)

    def velocity(m):
        matrix, offset = model_matrix(m)
        matrix = jnp.concatenate([matrix, gram_ref[m]], 1)
        product = jnp.dot(noisy, matrix, preferred_element_type=jnp.float32)
        by_gram = columns(product, 4) + columns(product, 5) + columns(product, 6)
        return combine(product, inverse_deviation(noisy_wide, by_gram, ones), offset)

    real_v = velocity(1)
    fake_v = velocity(2)
    total = jnp.sum(jnp.abs(clean - renoise + real_v))
    gap_scale = level * total * (1.0 / (2 * half * width)) + EPS_GAP
    score = level * (real_v - fake_v) / gap_scale
    score_ref[...] = score[:half]
    tokens = 4 * half * lax.axis_size("dp")
    cotangent = (score * (1.0 / math.sqrt(tokens))).astype(jnp.bfloat16)
    pairs = lax.dot_general(
        normal_ref[...], cotangent, CONTRACT_FIRST, preferred_element_type=jnp.float32
    )
    outer = pairs[:CH] + pltpu.roll(pairs[CH:], CH, 1)
    sums = jnp.sum(cotangent.astype(jnp.float32), axis=0, keepdims=True)
    sums = sums + pltpu.roll(sums, CH, 1)
    rest = jnp.zeros((MAP_ROWS - CH - 1, width), jnp.float32)
    payload_ref[:MAP_ROWS] = jnp.concatenate([outer, sums, rest], 0).astype(jnp.bfloat16)
    payload_ref[MAP_ROWS:] = mod_ref[...]


def token_phase(level, noise, first, second, renoise, inverse, normal, gram, maps, mod):
    return pl.pallas_call(
        token_kernel,
        out_shape=[
            jax.ShapeDtypeStruct(renoise.shape, jnp.float32),
            jax.ShapeDtypeStruct((MAP_ROWS + mod.shape[0], 2 * CH), jnp.bfloat16),
        ],
        in_specs=[pl.BlockSpec(memory_space=pltpu.SMEM)] + whole_specs(12),
        out_specs=whole_specs(2),
        compiler_params=vmem_params(),
        name="tokens",
    )(level, noise, first, second, renoise, inverse, normal, gram, *maps, mod)


GRAD_PIECES = 6


def grad_kernel(block_a, block_b, block_c, block_d, rows_ref, unembed_ref, grad_hbm, buffer, sems):
    rows = rows_ref.shape[2]
    packs = rows // PACK
    depth = rows // GRAD_PIECES
    blocks = [block[...] for block in (block_a, block_b, block_c, block_d)]
    left = jnp.concatenate([block[:MAP_ROWS, :CH] for block in blocks], 0)
    mods = [block[MAP_ROWS:].astype(jnp.float32) for block in blocks]
    unembed = unembed_ref[0]

    def piece(k):
        part = pl.ds(k * depth, depth)
        return pltpu.make_async_copy(buffer.at[part], grad_hbm.at[part], sems.at[k])

    for k in range(GRAD_PIECES):
        tiles = []
        for j in range(k * depth // PACK, (k + 1) * depth // PACK):
            embed_tile = rows_ref[0, :, j * PACK : (j + 1) * PACK]
            column = []
            for mod in mods:
                column += [
                    embed_tile * (1.0 + mod[packs + j : packs + j + 1]),
                    mod[j : j + 1],
                    jnp.zeros((MAP_ROWS - CH - 1, PACK), jnp.float32),
                ]
            tiles.append(jnp.concatenate(column, 0).astype(jnp.bfloat16))
        right = jnp.concatenate(tiles, 1)
        grad_map = lax.dot_general(
            left, right, CONTRACT_FIRST, preferred_element_type=jnp.float32
        ).astype(jnp.bfloat16)
        buffer[k * depth : (k + 1) * depth] = lax.dot_general(
            grad_map, unembed, CONTRACT_FIRST, preferred_element_type=jnp.float32
        )
        piece(k).start()
    for k in range(GRAD_PIECES):
        piece(k).wait()


def gradient(blocks, rows_part, unembed):
    rows = rows_part.shape[2]
    cols = unembed.shape[2]
    return pl.pallas_call(
        grad_kernel,
        out_shape=jax.ShapeDtypeStruct((rows, cols), jnp.float32),
        in_specs=whole_specs(6),
        out_specs=pl.BlockSpec(memory_space=pl.ANY),
        scratch_shapes=[
            pltpu.VMEM((rows, cols), jnp.float32),
            pltpu.SemaphoreType.DMA((GRAD_PIECES,)),
        ],
        compiler_params=vmem_params(),
        name="gradient",
    )(*blocks, rows_part, unembed)


def body(
    gen_noise, renoise, gen_step, renoise_step, text_pooled, embed, mod_weight, proj_weight, unembed
):
    mine, latents, through = streamed_weights(
        gen_step,
        renoise_step,
        text_pooled,
        gen_noise[0],
        renoise[0],
        mod_weight,
        proj_weight,
        unembed,
    )
    f = lax.axis_index("fsdp")
    theirs = swap(mine, "mp", 1)
    own_half = lax.axis_index("mp") % 2 == f
    kept = jnp.where(own_half, mine, theirs)
    got = swap(jnp.where(own_half, theirs, mine), "fsdp", 1)
    first = swap(latents, "fsdp", 1)
    got, first = lax.optimization_barrier((got, first))
    second = swap(first, "mp", 1)
    gram, rows_part, direct = embed_products(embed, unembed, proj_weight.shape[1])
    maps, mod = modulated_maps(kept, got, rows_part, through, direct)
    maps = (maps + swap(maps, "mp", 1)).astype(jnp.bfloat16)
    inverse, normal = noise_statistics(gen_noise[0], first, second, gram)
    plane = ("mp", "fsdp")
    maps = [maps] + [swap(maps, plane, mask) for mask in (4, 1, 5)]
    level = renoise_step.astype(jnp.float32) / 1000.0
    score_gap, payload = token_phase(
        level, gen_noise[0], first, second, renoise[0], inverse, normal, gram, maps, mod
    )
    blocks = gather_samples(payload)
    return (gradient(blocks, rows_part, unembed), score_gap[None])


def fits_kernels(mesh):
    return mesh.shape["mp"] == 4 and mesh.shape["fsdp"] == 2 and mesh.shape["dp"] == 4


def solution(mesh):
    return jax.shard_map(
        body if fits_kernels(mesh) else plain_body,
        mesh=mesh,
        in_specs=(
            P("dp", "fsdp", None),
            P("dp", "fsdp", None),
            P("dp"),
            P("dp"),
            P("dp", None),
            P(),
            P(None, None, "fsdp"),
            P(None, "fsdp", "mp"),
            P(None, None, "mp"),
        ),
        out_specs=(P("fsdp", "mp"), P("dp", "fsdp", None)),
        check_vma=False,
    )
```

```python
import math

import jax
import jax.numpy as jnp
from jax import lax
from jax.experimental import pallas as pl
from jax.experimental.pallas import tpu as pltpu
from jax.sharding import PartitionSpec as P

D = 3072
CH = 64
TEMB = 256

GUIDANCE = 3.5
EPS_NORM = 1e-06
EPS_GAP = 1e-05
HI = lax.Precision.HIGHEST


def sinusoid(timesteps):
    half_size = TEMB // 2
    frequency = jnp.exp(-math.log(10000.0) * jnp.arange(half_size, dtype=jnp.float32) / half_size)
    angles = timesteps.astype(jnp.float32)[:, None] * frequency[None, :]
    return jnp.concatenate([jnp.cos(angles), jnp.sin(angles)], axis=1)


def condition(timesteps, pooled):
    joined = jnp.concatenate([sinusoid(timesteps), pooled.astype(jnp.float32)], axis=1)
    return jax.nn.silu(joined).astype(jnp.bfloat16)


def swap(x, axes, mask):
    count = lax.axis_size(axes)
    return lax.ppermute(x, axes, [(i, i ^ mask) for i in range(count)])


def plane_sum(x):
    if lax.axis_size("mp") != 4 or lax.axis_size("fsdp") != 2:
        return lax.psum(x, ("mp", "fsdp"))
    x = x + swap(x, "mp", 1)
    plane = ("mp", "fsdp")
    parts = [swap(x, plane, mask) for mask in (4, 1, 5)]
    return (x + parts[0]) + (parts[1] + parts[2])


def chip_blocks(x):
    pairs = []
    for m in range(4):
        for f in range(2):
            pairs.append((m * 2 + f, (m * 2 + f) ^ (4 if m % 2 == 0 else 1)))
    side = lax.ppermute(x, ("mp", "fsdp"), pairs)
    across = swap(x, ("mp", "fsdp"), 5)
    return [x, side, swap(side, "mp", 1), across]


def gather_samples(x):
    count = lax.axis_size("dp")
    if lax.axis_size("mp") != 4 or count != 4:
        blocks = lax.all_gather(x, "dp")
        return [blocks[i] for i in range(count)]
    pairs = []
    for m in range(4):
        for s in range(4):
            pairs.append((m * 4 + s, m * 4 + (s ^ (1 if m % 2 == 0 else 2))))
    near = lax.ppermute(x, ("mp", "dp"), pairs)
    far = swap(x, "dp", 3)
    return [x, near, swap(near, "mp", 1), far]


def exchange_modulation(local_mod, rows):
    if lax.axis_size("fsdp") == 2:
        f = lax.axis_index("fsdp")
        mine = lax.dynamic_slice_in_dim(local_mod, f * rows, rows, 1)
        theirs = swap(lax.dynamic_slice_in_dim(local_mod, (1 - f) * rows, rows, 1), "fsdp", 1)
        return jnp.where(f == 0, mine, theirs), jnp.where(f == 0, theirs, mine)
    whole = lax.all_gather(local_mod, "fsdp", axis=1, tiled=True)
    start = lax.axis_index("fsdp") * rows
    return (
        lax.dynamic_slice_in_dim(whole[:, :D], start, rows, 1),
        lax.dynamic_slice_in_dim(whole[:, D:], start, rows, 1),
    )


def dot(a, b, precision=HI):
    return jnp.dot(a, b, precision=precision, preferred_element_type=jnp.float32)


def both(x):
    zero = jnp.zeros_like(x)
    return jnp.concatenate(
        [jnp.concatenate([x, zero], 1), jnp.concatenate([zero, x], 1)], 0
    )


def plain_body(
    gen_noise, renoise, gen_step, renoise_step, text_pooled, embed, mod_weight, proj_weight, unembed
):
    rows, cols = proj_weight.shape[1], proj_weight.shape[2]
    f = lax.axis_index("fsdp")
    noise_all = lax.all_gather(gen_noise[0], "fsdp", axis=0, tiled=True)
    renoise_all = lax.all_gather(renoise[0], "fsdp", axis=0, tiled=True)

    blank_text = jnp.zeros_like(text_pooled)
    gen_vec = condition(gen_step, text_pooled)
    real_vec = jnp.concatenate(
        [condition(renoise_step, text_pooled), condition(renoise_step, blank_text)], 0
    )
    teacher_mod = jnp.dot(real_vec, mod_weight[1], preferred_element_type=jnp.float32)
    local_mod = jnp.concatenate(
        [
            jnp.dot(gen_vec, mod_weight[0], preferred_element_type=jnp.float32),
            GUIDANCE * teacher_mod[0:1] + (1.0 - GUIDANCE) * teacher_mod[1:2],
            jnp.dot(real_vec[0:1], mod_weight[2], preferred_element_type=jnp.float32),
        ],
        axis=0,
    )
    shift, scale = exchange_modulation(local_mod, rows)

    centred = embed.astype(jnp.float32)
    centred = centred - jnp.mean(centred, axis=2, keepdims=True)
    gram = [dot(centred[m], centred[m].T) / D for m in range(3)]
    centred_rows = lax.dynamic_slice_in_dim(centred, f * rows, rows, 2)
    embed_cols = lax.dynamic_slice_in_dim(embed, lax.axis_index("mp") * cols, cols, 2)

    pieces = []
    for m in range(3):
        through = lax.dot_general(
            proj_weight[m], unembed[m], (((1,), (1,)), ((), ())), preferred_element_type=jnp.float32
        )
        direct = lax.dot_general(
            embed_cols[m], unembed[m], (((1,), (1,)), ((), ())), preferred_element_type=jnp.float32
        )
        direct = jnp.where(f == 0, direct, 0.0)
        modulated = dot(centred_rows[m] * (1.0 + scale[m : m + 1]), through)
        offset = dot(shift[m : m + 1], through)
        offset = jnp.concatenate([offset, jnp.zeros((7, CH), jnp.float32)], 0)
        pieces.append(
            jnp.concatenate(
                [
                    jnp.concatenate([direct, modulated], 1),
                    jnp.concatenate([offset, jnp.zeros_like(offset)], 1),
                ],
                0,
            )
        )
    maps = plane_sum(jnp.concatenate(pieces, 0)).reshape(3, CH + 8, 2 * CH)
    direct = [both(maps[m, :CH, :CH]) for m in range(3)]
    modulated = [both(maps[m, :CH, CH:]) for m in range(3)]
    offset = [jnp.concatenate([maps[m, CH : CH + 1, :CH]] * 2, 1) for m in range(3)]

    ones = both(jnp.ones((CH, CH), jnp.float32))

    def normalized(u, m):
        spread = dot(dot(u, both(gram[m])) * u, ones)
        return u * lax.rsqrt(jnp.maximum(spread, 0.0) + EPS_NORM)

    def model(u, u_norm, m):
        return dot(u, direct[m]) + dot(u_norm, modulated[m]) + offset[m]

    noise = noise_all.astype(jnp.bfloat16).astype(jnp.float32)
    noise_norm = normalized(noise, 0)
    clean = model(noise, noise_norm, 0)
    level = renoise_step[0].astype(jnp.float32) / 1000.0
    noisy = (1.0 - level) * clean + level * renoise_all
    noisy = noisy.astype(jnp.bfloat16).astype(jnp.float32)
    real_v = model(noisy, normalized(noisy, 1), 1)
    fake_v = model(noisy, normalized(noisy, 2), 2)
    total = jnp.sum(jnp.abs(clean - renoise_all + real_v))
    gap_scale = level * total / (noise_all.shape[0] * 2 * CH) + EPS_GAP
    score = level * (real_v - fake_v) / gap_scale
    local_rows = gen_noise.shape[1]
    score_gap = lax.dynamic_slice_in_dim(score, f * local_rows, local_rows, 0)

    all_tokens = noise_all.shape[0] * 2 * lax.axis_size("dp")
    cotangent = (score / math.sqrt(all_tokens)).astype(jnp.bfloat16).astype(jnp.float32)
    pairs = dot(noise_norm.T, cotangent)
    outer = pairs[:CH, :CH] + pairs[CH:, CH:]
    sums = jnp.sum(cotangent, axis=0)
    sums = sums[:CH] + sums[CH:]
    payload = jnp.concatenate(
        [
            jnp.pad(outer, ((0, 0), (0, CH))),
            jnp.pad(sums[None], ((0, 7), (0, CH))),
            jnp.concatenate([shift[0], scale[0]]).reshape(-1, 2 * CH),
        ],
        0,
    )
    blocks = gather_samples(payload)
    grad_map = jnp.zeros((CH, rows), jnp.float32)
    for block in blocks:
        block_mod = block[CH + 8 :].reshape(2, rows)
        grad_map += dot(block[:CH, :CH].T, centred_rows[0]) * (1.0 + block_mod[1:2])
        grad_map += block[CH, :CH][:, None] * block_mod[0:1]
    gen_grad = lax.dot_general(
        grad_map.astype(jnp.bfloat16),
        unembed[0],
        (((0,), (0,)), ((), ())),
        preferred_element_type=jnp.float32,
    )
    return (gen_grad, score_gap[None])


def vmem_params():
    return pltpu.CompilerParams(vmem_limit_bytes=48 * 1024 * 1024)


def whole_specs(count):
    return [pl.BlockSpec(memory_space=pltpu.VMEM)] * count


def split_two(x):
    high = x.astype(jnp.bfloat16)
    return high, (x - high.astype(jnp.float32)).astype(jnp.bfloat16)


def split_three(x):
    high = x.astype(jnp.bfloat16)
    rest = x - high.astype(jnp.float32)
    middle = rest.astype(jnp.bfloat16)
    return high, middle, (rest - middle.astype(jnp.float32)).astype(jnp.bfloat16)


def lane_index(shape):
    return lax.broadcasted_iota(jnp.int32, shape, len(shape) - 1)


def block_diagonal(left_copy, right_copy):
    lanes = lane_index(left_copy.shape)
    top = jnp.where(lanes < CH, left_copy, 0.0)
    bottom = jnp.where(lanes >= CH, right_copy, 0.0)
    return jnp.concatenate([top, bottom], 0)


MOD_PIECES = 4
PROJ_PIECES = 2
IN_FLIGHT = 6
PACK = 128
CONTRACT_LAST = (((1,), (1,)), ((), ()))
CONTRACT_FIRST = (((0,), (0,)), ((), ()))


def stream_kernel(
    gen_step_ref,
    renoise_step_ref,
    text_hbm,
    noise_hbm,
    renoise_hbm,
    mod_hbm,
    proj_hbm,
    unembed_hbm,
    mod_ref,
    latents_ref,
    through_ref,
    text_ref,
    noise_ref,
    renoise_ref,
    unembed_ref,
    mod_buffer,
    proj_buffer,
    mod_sems,
    proj_sems,
    small_sems,
):
    width = mod_buffer.shape[2]
    rows, cols = proj_buffer.shape[1:]
    mod_depth = mod_buffer.shape[1] // MOD_PIECES
    proj_depth = rows // PROJ_PIECES
    mod_start = pl.multiple_of((lax.axis_index("mp") % 2) * width, 128)

    def mod_piece(m, k):
        part = pl.ds(k * mod_depth, mod_depth)
        return pltpu.make_async_copy(
            mod_hbm.at[m, part, pl.ds(mod_start, width)], mod_buffer.at[m, part], mod_sems.at[m, k]
        )

    def proj_piece(m, k):
        part = pl.ds(k * proj_depth, proj_depth)
        return pltpu.make_async_copy(
            proj_hbm.at[m, part], proj_buffer.at[m, part], proj_sems.at[m, k]
        )

    small = [
        pltpu.make_async_copy(source, target, small_sems.at[k])
        for k, (source, target) in enumerate(
            (
                (text_hbm, text_ref),
                (unembed_hbm, unembed_ref),
                (noise_hbm, noise_ref),
                (renoise_hbm, renoise_ref),
            )
        )
    ]
    order = []
    for m in range(3):
        order += [proj_piece(m, k) for k in range(PROJ_PIECES)]
        order += [mod_piece(m, k) for k in range(MOD_PIECES)]
    order = small[:2] + order[:IN_FLIGHT] + small[2:] + order[IN_FLIGHT:]
    ahead = IN_FLIGHT + 4
    for copy in order[:ahead]:
        copy.start()

    def take(position):
        order[position].wait()
        if position + ahead < len(order):
            order[position + ahead].start()

    take(0)
    half_size = TEMB // 2
    place = lane_index((8, half_size)).astype(jnp.float32)
    frequency = jnp.exp(place * (-math.log(10000.0) / half_size))
    level = lax.broadcasted_iota(jnp.int32, (8, half_size), 0)
    steps = jnp.where(level == 0, gen_step_ref[0], renoise_step_ref[0]).astype(jnp.float32)
    angles = steps * frequency
    text = jnp.broadcast_to(text_ref[...].astype(jnp.float32), (8, text_ref.shape[1]))
    text = jnp.where(lax.broadcasted_iota(jnp.int32, text.shape, 0) < 2, text, 0.0)
    joined = jnp.concatenate([jnp.cos(angles), jnp.sin(angles), text], 1)
    vectors = (joined / (1.0 + jnp.exp(-joined))).astype(jnp.bfloat16)
    packs = width // PACK
    mod_ref[...] = jnp.zeros_like(mod_ref)
    take(1)
    place = 2
    for m in range(3):
        total = jnp.zeros((8, width), jnp.float32)
        for k in range(PROJ_PIECES + MOD_PIECES):
            if place == IN_FLIGHT + 2:
                take(place)
                take(place + 1)
                latents = jnp.where(lax.axis_index("mp") % 2 == 0, noise_ref[...], renoise_ref[...])
                latents_ref[...] = latents.astype(jnp.bfloat16)
                place += 2
            take(place)
            place += 1
            if k < PROJ_PIECES:
                part = slice(k * proj_depth, (k + 1) * proj_depth)
                through_ref[m, :, part] = lax.dot_general(
                    unembed_ref[m],
                    proj_buffer[m, part],
                    CONTRACT_LAST,
                    preferred_element_type=jnp.float32,
                ).astype(jnp.bfloat16)
            else:
                part = slice((k - PROJ_PIECES) * mod_depth, (k - PROJ_PIECES + 1) * mod_depth)
                total += jnp.dot(
                    vectors[:, part], mod_buffer[m, part], preferred_element_type=jnp.float32
                )
        if m == 0:
            line = total[0:1]
        elif m == 1:
            line = GUIDANCE * total[1:2] + (1.0 - GUIDANCE) * total[2:3]
        else:
            line = total[1:2]
        for j in range(packs):
            mod_ref[m * packs + j : m * packs + j + 1] = line[:, j * PACK : (j + 1) * PACK]


def streamed_weights(
    gen_step, renoise_step, text, noise, renoise, mod_weight, proj_weight, unembed
):
    depth, width = mod_weight.shape[1], mod_weight.shape[2] // 2
    rows, cols = proj_weight.shape[1:]
    pack_rows = -(-3 * width // PACK // 8) * 8
    return pl.pallas_call(
        stream_kernel,
        out_shape=[
            jax.ShapeDtypeStruct((pack_rows, PACK), jnp.float32),
            jax.ShapeDtypeStruct(noise.shape, jnp.bfloat16),
            jax.ShapeDtypeStruct((3, CH, rows), jnp.bfloat16),
        ],
        in_specs=[pl.BlockSpec(memory_space=pltpu.SMEM)] * 2
        + [pl.BlockSpec(memory_space=pltpu.HBM)] * 6,
        out_specs=whole_specs(3),
        scratch_shapes=[
            pltpu.VMEM(text.shape, text.dtype),
            pltpu.VMEM(noise.shape, noise.dtype),
            pltpu.VMEM(renoise.shape, renoise.dtype),
            pltpu.VMEM(unembed.shape, unembed.dtype),
            pltpu.VMEM((3, depth, width), jnp.bfloat16),
            pltpu.VMEM((3, rows, cols), jnp.bfloat16),
            pltpu.SemaphoreType.DMA((3, MOD_PIECES)),
            pltpu.SemaphoreType.DMA((3, PROJ_PIECES)),
            pltpu.SemaphoreType.DMA((4,)),
        ],
        compiler_params=vmem_params(),
        name="stream_weights",
    )(
        gen_step,
        renoise_step,
        *(
            pltpu.with_memory_space_constraint(x, pltpu.HBM)
            for x in (text, noise, renoise, mod_weight, proj_weight, unembed)
        ),
    )


def embed_kernel(embed_ref, unembed_ref, gram_ref, rows_ref, direct_ref):
    rows, cols = rows_ref.shape[2], unembed_ref.shape[2]
    f = lax.axis_index("fsdp")
    row_start = pl.multiple_of(f * rows, 128)
    col_start = pl.multiple_of(lax.axis_index("mp") * cols, 128)
    nothing = jnp.zeros((CH, cols), jnp.bfloat16)
    for m in range(3):
        whole = embed_ref[m].astype(jnp.float32)
        average = jnp.sum(whole, axis=1, keepdims=True) * (1.0 / D)
        rows_ref[m] = embed_ref[m, :, pl.ds(row_start, rows)].astype(jnp.float32) - average
        direct = lax.dot_general(
            embed_ref[m, :, pl.ds(col_start, cols)],
            jnp.concatenate([unembed_ref[m], nothing], 0),
            CONTRACT_LAST,
            preferred_element_type=jnp.float32,
        )
        direct_ref[m] = jnp.where(f == 0, direct, 0.0)
        pair = jnp.concatenate(split_two(whole - average), 0)
        product = lax.dot_general(pair, pair, CONTRACT_LAST, preferred_element_type=jnp.float32)
        product = product[:CH] + product[CH:]
        gram = (product + pltpu.roll(product, CH, 1)) * (1.0 / D)
        gram_ref[m] = jnp.concatenate(split_three(block_diagonal(gram, gram)), 1)


def embed_products(embed, unembed, rows):
    return pl.pallas_call(
        embed_kernel,
        out_shape=[
            jax.ShapeDtypeStruct((3, 2 * CH, 6 * CH), jnp.bfloat16),
            jax.ShapeDtypeStruct((3, CH, rows), jnp.float32),
            jax.ShapeDtypeStruct((3, CH, 2 * CH), jnp.float32),
        ],
        in_specs=whole_specs(2),
        out_specs=whole_specs(3),
        compiler_params=vmem_params(),
        cost_estimate=pl.CostEstimate(
            flops=6 * 128 * 128 * D, bytes_accessed=6 * CH * D, transcendentals=0
        ),
        name="embed_products",
    )(embed, unembed)


def pair_ones():
    shape = (2 * CH, 2 * CH)
    lanes = lane_index(shape)
    subs = lax.broadcasted_iota(jnp.int32, shape, 0)
    ones = jnp.where((lanes < CH) == (subs < CH), 1.0, 0.0).astype(jnp.bfloat16)
    return jnp.concatenate([ones, ones], 0)


def inverse_deviation(u, by_gram, ones):
    squares = jnp.concatenate(split_two(by_gram * u), 1)
    spread = jnp.dot(squares, ones, preferred_element_type=jnp.float32)
    return lax.rsqrt(jnp.maximum(spread, 0.0) + EPS_NORM)


def columns(product, i):
    return product[:, i * 2 * CH : (i + 1) * 2 * CH]


def sample_latents(noise_ref, first_ref, second_ref):
    first, second = first_ref[...], second_ref[...]
    core = lax.axis_index("mp") % 2
    other = jnp.where(core == 0, first, second)
    other_renoise = jnp.where(core == 0, second, first)
    return jnp.concatenate([noise_ref[...].astype(jnp.bfloat16), other], 0), other_renoise


def noise_kernel(noise_ref, first_ref, second_ref, gram_ref, inverse_ref, normal_ref):
    noise, _ = sample_latents(noise_ref, first_ref, second_ref)
    product = jnp.dot(noise, gram_ref[0], preferred_element_type=jnp.float32)
    noise = noise.astype(jnp.float32)
    by_gram = columns(product, 0) + columns(product, 1) + columns(product, 2)
    inverse = inverse_deviation(noise, by_gram, pair_ones())
    inverse_ref[...] = inverse
    normal_ref[...] = (noise * inverse).astype(jnp.bfloat16)


def noise_statistics(noise, first, second, gram):
    shape = (2 * noise.shape[0], noise.shape[1])
    return pl.pallas_call(
        noise_kernel,
        out_shape=[
            jax.ShapeDtypeStruct(shape, jnp.float32),
            jax.ShapeDtypeStruct(shape, jnp.bfloat16),
        ],
        in_specs=whole_specs(4),
        out_specs=whole_specs(2),
        compiler_params=vmem_params(),
        name="noise_statistics",
    )(noise, first, second, gram)


def maps_kernel(kept_ref, got_ref, rows_ref, through_ref, direct_ref, maps_ref, mod_ref):
    rows = rows_ref.shape[2]
    packs = rows // PACK
    f = lax.axis_index("fsdp")
    kept, got = kept_ref[...], got_ref[...]
    shift = jnp.where(f == 0, kept, got)
    scale = jnp.where(f == 0, got, kept)
    for m in range(3):
        pieces = []
        for j in range(packs):
            line = slice(m * packs + j, m * packs + j + 1)
            pieces.append(
                jnp.concatenate(
                    [
                        rows_ref[m, :, j * PACK : (j + 1) * PACK] * (1.0 + scale[line]),
                        shift[line],
                        jnp.zeros((7, PACK), jnp.float32),
                    ],
                    0,
                )
            )
        left = jnp.concatenate(pieces, 1).astype(jnp.bfloat16)
        through = jnp.concatenate([jnp.zeros((CH, rows), jnp.bfloat16), through_ref[m]], 0)
        product = lax.dot_general(
            left, through, CONTRACT_LAST, preferred_element_type=jnp.float32
        )
        base = m * (CH + 8)
        maps_ref[base : base + CH] = product[:CH] + direct_ref[m]
        maps_ref[base + CH : base + CH + 8] = product[CH:]
    rest = jnp.zeros((mod_ref.shape[0] - 2 * packs, PACK), jnp.float32)
    mod_ref[...] = jnp.concatenate([shift[:packs], scale[:packs], rest], 0).astype(jnp.bfloat16)


def modulated_maps(kept, got, rows_part, through, direct):
    packs = rows_part.shape[2] // PACK
    return pl.pallas_call(
        maps_kernel,
        out_shape=[
            jax.ShapeDtypeStruct((3 * (CH + 8), 2 * CH), jnp.float32),
            jax.ShapeDtypeStruct((-(-2 * packs // 16) * 16, PACK), jnp.bfloat16),
        ],
        in_specs=whole_specs(5),
        out_specs=whole_specs(2),
        compiler_params=vmem_params(),
        name="modulated_maps",
    )(kept, got, rows_part, through, direct)


MAP_ROWS = CH + 16


def token_kernel(
    level_ref,
    noise_ref,
    first_ref,
    second_ref,
    renoise_ref,
    inverse_ref,
    normal_ref,
    gram_ref,
    maps_a,
    maps_b,
    maps_c,
    maps_d,
    mod_ref,
    score_ref,
    payload_ref,
):
    half = renoise_ref.shape[0]
    level = level_ref[0]
    maps = [part[...].astype(jnp.float32) for part in (maps_a, maps_b, maps_c, maps_d)]
    maps = (maps[0] + maps[1]) + (maps[2] + maps[3])
    width = 2 * CH
    ones = pair_ones()

    def model_matrix(m):
        base = m * (CH + 8)
        pair = maps[base : base + CH]
        turned = pltpu.roll(pair, CH, 1)
        direct = split_two(block_diagonal(pair, turned))
        modulated = split_two(block_diagonal(turned, pair))
        offset = maps[base + CH : base + CH + 1]
        return jnp.concatenate(direct + modulated, 1), offset + pltpu.roll(offset, CH, 1)

    def combine(product, inverse, offset):
        direct = columns(product, 0) + columns(product, 1)
        return direct + inverse * (columns(product, 2) + columns(product, 3)) + offset

    noise, other_renoise = sample_latents(noise_ref, first_ref, second_ref)
    renoise = jnp.concatenate([renoise_ref[...], other_renoise.astype(jnp.float32)], 0)
    matrix, offset = model_matrix(0)
    product = jnp.dot(noise, matrix, preferred_element_type=jnp.float32)
    clean = combine(product, inverse_ref[...], offset)
    noisy = ((1.0 - level) * clean + level * renoise).astype(jnp.bfloat16)
    noisy_wide = noisy.astype(jnp.float32)

    def velocity(m):
        matrix, offset = model_matrix(m)
        matrix = jnp.concatenate([matrix, gram_ref[m]], 1)
        product = jnp.dot(noisy, matrix, preferred_element_type=jnp.float32)
        by_gram = columns(product, 4) + columns(product, 5) + columns(product, 6)
        return combine(product, inverse_deviation(noisy_wide, by_gram, ones), offset)

    real_v = velocity(1)
    fake_v = velocity(2)
    total = jnp.sum(jnp.abs(clean - renoise + real_v))
    gap_scale = level * total * (1.0 / (2 * half * width)) + EPS_GAP
    score = level * (real_v - fake_v) / gap_scale
    score_ref[...] = score[:half]
    tokens = 4 * half * lax.axis_size("dp")
    cotangent = (score * (1.0 / math.sqrt(tokens))).astype(jnp.bfloat16)
    pairs = lax.dot_general(
        normal_ref[...], cotangent, CONTRACT_FIRST, preferred_element_type=jnp.float32
    )
    outer = pairs[:CH] + pltpu.roll(pairs[CH:], CH, 1)
    sums = jnp.sum(cotangent.astype(jnp.float32), axis=0, keepdims=True)
    sums = sums + pltpu.roll(sums, CH, 1)
    rest = jnp.zeros((MAP_ROWS - CH - 1, width), jnp.float32)
    payload_ref[:MAP_ROWS] = jnp.concatenate([outer, sums, rest], 0).astype(jnp.bfloat16)
    payload_ref[MAP_ROWS:] = mod_ref[...]


def token_phase(level, noise, first, second, renoise, inverse, normal, gram, maps, mod):
    return pl.pallas_call(
        token_kernel,
        out_shape=[
            jax.ShapeDtypeStruct(renoise.shape, jnp.float32),
            jax.ShapeDtypeStruct((MAP_ROWS + mod.shape[0], 2 * CH), jnp.bfloat16),
        ],
        in_specs=[pl.BlockSpec(memory_space=pltpu.SMEM)] + whole_specs(12),
        out_specs=whole_specs(2),
        compiler_params=vmem_params(),
        name="tokens",
    )(level, noise, first, second, renoise, inverse, normal, gram, *maps, mod)


GRAD_PIECES = 6


def grad_kernel(
    block_a,
    block_b,
    block_c,
    block_d,
    rows_ref,
    unembed_ref,
    score_ref,
    grad_hbm,
    score_hbm,
    buffer,
    sems,
):
    score_copy = pltpu.make_async_copy(score_ref, score_hbm, sems.at[GRAD_PIECES])
    score_copy.start()
    rows = rows_ref.shape[2]
    packs = rows // PACK
    depth = rows // GRAD_PIECES
    blocks = [block[...] for block in (block_a, block_b, block_c, block_d)]
    left = jnp.concatenate([block[:MAP_ROWS, :CH] for block in blocks], 0)
    mods = [block[MAP_ROWS:].astype(jnp.float32) for block in blocks]
    unembed = unembed_ref[0]

    def piece(k):
        part = pl.ds(k * depth, depth)
        return pltpu.make_async_copy(buffer.at[part], grad_hbm.at[part], sems.at[k])

    tiles = []
    for j in range(packs):
        embed_tile = rows_ref[0, :, j * PACK : (j + 1) * PACK]
        column = []
        for mod in mods:
            column += [
                embed_tile * (1.0 + mod[packs + j : packs + j + 1]),
                mod[j : j + 1],
                jnp.zeros((MAP_ROWS - CH - 1, PACK), jnp.float32),
            ]
        tiles.append(jnp.concatenate(column, 0).astype(jnp.bfloat16))
    grad_map = lax.dot_general(
        left, jnp.concatenate(tiles, 1), CONTRACT_FIRST, preferred_element_type=jnp.float32
    ).astype(jnp.bfloat16)
    for k in range(GRAD_PIECES):
        part = slice(k * depth, (k + 1) * depth)
        buffer[part] = lax.dot_general(
            grad_map[:, part], unembed, CONTRACT_FIRST, preferred_element_type=jnp.float32
        )
        piece(k).start()
    for k in range(GRAD_PIECES):
        piece(k).wait()
    score_copy.wait()


def gradient(blocks, rows_part, unembed, score):
    rows = rows_part.shape[2]
    cols = unembed.shape[2]
    return pl.pallas_call(
        grad_kernel,
        out_shape=[
            jax.ShapeDtypeStruct((rows, cols), jnp.float32),
            jax.ShapeDtypeStruct(score.shape, jnp.float32),
        ],
        in_specs=whole_specs(7),
        out_specs=[pl.BlockSpec(memory_space=pl.ANY)] * 2,
        scratch_shapes=[
            pltpu.VMEM((rows, cols), jnp.float32),
            pltpu.SemaphoreType.DMA((GRAD_PIECES + 1,)),
        ],
        compiler_params=vmem_params(),
        name="gradient",
    )(*blocks, rows_part, unembed, score)


def body(
    gen_noise, renoise, gen_step, renoise_step, text_pooled, embed, mod_weight, proj_weight, unembed
):
    mine, latents, through = streamed_weights(
        gen_step,
        renoise_step,
        text_pooled,
        gen_noise[0],
        renoise[0],
        mod_weight,
        proj_weight,
        unembed,
    )
    f = lax.axis_index("fsdp")
    theirs = swap(mine, "mp", 1)
    own_half = lax.axis_index("mp") % 2 == f
    kept = jnp.where(own_half, mine, theirs)
    got = swap(jnp.where(own_half, theirs, mine), "fsdp", 1)
    first = swap(latents, "fsdp", 1)
    got, first = lax.optimization_barrier((got, first))
    second = swap(first, "mp", 1)
    gram, rows_part, direct = embed_products(embed, unembed, proj_weight.shape[1])
    maps, mod = modulated_maps(kept, got, rows_part, through, direct)
    maps = (maps + swap(maps, "mp", 1)).astype(jnp.bfloat16)
    inverse, normal = noise_statistics(gen_noise[0], first, second, gram)
    maps = chip_blocks(maps)
    level = renoise_step.astype(jnp.float32) / 1000.0
    score, payload = token_phase(
        level, gen_noise[0], first, second, renoise[0], inverse, normal, gram, maps, mod
    )
    blocks = gather_samples(payload)
    gen_grad, score_gap = gradient(blocks, rows_part, unembed, score)
    return (gen_grad, score_gap[None])


def fits_kernels(mesh):
    return mesh.shape["mp"] == 4 and mesh.shape["fsdp"] == 2 and mesh.shape["dp"] == 4


def solution(mesh):
    return jax.shard_map(
        body if fits_kernels(mesh) else plain_body,
        mesh=mesh,
        in_specs=(
            P("dp", "fsdp", None),
            P("dp", "fsdp", None),
            P("dp"),
            P("dp"),
            P("dp", None),
            P(),
            P(None, None, "fsdp"),
            P(None, "fsdp", "mp"),
            P(None, None, "mp"),
        ),
        out_specs=(P("fsdp", "mp"), P("dp", "fsdp", None)),
        check_vma=False,
    )
```

```python
import math

import jax
import jax.numpy as jnp
from jax import lax
from jax.experimental import pallas as pl
from jax.experimental.pallas import tpu as pltpu
from jax.sharding import PartitionSpec as P

D = 3072
CH = 64
TEMB = 256

GUIDANCE = 3.5
EPS_NORM = 1e-06
EPS_GAP = 1e-05
HI = lax.Precision.HIGHEST


def sinusoid(timesteps):
    half_size = TEMB // 2
    frequency = jnp.exp(-math.log(10000.0) * jnp.arange(half_size, dtype=jnp.float32) / half_size)
    angles = timesteps.astype(jnp.float32)[:, None] * frequency[None, :]
    return jnp.concatenate([jnp.cos(angles), jnp.sin(angles)], axis=1)


def condition(timesteps, pooled):
    joined = jnp.concatenate([sinusoid(timesteps), pooled.astype(jnp.float32)], axis=1)
    return jax.nn.silu(joined).astype(jnp.bfloat16)


def swap(x, axes, mask):
    count = lax.axis_size(axes)
    return lax.ppermute(x, axes, [(i, i ^ mask) for i in range(count)])


def plane_sum(x):
    if lax.axis_size("mp") != 4 or lax.axis_size("fsdp") != 2:
        return lax.psum(x, ("mp", "fsdp"))
    x = x + swap(x, "mp", 1)
    plane = ("mp", "fsdp")
    parts = [swap(x, plane, mask) for mask in (4, 1, 5)]
    return (x + parts[0]) + (parts[1] + parts[2])


def chip_blocks(x):
    pairs = []
    for m in range(4):
        for f in range(2):
            pairs.append((m * 2 + f, (m * 2 + f) ^ (4 if m % 2 == 0 else 1)))
    side = lax.ppermute(x, ("mp", "fsdp"), pairs)
    across = swap(x, ("mp", "fsdp"), 5)
    return [x, side, swap(side, "mp", 1), across]


def gather_samples(x):
    count = lax.axis_size("dp")
    if lax.axis_size("mp") != 4 or count != 4:
        blocks = lax.all_gather(x, "dp")
        return [blocks[i] for i in range(count)]
    pairs = []
    for m in range(4):
        for s in range(4):
            pairs.append((m * 4 + s, m * 4 + (s ^ (1 if m % 2 == 0 else 2))))
    near = lax.ppermute(x, ("mp", "dp"), pairs)
    far = swap(x, "dp", 3)
    return [x, near, swap(near, "mp", 1), far]


def exchange_modulation(local_mod, rows):
    if lax.axis_size("fsdp") == 2:
        f = lax.axis_index("fsdp")
        mine = lax.dynamic_slice_in_dim(local_mod, f * rows, rows, 1)
        theirs = swap(lax.dynamic_slice_in_dim(local_mod, (1 - f) * rows, rows, 1), "fsdp", 1)
        return jnp.where(f == 0, mine, theirs), jnp.where(f == 0, theirs, mine)
    whole = lax.all_gather(local_mod, "fsdp", axis=1, tiled=True)
    start = lax.axis_index("fsdp") * rows
    return (
        lax.dynamic_slice_in_dim(whole[:, :D], start, rows, 1),
        lax.dynamic_slice_in_dim(whole[:, D:], start, rows, 1),
    )


def dot(a, b, precision=HI):
    return jnp.dot(a, b, precision=precision, preferred_element_type=jnp.float32)


def both(x):
    zero = jnp.zeros_like(x)
    return jnp.concatenate(
        [jnp.concatenate([x, zero], 1), jnp.concatenate([zero, x], 1)], 0
    )


def plain_body(
    gen_noise, renoise, gen_step, renoise_step, text_pooled, embed, mod_weight, proj_weight, unembed
):
    rows, cols = proj_weight.shape[1], proj_weight.shape[2]
    f = lax.axis_index("fsdp")
    noise_all = lax.all_gather(gen_noise[0], "fsdp", axis=0, tiled=True)
    renoise_all = lax.all_gather(renoise[0], "fsdp", axis=0, tiled=True)

    blank_text = jnp.zeros_like(text_pooled)
    gen_vec = condition(gen_step, text_pooled)
    real_vec = jnp.concatenate(
        [condition(renoise_step, text_pooled), condition(renoise_step, blank_text)], 0
    )
    teacher_mod = jnp.dot(real_vec, mod_weight[1], preferred_element_type=jnp.float32)
    local_mod = jnp.concatenate(
        [
            jnp.dot(gen_vec, mod_weight[0], preferred_element_type=jnp.float32),
            GUIDANCE * teacher_mod[0:1] + (1.0 - GUIDANCE) * teacher_mod[1:2],
            jnp.dot(real_vec[0:1], mod_weight[2], preferred_element_type=jnp.float32),
        ],
        axis=0,
    )
    shift, scale = exchange_modulation(local_mod, rows)

    centred = embed.astype(jnp.float32)
    centred = centred - jnp.mean(centred, axis=2, keepdims=True)
    gram = [dot(centred[m], centred[m].T) / D for m in range(3)]
    centred_rows = lax.dynamic_slice_in_dim(centred, f * rows, rows, 2)
    embed_cols = lax.dynamic_slice_in_dim(embed, lax.axis_index("mp") * cols, cols, 2)

    pieces = []
    for m in range(3):
        through = lax.dot_general(
            proj_weight[m], unembed[m], (((1,), (1,)), ((), ())), preferred_element_type=jnp.float32
        )
        direct = lax.dot_general(
            embed_cols[m], unembed[m], (((1,), (1,)), ((), ())), preferred_element_type=jnp.float32
        )
        direct = jnp.where(f == 0, direct, 0.0)
        modulated = dot(centred_rows[m] * (1.0 + scale[m : m + 1]), through)
        offset = dot(shift[m : m + 1], through)
        offset = jnp.concatenate([offset, jnp.zeros((7, CH), jnp.float32)], 0)
        pieces.append(
            jnp.concatenate(
                [
                    jnp.concatenate([direct, modulated], 1),
                    jnp.concatenate([offset, jnp.zeros_like(offset)], 1),
                ],
                0,
            )
        )
    maps = plane_sum(jnp.concatenate(pieces, 0)).reshape(3, CH + 8, 2 * CH)
    direct = [both(maps[m, :CH, :CH]) for m in range(3)]
    modulated = [both(maps[m, :CH, CH:]) for m in range(3)]
    offset = [jnp.concatenate([maps[m, CH : CH + 1, :CH]] * 2, 1) for m in range(3)]

    ones = both(jnp.ones((CH, CH), jnp.float32))

    def normalized(u, m):
        spread = dot(dot(u, both(gram[m])) * u, ones)
        return u * lax.rsqrt(jnp.maximum(spread, 0.0) + EPS_NORM)

    def model(u, u_norm, m):
        return dot(u, direct[m]) + dot(u_norm, modulated[m]) + offset[m]

    noise = noise_all.astype(jnp.bfloat16).astype(jnp.float32)
    noise_norm = normalized(noise, 0)
    clean = model(noise, noise_norm, 0)
    level = renoise_step[0].astype(jnp.float32) / 1000.0
    noisy = (1.0 - level) * clean + level * renoise_all
    noisy = noisy.astype(jnp.bfloat16).astype(jnp.float32)
    real_v = model(noisy, normalized(noisy, 1), 1)
    fake_v = model(noisy, normalized(noisy, 2), 2)
    total = jnp.sum(jnp.abs(clean - renoise_all + real_v))
    gap_scale = level * total / (noise_all.shape[0] * 2 * CH) + EPS_GAP
    score = level * (real_v - fake_v) / gap_scale
    local_rows = gen_noise.shape[1]
    score_gap = lax.dynamic_slice_in_dim(score, f * local_rows, local_rows, 0)

    all_tokens = noise_all.shape[0] * 2 * lax.axis_size("dp")
    cotangent = (score / math.sqrt(all_tokens)).astype(jnp.bfloat16).astype(jnp.float32)
    pairs = dot(noise_norm.T, cotangent)
    outer = pairs[:CH, :CH] + pairs[CH:, CH:]
    sums = jnp.sum(cotangent, axis=0)
    sums = sums[:CH] + sums[CH:]
    payload = jnp.concatenate(
        [
            jnp.pad(outer, ((0, 0), (0, CH))),
            jnp.pad(sums[None], ((0, 7), (0, CH))),
            jnp.concatenate([shift[0], scale[0]]).reshape(-1, 2 * CH),
        ],
        0,
    )
    blocks = gather_samples(payload)
    grad_map = jnp.zeros((CH, rows), jnp.float32)
    for block in blocks:
        block_mod = block[CH + 8 :].reshape(2, rows)
        grad_map += dot(block[:CH, :CH].T, centred_rows[0]) * (1.0 + block_mod[1:2])
        grad_map += block[CH, :CH][:, None] * block_mod[0:1]
    gen_grad = lax.dot_general(
        grad_map.astype(jnp.bfloat16),
        unembed[0],
        (((0,), (0,)), ((), ())),
        preferred_element_type=jnp.float32,
    )
    return (gen_grad, score_gap[None])


def vmem_params():
    return pltpu.CompilerParams(vmem_limit_bytes=48 * 1024 * 1024)


def whole_specs(count):
    return [pl.BlockSpec(memory_space=pltpu.VMEM)] * count


def split_two(x):
    high = x.astype(jnp.bfloat16)
    return high, (x - high.astype(jnp.float32)).astype(jnp.bfloat16)


def split_three(x):
    high = x.astype(jnp.bfloat16)
    rest = x - high.astype(jnp.float32)
    middle = rest.astype(jnp.bfloat16)
    return high, middle, (rest - middle.astype(jnp.float32)).astype(jnp.bfloat16)


def lane_index(shape):
    return lax.broadcasted_iota(jnp.int32, shape, len(shape) - 1)


def block_diagonal(left_copy, right_copy):
    lanes = lane_index(left_copy.shape)
    top = jnp.where(lanes < CH, left_copy, 0.0)
    bottom = jnp.where(lanes >= CH, right_copy, 0.0)
    return jnp.concatenate([top, bottom], 0)


MOD_PIECES = 4
PROJ_PIECES = 3
IN_FLIGHT = 12
LATENTS_AFTER = 8
PACK = 128
CONTRACT_LAST = (((1,), (1,)), ((), ()))
CONTRACT_FIRST = (((0,), (0,)), ((), ()))


def stream_kernel(
    gen_step_ref,
    renoise_step_ref,
    text_hbm,
    noise_hbm,
    renoise_hbm,
    mod_hbm,
    proj_hbm,
    unembed_hbm,
    mod_ref,
    latents_ref,
    through_ref,
    text_ref,
    noise_ref,
    renoise_ref,
    unembed_ref,
    mod_buffer,
    proj_buffer,
    mod_sems,
    proj_sems,
    small_sems,
):
    width = mod_buffer.shape[2]
    rows, cols = proj_buffer.shape[1:]
    mod_depth = mod_buffer.shape[1] // MOD_PIECES
    proj_depth = rows // PROJ_PIECES
    mod_start = pl.multiple_of((lax.axis_index("mp") % 2) * width, 128)

    def mod_piece(m, k):
        part = pl.ds(k * mod_depth, mod_depth)
        return pltpu.make_async_copy(
            mod_hbm.at[m, part, pl.ds(mod_start, width)], mod_buffer.at[m, part], mod_sems.at[m, k]
        )

    def proj_piece(m, k):
        part = pl.ds(k * proj_depth, proj_depth)
        return pltpu.make_async_copy(
            proj_hbm.at[m, part], proj_buffer.at[m, part], proj_sems.at[m, k]
        )

    small = [
        pltpu.make_async_copy(source, target, small_sems.at[k])
        for k, (source, target) in enumerate(
            (
                (text_hbm, text_ref),
                (unembed_hbm, unembed_ref),
                (noise_hbm, noise_ref),
                (renoise_hbm, renoise_ref),
            )
        )
    ]
    order = []
    for m in range(3):
        order += [proj_piece(m, k) for k in range(PROJ_PIECES)]
        order += [mod_piece(m, k) for k in range(MOD_PIECES)]
    order = small[:2] + order[:LATENTS_AFTER] + small[2:] + order[LATENTS_AFTER:]
    for copy in order[:IN_FLIGHT]:
        copy.start()

    def take(position):
        order[position].wait()
        if position + IN_FLIGHT < len(order):
            order[position + IN_FLIGHT].start()

    take(0)
    half_size = TEMB // 2
    place = lane_index((8, half_size)).astype(jnp.float32)
    frequency = jnp.exp(place * (-math.log(10000.0) / half_size))
    level = lax.broadcasted_iota(jnp.int32, (8, half_size), 0)
    steps = jnp.where(level == 0, gen_step_ref[0], renoise_step_ref[0]).astype(jnp.float32)
    angles = steps * frequency
    text = jnp.broadcast_to(text_ref[...].astype(jnp.float32), (8, text_ref.shape[1]))
    text = jnp.where(lax.broadcasted_iota(jnp.int32, text.shape, 0) < 2, text, 0.0)
    joined = jnp.concatenate([jnp.cos(angles), jnp.sin(angles), text], 1)
    vectors = (joined / (1.0 + jnp.exp(-joined))).astype(jnp.bfloat16)
    packs = width // PACK
    mod_ref[...] = jnp.zeros_like(mod_ref)
    take(1)
    place = 2
    for m in range(3):
        total = jnp.zeros((8, width), jnp.float32)
        for k in range(PROJ_PIECES + MOD_PIECES):
            if place == LATENTS_AFTER + 2:
                take(place)
                take(place + 1)
                latents = jnp.where(lax.axis_index("mp") % 2 == 0, noise_ref[...], renoise_ref[...])
                latents_ref[...] = latents.astype(jnp.bfloat16)
                place += 2
            take(place)
            place += 1
            if k < PROJ_PIECES:
                part = slice(k * proj_depth, (k + 1) * proj_depth)
                through_ref[m, :, part] = lax.dot_general(
                    unembed_ref[m],
                    proj_buffer[m, part],
                    CONTRACT_LAST,
                    preferred_element_type=jnp.float32,
                ).astype(jnp.bfloat16)
            else:
                part = slice((k - PROJ_PIECES) * mod_depth, (k - PROJ_PIECES + 1) * mod_depth)
                total += jnp.dot(
                    vectors[:, part], mod_buffer[m, part], preferred_element_type=jnp.float32
                )
        if m == 0:
            line = total[0:1]
        elif m == 1:
            line = GUIDANCE * total[1:2] + (1.0 - GUIDANCE) * total[2:3]
        else:
            line = total[1:2]
        for j in range(packs):
            mod_ref[m * packs + j : m * packs + j + 1] = line[:, j * PACK : (j + 1) * PACK]


def streamed_weights(
    gen_step, renoise_step, text, noise, renoise, mod_weight, proj_weight, unembed
):
    depth, width = mod_weight.shape[1], mod_weight.shape[2] // 2
    rows, cols = proj_weight.shape[1:]
    pack_rows = -(-3 * width // PACK // 8) * 8
    return pl.pallas_call(
        stream_kernel,
        out_shape=[
            jax.ShapeDtypeStruct((pack_rows, PACK), jnp.float32),
            jax.ShapeDtypeStruct(noise.shape, jnp.bfloat16),
            jax.ShapeDtypeStruct((3, CH, rows), jnp.bfloat16),
        ],
        in_specs=[pl.BlockSpec(memory_space=pltpu.SMEM)] * 2
        + [pl.BlockSpec(memory_space=pltpu.HBM)] * 6,
        out_specs=whole_specs(3),
        scratch_shapes=[
            pltpu.VMEM(text.shape, text.dtype),
            pltpu.VMEM(noise.shape, noise.dtype),
            pltpu.VMEM(renoise.shape, renoise.dtype),
            pltpu.VMEM(unembed.shape, unembed.dtype),
            pltpu.VMEM((3, depth, width), jnp.bfloat16),
            pltpu.VMEM((3, rows, cols), jnp.bfloat16),
            pltpu.SemaphoreType.DMA((3, MOD_PIECES)),
            pltpu.SemaphoreType.DMA((3, PROJ_PIECES)),
            pltpu.SemaphoreType.DMA((4,)),
        ],
        compiler_params=vmem_params(),
        name="stream_weights",
    )(
        gen_step,
        renoise_step,
        *(
            pltpu.with_memory_space_constraint(x, pltpu.HBM)
            for x in (text, noise, renoise, mod_weight, proj_weight, unembed)
        ),
    )


def embed_kernel(embed_ref, unembed_ref, gram_ref, rows_ref, direct_ref):
    rows, cols = rows_ref.shape[2], unembed_ref.shape[2]
    f = lax.axis_index("fsdp")
    row_start = pl.multiple_of(f * rows, 128)
    col_start = pl.multiple_of(lax.axis_index("mp") * cols, 128)
    nothing = jnp.zeros((CH, cols), jnp.bfloat16)
    for m in range(3):
        whole = embed_ref[m].astype(jnp.float32)
        average = jnp.sum(whole, axis=1, keepdims=True) * (1.0 / D)
        rows_ref[m] = embed_ref[m, :, pl.ds(row_start, rows)].astype(jnp.float32) - average
        direct = lax.dot_general(
            embed_ref[m, :, pl.ds(col_start, cols)],
            jnp.concatenate([unembed_ref[m], nothing], 0),
            CONTRACT_LAST,
            preferred_element_type=jnp.float32,
        )
        direct_ref[m] = jnp.where(f == 0, direct, 0.0)
        pair = jnp.concatenate(split_two(whole - average), 0)
        product = lax.dot_general(pair, pair, CONTRACT_LAST, preferred_element_type=jnp.float32)
        product = product[:CH] + product[CH:]
        gram = (product + pltpu.roll(product, CH, 1)) * (1.0 / D)
        gram_ref[m] = jnp.concatenate(split_three(block_diagonal(gram, gram)), 1)


def embed_products(embed, unembed, rows):
    return pl.pallas_call(
        embed_kernel,
        out_shape=[
            jax.ShapeDtypeStruct((3, 2 * CH, 6 * CH), jnp.bfloat16),
            jax.ShapeDtypeStruct((3, CH, rows), jnp.float32),
            jax.ShapeDtypeStruct((3, CH, 2 * CH), jnp.float32),
        ],
        in_specs=whole_specs(2),
        out_specs=whole_specs(3),
        compiler_params=vmem_params(),
        cost_estimate=pl.CostEstimate(
            flops=6 * 128 * 128 * D, bytes_accessed=6 * CH * D, transcendentals=0
        ),
        name="embed_products",
    )(embed, unembed)


def pair_ones():
    shape = (2 * CH, 2 * CH)
    lanes = lane_index(shape)
    subs = lax.broadcasted_iota(jnp.int32, shape, 0)
    ones = jnp.where((lanes < CH) == (subs < CH), 1.0, 0.0).astype(jnp.bfloat16)
    return jnp.concatenate([ones, ones], 0)


def inverse_deviation(u, by_gram, ones):
    squares = jnp.concatenate(split_two(by_gram * u), 1)
    spread = jnp.dot(squares, ones, preferred_element_type=jnp.float32)
    return lax.rsqrt(jnp.maximum(spread, 0.0) + EPS_NORM)


def columns(product, i):
    return product[:, i * 2 * CH : (i + 1) * 2 * CH]


def sample_latents(noise_ref, first_ref, second_ref):
    first, second = first_ref[...], second_ref[...]
    core = lax.axis_index("mp") % 2
    other = jnp.where(core == 0, first, second)
    other_renoise = jnp.where(core == 0, second, first)
    return jnp.concatenate([noise_ref[...].astype(jnp.bfloat16), other], 0), other_renoise


def noise_kernel(noise_ref, first_ref, second_ref, gram_ref, inverse_ref, normal_ref):
    noise, _ = sample_latents(noise_ref, first_ref, second_ref)
    product = jnp.dot(noise, gram_ref[0], preferred_element_type=jnp.float32)
    noise = noise.astype(jnp.float32)
    by_gram = columns(product, 0) + columns(product, 1) + columns(product, 2)
    inverse = inverse_deviation(noise, by_gram, pair_ones())
    inverse_ref[...] = inverse
    normal_ref[...] = (noise * inverse).astype(jnp.bfloat16)


def noise_statistics(noise, first, second, gram):
    shape = (2 * noise.shape[0], noise.shape[1])
    return pl.pallas_call(
        noise_kernel,
        out_shape=[
            jax.ShapeDtypeStruct(shape, jnp.float32),
            jax.ShapeDtypeStruct(shape, jnp.bfloat16),
        ],
        in_specs=whole_specs(4),
        out_specs=whole_specs(2),
        compiler_params=vmem_params(),
        name="noise_statistics",
    )(noise, first, second, gram)


def maps_kernel(kept_ref, got_ref, rows_ref, through_ref, direct_ref, maps_ref, mod_ref):
    rows = rows_ref.shape[2]
    packs = rows // PACK
    f = lax.axis_index("fsdp")
    kept, got = kept_ref[...], got_ref[...]
    shift = jnp.where(f == 0, kept, got)
    scale = jnp.where(f == 0, got, kept)
    for m in range(3):
        pieces = []
        for j in range(packs):
            line = slice(m * packs + j, m * packs + j + 1)
            pieces.append(
                jnp.concatenate(
                    [
                        rows_ref[m, :, j * PACK : (j + 1) * PACK] * (1.0 + scale[line]),
                        shift[line],
                        jnp.zeros((7, PACK), jnp.float32),
                    ],
                    0,
                )
            )
        left = jnp.concatenate(pieces, 1).astype(jnp.bfloat16)
        through = jnp.concatenate([jnp.zeros((CH, rows), jnp.bfloat16), through_ref[m]], 0)
        product = lax.dot_general(
            left, through, CONTRACT_LAST, preferred_element_type=jnp.float32
        )
        base = m * (CH + 8)
        maps_ref[base : base + CH] = product[:CH] + direct_ref[m]
        maps_ref[base + CH : base + CH + 8] = product[CH:]
    rest = jnp.zeros((mod_ref.shape[0] - 2 * packs, PACK), jnp.float32)
    mod_ref[...] = jnp.concatenate([shift[:packs], scale[:packs], rest], 0).astype(jnp.bfloat16)


def modulated_maps(kept, got, rows_part, through, direct):
    packs = rows_part.shape[2] // PACK
    return pl.pallas_call(
        maps_kernel,
        out_shape=[
            jax.ShapeDtypeStruct((3 * (CH + 8), 2 * CH), jnp.float32),
            jax.ShapeDtypeStruct((-(-2 * packs // 16) * 16, PACK), jnp.bfloat16),
        ],
        in_specs=whole_specs(5),
        out_specs=whole_specs(2),
        compiler_params=vmem_params(),
        name="modulated_maps",
    )(kept, got, rows_part, through, direct)


MAP_ROWS = CH + 16


def token_kernel(
    level_ref,
    noise_ref,
    first_ref,
    second_ref,
    renoise_ref,
    inverse_ref,
    normal_ref,
    gram_ref,
    maps_a,
    maps_b,
    maps_c,
    maps_d,
    mod_ref,
    score_ref,
    payload_ref,
):
    half = renoise_ref.shape[0]
    level = level_ref[0]
    maps = [part[...].astype(jnp.float32) for part in (maps_a, maps_b, maps_c, maps_d)]
    maps = (maps[0] + maps[1]) + (maps[2] + maps[3])
    width = 2 * CH
    ones = pair_ones()

    def model_matrix(m):
        base = m * (CH + 8)
        pair = maps[base : base + CH]
        turned = pltpu.roll(pair, CH, 1)
        direct = split_two(block_diagonal(pair, turned))
        modulated = split_two(block_diagonal(turned, pair))
        offset = maps[base + CH : base + CH + 1]
        return jnp.concatenate(direct + modulated, 1), offset + pltpu.roll(offset, CH, 1)

    def combine(product, inverse, offset):
        direct = columns(product, 0) + columns(product, 1)
        return direct + inverse * (columns(product, 2) + columns(product, 3)) + offset

    noise, other_renoise = sample_latents(noise_ref, first_ref, second_ref)
    renoise = jnp.concatenate([renoise_ref[...], other_renoise.astype(jnp.float32)], 0)
    matrix, offset = model_matrix(0)
    product = jnp.dot(noise, matrix, preferred_element_type=jnp.float32)
    clean = combine(product, inverse_ref[...], offset)
    noisy = ((1.0 - level) * clean + level * renoise).astype(jnp.bfloat16)
    noisy_wide = noisy.astype(jnp.float32)

    def velocity(m):
        matrix, offset = model_matrix(m)
        matrix = jnp.concatenate([matrix, gram_ref[m]], 1)
        product = jnp.dot(noisy, matrix, preferred_element_type=jnp.float32)
        by_gram = columns(product, 4) + columns(product, 5) + columns(product, 6)
        return combine(product, inverse_deviation(noisy_wide, by_gram, ones), offset)

    real_v = velocity(1)
    fake_v = velocity(2)
    total = jnp.sum(jnp.abs(clean - renoise + real_v))
    gap_scale = level * total * (1.0 / (2 * half * width)) + EPS_GAP
    score = level * (real_v - fake_v) / gap_scale
    score_ref[...] = score[:half]
    tokens = 4 * half * lax.axis_size("dp")
    cotangent = (score * (1.0 / math.sqrt(tokens))).astype(jnp.bfloat16)
    pairs = lax.dot_general(
        normal_ref[...], cotangent, CONTRACT_FIRST, preferred_element_type=jnp.float32
    )
    outer = pairs[:CH] + pltpu.roll(pairs[CH:], CH, 1)
    sums = jnp.sum(cotangent.astype(jnp.float32), axis=0, keepdims=True)
    sums = sums + pltpu.roll(sums, CH, 1)
    rest = jnp.zeros((MAP_ROWS - CH - 1, width), jnp.float32)
    payload_ref[:MAP_ROWS] = jnp.concatenate([outer, sums, rest], 0).astype(jnp.bfloat16)
    payload_ref[MAP_ROWS:] = mod_ref[...]


def token_phase(level, noise, first, second, renoise, inverse, normal, gram, maps, mod):
    return pl.pallas_call(
        token_kernel,
        out_shape=[
            jax.ShapeDtypeStruct(renoise.shape, jnp.float32),
            jax.ShapeDtypeStruct((MAP_ROWS + mod.shape[0], 2 * CH), jnp.bfloat16),
        ],
        in_specs=[pl.BlockSpec(memory_space=pltpu.SMEM)] + whole_specs(12),
        out_specs=whole_specs(2),
        compiler_params=vmem_params(),
        name="tokens",
    )(level, noise, first, second, renoise, inverse, normal, gram, *maps, mod)


GRAD_PIECES = 6


def grad_kernel(
    block_a,
    block_b,
    block_c,
    block_d,
    rows_ref,
    unembed_ref,
    score_ref,
    grad_hbm,
    score_hbm,
    buffer,
    sems,
):
    score_copy = pltpu.make_async_copy(score_ref, score_hbm, sems.at[GRAD_PIECES])
    score_copy.start()
    rows = rows_ref.shape[2]
    packs = rows // PACK
    depth = rows // GRAD_PIECES
    blocks = [block[...] for block in (block_a, block_b, block_c, block_d)]
    left = jnp.concatenate([block[:MAP_ROWS, :CH] for block in blocks], 0)
    mods = [block[MAP_ROWS:].astype(jnp.float32) for block in blocks]
    unembed = unembed_ref[0]

    def piece(k):
        part = pl.ds(k * depth, depth)
        return pltpu.make_async_copy(buffer.at[part], grad_hbm.at[part], sems.at[k])

    tiles = []
    for j in range(packs):
        embed_tile = rows_ref[0, :, j * PACK : (j + 1) * PACK]
        column = []
        for mod in mods:
            column += [
                embed_tile * (1.0 + mod[packs + j : packs + j + 1]),
                mod[j : j + 1],
                jnp.zeros((MAP_ROWS - CH - 1, PACK), jnp.float32),
            ]
        tiles.append(jnp.concatenate(column, 0).astype(jnp.bfloat16))
    grad_map = lax.dot_general(
        left, jnp.concatenate(tiles, 1), CONTRACT_FIRST, preferred_element_type=jnp.float32
    ).astype(jnp.bfloat16)
    for k in range(GRAD_PIECES):
        part = slice(k * depth, (k + 1) * depth)
        buffer[part] = lax.dot_general(
            grad_map[:, part], unembed, CONTRACT_FIRST, preferred_element_type=jnp.float32
        )
        piece(k).start()
    for k in range(GRAD_PIECES):
        piece(k).wait()
    score_copy.wait()


def gradient(blocks, rows_part, unembed, score):
    rows = rows_part.shape[2]
    cols = unembed.shape[2]
    return pl.pallas_call(
        grad_kernel,
        out_shape=[
            jax.ShapeDtypeStruct((rows, cols), jnp.float32),
            jax.ShapeDtypeStruct(score.shape, jnp.float32),
        ],
        in_specs=whole_specs(7),
        out_specs=[pl.BlockSpec(memory_space=pl.ANY)] * 2,
        scratch_shapes=[
            pltpu.VMEM((rows, cols), jnp.float32),
            pltpu.SemaphoreType.DMA((GRAD_PIECES + 1,)),
        ],
        compiler_params=vmem_params(),
        name="gradient",
    )(*blocks, rows_part, unembed, score)


def body(
    gen_noise, renoise, gen_step, renoise_step, text_pooled, embed, mod_weight, proj_weight, unembed
):
    mine, latents, through = streamed_weights(
        gen_step,
        renoise_step,
        text_pooled,
        gen_noise[0],
        renoise[0],
        mod_weight,
        proj_weight,
        unembed,
    )
    f = lax.axis_index("fsdp")
    theirs = swap(mine, "mp", 1)
    own_half = lax.axis_index("mp") % 2 == f
    kept = jnp.where(own_half, mine, theirs)
    got = swap(jnp.where(own_half, theirs, mine), "fsdp", 1)
    first = swap(latents, "fsdp", 1)
    got, first = lax.optimization_barrier((got, first))
    second = swap(first, "mp", 1)
    gram, rows_part, direct = embed_products(embed, unembed, proj_weight.shape[1])
    maps, mod = modulated_maps(kept, got, rows_part, through, direct)
    maps = (maps + swap(maps, "mp", 1)).astype(jnp.bfloat16)
    inverse, normal = noise_statistics(gen_noise[0], first, second, gram)
    maps = chip_blocks(maps)
    level = renoise_step.astype(jnp.float32) / 1000.0
    score, payload = token_phase(
        level, gen_noise[0], first, second, renoise[0], inverse, normal, gram, maps, mod
    )
    blocks = gather_samples(payload)
    gen_grad, score_gap = gradient(blocks, rows_part, unembed, score)
    return (gen_grad, score_gap[None])


def fits_kernels(mesh):
    return mesh.shape["mp"] == 4 and mesh.shape["fsdp"] == 2 and mesh.shape["dp"] == 4


def solution(mesh):
    return jax.shard_map(
        body if fits_kernels(mesh) else plain_body,
        mesh=mesh,
        in_specs=(
            P("dp", "fsdp", None),
            P("dp", "fsdp", None),
            P("dp"),
            P("dp"),
            P("dp", None),
            P(),
            P(None, None, "fsdp"),
            P(None, "fsdp", "mp"),
            P(None, None, "mp"),
        ),
        out_specs=(P("fsdp", "mp"), P("dp", "fsdp", None)),
        check_vma=False,
    )
```

```python
import math

import jax
import jax.numpy as jnp
from jax import lax
from jax.experimental import pallas as pl
from jax.experimental.pallas import tpu as pltpu
from jax.sharding import PartitionSpec as P

D = 3072
CH = 64
TEMB = 256

GUIDANCE = 3.5
EPS_NORM = 1e-06
EPS_GAP = 1e-05
HI = lax.Precision.HIGHEST


def sinusoid(timesteps):
    half_size = TEMB // 2
    frequency = jnp.exp(-math.log(10000.0) * jnp.arange(half_size, dtype=jnp.float32) / half_size)
    angles = timesteps.astype(jnp.float32)[:, None] * frequency[None, :]
    return jnp.concatenate([jnp.cos(angles), jnp.sin(angles)], axis=1)


def condition(timesteps, pooled):
    joined = jnp.concatenate([sinusoid(timesteps), pooled.astype(jnp.float32)], axis=1)
    return jax.nn.silu(joined).astype(jnp.bfloat16)


def swap(x, axes, mask):
    count = lax.axis_size(axes)
    return lax.ppermute(x, axes, [(i, i ^ mask) for i in range(count)])


def plane_sum(x):
    if lax.axis_size("mp") != 4 or lax.axis_size("fsdp") != 2:
        return lax.psum(x, ("mp", "fsdp"))
    x = x + swap(x, "mp", 1)
    plane = ("mp", "fsdp")
    parts = [swap(x, plane, mask) for mask in (4, 1, 5)]
    return (x + parts[0]) + (parts[1] + parts[2])


def chip_blocks(x):
    pairs = []
    for m in range(4):
        for f in range(2):
            pairs.append((m * 2 + f, (m * 2 + f) ^ (4 if m % 2 == 0 else 1)))
    side = lax.ppermute(x, ("mp", "fsdp"), pairs)
    across = swap(x, ("mp", "fsdp"), 5)
    return [x, side, swap(side, "mp", 1), across]


def gather_samples(x):
    count = lax.axis_size("dp")
    if lax.axis_size("mp") != 4 or count != 4:
        blocks = lax.all_gather(x, "dp")
        return [blocks[i] for i in range(count)]
    pairs = []
    for m in range(4):
        for s in range(4):
            pairs.append((m * 4 + s, m * 4 + (s ^ (1 if m % 2 == 0 else 2))))
    near = lax.ppermute(x, ("mp", "dp"), pairs)
    far = swap(x, "dp", 3)
    return [x, near, swap(near, "mp", 1), far]


def exchange_modulation(local_mod, rows):
    if lax.axis_size("fsdp") == 2:
        f = lax.axis_index("fsdp")
        mine = lax.dynamic_slice_in_dim(local_mod, f * rows, rows, 1)
        theirs = swap(lax.dynamic_slice_in_dim(local_mod, (1 - f) * rows, rows, 1), "fsdp", 1)
        return jnp.where(f == 0, mine, theirs), jnp.where(f == 0, theirs, mine)
    whole = lax.all_gather(local_mod, "fsdp", axis=1, tiled=True)
    start = lax.axis_index("fsdp") * rows
    return (
        lax.dynamic_slice_in_dim(whole[:, :D], start, rows, 1),
        lax.dynamic_slice_in_dim(whole[:, D:], start, rows, 1),
    )


def dot(a, b, precision=HI):
    return jnp.dot(a, b, precision=precision, preferred_element_type=jnp.float32)


def both(x):
    zero = jnp.zeros_like(x)
    return jnp.concatenate(
        [jnp.concatenate([x, zero], 1), jnp.concatenate([zero, x], 1)], 0
    )


def plain_body(
    gen_noise, renoise, gen_step, renoise_step, text_pooled, embed, mod_weight, proj_weight, unembed
):
    rows, cols = proj_weight.shape[1], proj_weight.shape[2]
    f = lax.axis_index("fsdp")
    noise_all = lax.all_gather(gen_noise[0], "fsdp", axis=0, tiled=True)
    renoise_all = lax.all_gather(renoise[0], "fsdp", axis=0, tiled=True)

    blank_text = jnp.zeros_like(text_pooled)
    gen_vec = condition(gen_step, text_pooled)
    real_vec = jnp.concatenate(
        [condition(renoise_step, text_pooled), condition(renoise_step, blank_text)], 0
    )
    teacher_mod = jnp.dot(real_vec, mod_weight[1], preferred_element_type=jnp.float32)
    local_mod = jnp.concatenate(
        [
            jnp.dot(gen_vec, mod_weight[0], preferred_element_type=jnp.float32),
            GUIDANCE * teacher_mod[0:1] + (1.0 - GUIDANCE) * teacher_mod[1:2],
            jnp.dot(real_vec[0:1], mod_weight[2], preferred_element_type=jnp.float32),
        ],
        axis=0,
    )
    shift, scale = exchange_modulation(local_mod, rows)

    centred = embed.astype(jnp.float32)
    centred = centred - jnp.mean(centred, axis=2, keepdims=True)
    gram = [dot(centred[m], centred[m].T) / D for m in range(3)]
    centred_rows = lax.dynamic_slice_in_dim(centred, f * rows, rows, 2)
    embed_cols = lax.dynamic_slice_in_dim(embed, lax.axis_index("mp") * cols, cols, 2)

    pieces = []
    for m in range(3):
        through = lax.dot_general(
            proj_weight[m], unembed[m], (((1,), (1,)), ((), ())), preferred_element_type=jnp.float32
        )
        direct = lax.dot_general(
            embed_cols[m], unembed[m], (((1,), (1,)), ((), ())), preferred_element_type=jnp.float32
        )
        direct = jnp.where(f == 0, direct, 0.0)
        modulated = dot(centred_rows[m] * (1.0 + scale[m : m + 1]), through)
        offset = dot(shift[m : m + 1], through)
        offset = jnp.concatenate([offset, jnp.zeros((7, CH), jnp.float32)], 0)
        pieces.append(
            jnp.concatenate(
                [
                    jnp.concatenate([direct, modulated], 1),
                    jnp.concatenate([offset, jnp.zeros_like(offset)], 1),
                ],
                0,
            )
        )
    maps = plane_sum(jnp.concatenate(pieces, 0)).reshape(3, CH + 8, 2 * CH)
    direct = [both(maps[m, :CH, :CH]) for m in range(3)]
    modulated = [both(maps[m, :CH, CH:]) for m in range(3)]
    offset = [jnp.concatenate([maps[m, CH : CH + 1, :CH]] * 2, 1) for m in range(3)]

    ones = both(jnp.ones((CH, CH), jnp.float32))

    def normalized(u, m):
        spread = dot(dot(u, both(gram[m])) * u, ones)
        return u * lax.rsqrt(jnp.maximum(spread, 0.0) + EPS_NORM)

    def model(u, u_norm, m):
        return dot(u, direct[m]) + dot(u_norm, modulated[m]) + offset[m]

    noise = noise_all.astype(jnp.bfloat16).astype(jnp.float32)
    noise_norm = normalized(noise, 0)
    clean = model(noise, noise_norm, 0)
    level = renoise_step[0].astype(jnp.float32) / 1000.0
    noisy = (1.0 - level) * clean + level * renoise_all
    noisy = noisy.astype(jnp.bfloat16).astype(jnp.float32)
    real_v = model(noisy, normalized(noisy, 1), 1)
    fake_v = model(noisy, normalized(noisy, 2), 2)
    total = jnp.sum(jnp.abs(clean - renoise_all + real_v))
    gap_scale = level * total / (noise_all.shape[0] * 2 * CH) + EPS_GAP
    score = level * (real_v - fake_v) / gap_scale
    local_rows = gen_noise.shape[1]
    score_gap = lax.dynamic_slice_in_dim(score, f * local_rows, local_rows, 0)

    all_tokens = noise_all.shape[0] * 2 * lax.axis_size("dp")
    cotangent = (score / math.sqrt(all_tokens)).astype(jnp.bfloat16).astype(jnp.float32)
    pairs = dot(noise_norm.T, cotangent)
    outer = pairs[:CH, :CH] + pairs[CH:, CH:]
    sums = jnp.sum(cotangent, axis=0)
    sums = sums[:CH] + sums[CH:]
    payload = jnp.concatenate(
        [
            jnp.pad(outer, ((0, 0), (0, CH))),
            jnp.pad(sums[None], ((0, 7), (0, CH))),
            jnp.concatenate([shift[0], scale[0]]).reshape(-1, 2 * CH),
        ],
        0,
    )
    blocks = gather_samples(payload)
    grad_map = jnp.zeros((CH, rows), jnp.float32)
    for block in blocks:
        block_mod = block[CH + 8 :].reshape(2, rows)
        grad_map += dot(block[:CH, :CH].T, centred_rows[0]) * (1.0 + block_mod[1:2])
        grad_map += block[CH, :CH][:, None] * block_mod[0:1]
    gen_grad = lax.dot_general(
        grad_map.astype(jnp.bfloat16),
        unembed[0],
        (((0,), (0,)), ((), ())),
        preferred_element_type=jnp.float32,
    )
    return (gen_grad, score_gap[None])


def vmem_params():
    return pltpu.CompilerParams(vmem_limit_bytes=48 * 1024 * 1024)


def whole_specs(count):
    return [pl.BlockSpec(memory_space=pltpu.VMEM)] * count


def split_two(x):
    high = x.astype(jnp.bfloat16)
    return high, (x - high.astype(jnp.float32)).astype(jnp.bfloat16)


def split_three(x):
    high = x.astype(jnp.bfloat16)
    rest = x - high.astype(jnp.float32)
    middle = rest.astype(jnp.bfloat16)
    return high, middle, (rest - middle.astype(jnp.float32)).astype(jnp.bfloat16)


def lane_index(shape):
    return lax.broadcasted_iota(jnp.int32, shape, len(shape) - 1)


def block_diagonal(left_copy, right_copy):
    lanes = lane_index(left_copy.shape)
    top = jnp.where(lanes < CH, left_copy, 0.0)
    bottom = jnp.where(lanes >= CH, right_copy, 0.0)
    return jnp.concatenate([top, bottom], 0)


MOD_PIECES = 4
PROJ_PIECES = 3
IN_FLIGHT = 12
LATENTS_AFTER = 8
PACK = 128
CONTRACT_LAST = (((1,), (1,)), ((), ()))
CONTRACT_FIRST = (((0,), (0,)), ((), ()))


def stream_kernel(
    gen_step_ref,
    renoise_step_ref,
    text_hbm,
    noise_hbm,
    renoise_hbm,
    mod_hbm,
    proj_hbm,
    unembed_hbm,
    mod_ref,
    latents_ref,
    through_ref,
    text_ref,
    noise_ref,
    renoise_ref,
    unembed_ref,
    mod_buffer,
    proj_buffer,
    mod_sems,
    proj_sems,
    small_sems,
):
    width = mod_buffer.shape[2]
    rows, cols = proj_buffer.shape[1:]
    mod_depth = mod_buffer.shape[1] // MOD_PIECES
    proj_depth = rows // PROJ_PIECES
    mod_start = pl.multiple_of((lax.axis_index("mp") % 2) * width, 128)

    def mod_piece(m, k):
        part = pl.ds(k * mod_depth, mod_depth)
        return pltpu.make_async_copy(
            mod_hbm.at[m, part, pl.ds(mod_start, width)], mod_buffer.at[m, part], mod_sems.at[m, k]
        )

    def proj_piece(m, k):
        part = pl.ds(k * proj_depth, proj_depth)
        return pltpu.make_async_copy(
            proj_hbm.at[m, part], proj_buffer.at[m, part], proj_sems.at[m, k]
        )

    small = [
        pltpu.make_async_copy(source, target, small_sems.at[k])
        for k, (source, target) in enumerate(
            (
                (text_hbm, text_ref),
                (unembed_hbm, unembed_ref),
                (noise_hbm, noise_ref),
                (renoise_hbm, renoise_ref),
            )
        )
    ]
    order = []
    for m in range(3):
        order += [proj_piece(m, k) for k in range(PROJ_PIECES)]
        order += [mod_piece(m, k) for k in range(MOD_PIECES)]
    order = small[:2] + order[:LATENTS_AFTER] + small[2:] + order[LATENTS_AFTER:]
    for copy in order[:IN_FLIGHT]:
        copy.start()

    def take(position):
        order[position].wait()
        if position + IN_FLIGHT < len(order):
            order[position + IN_FLIGHT].start()

    take(0)
    half_size = TEMB // 2
    place = lane_index((8, half_size)).astype(jnp.float32)
    frequency = jnp.exp(place * (-math.log(10000.0) / half_size))
    level = lax.broadcasted_iota(jnp.int32, (8, half_size), 0)
    steps = jnp.where(level == 0, gen_step_ref[0], renoise_step_ref[0]).astype(jnp.float32)
    angles = steps * frequency
    text = jnp.broadcast_to(text_ref[...].astype(jnp.float32), (8, text_ref.shape[1]))
    text = jnp.where(lax.broadcasted_iota(jnp.int32, text.shape, 0) < 2, text, 0.0)
    joined = jnp.concatenate([jnp.cos(angles), jnp.sin(angles), text], 1)
    vectors = (joined / (1.0 + jnp.exp(-joined))).astype(jnp.bfloat16)
    packs = width // PACK
    mod_ref[...] = jnp.zeros_like(mod_ref)
    take(1)
    place = 2
    for m in range(3):
        total = jnp.zeros((8, width), jnp.float32)
        for k in range(PROJ_PIECES + MOD_PIECES):
            if place == LATENTS_AFTER + 2:
                take(place)
                take(place + 1)
                latents = jnp.where(lax.axis_index("mp") % 2 == 0, noise_ref[...], renoise_ref[...])
                latents_ref[...] = latents.astype(jnp.bfloat16)
                place += 2
            take(place)
            place += 1
            if k < PROJ_PIECES:
                part = slice(k * proj_depth, (k + 1) * proj_depth)
                through_ref[m, :, part] = lax.dot_general(
                    unembed_ref[m],
                    proj_buffer[m, part],
                    CONTRACT_LAST,
                    preferred_element_type=jnp.float32,
                ).astype(jnp.bfloat16)
            else:
                part = slice((k - PROJ_PIECES) * mod_depth, (k - PROJ_PIECES + 1) * mod_depth)
                total += jnp.dot(
                    vectors[:, part], mod_buffer[m, part], preferred_element_type=jnp.float32
                )
        if m == 0:
            line = total[0:1]
        elif m == 1:
            line = GUIDANCE * total[1:2] + (1.0 - GUIDANCE) * total[2:3]
        else:
            line = total[1:2]
        for j in range(packs):
            mod_ref[m * packs + j : m * packs + j + 1] = line[:, j * PACK : (j + 1) * PACK]


def streamed_weights(
    gen_step, renoise_step, text, noise, renoise, mod_weight, proj_weight, unembed
):
    depth, width = mod_weight.shape[1], mod_weight.shape[2] // 2
    rows, cols = proj_weight.shape[1:]
    pack_rows = -(-3 * width // PACK // 8) * 8
    return pl.pallas_call(
        stream_kernel,
        out_shape=[
            jax.ShapeDtypeStruct((pack_rows, PACK), jnp.float32),
            jax.ShapeDtypeStruct(noise.shape, jnp.bfloat16),
            jax.ShapeDtypeStruct((3, CH, rows), jnp.bfloat16),
        ],
        in_specs=[pl.BlockSpec(memory_space=pltpu.SMEM)] * 2
        + [pl.BlockSpec(memory_space=pltpu.HBM)] * 6,
        out_specs=whole_specs(3),
        scratch_shapes=[
            pltpu.VMEM(text.shape, text.dtype),
            pltpu.VMEM(noise.shape, noise.dtype),
            pltpu.VMEM(renoise.shape, renoise.dtype),
            pltpu.VMEM(unembed.shape, unembed.dtype),
            pltpu.VMEM((3, depth, width), jnp.bfloat16),
            pltpu.VMEM((3, rows, cols), jnp.bfloat16),
            pltpu.SemaphoreType.DMA((3, MOD_PIECES)),
            pltpu.SemaphoreType.DMA((3, PROJ_PIECES)),
            pltpu.SemaphoreType.DMA((4,)),
        ],
        compiler_params=vmem_params(),
        name="stream_weights",
    )(
        gen_step,
        renoise_step,
        *(
            pltpu.with_memory_space_constraint(x, pltpu.HBM)
            for x in (text, noise, renoise, mod_weight, proj_weight, unembed)
        ),
    )


def embed_kernel(embed_ref, unembed_ref, gram_ref, rows_ref, direct_ref):
    rows, cols = rows_ref.shape[2], unembed_ref.shape[2]
    f = lax.axis_index("fsdp")
    row_start = pl.multiple_of(f * rows, 128)
    col_start = pl.multiple_of(lax.axis_index("mp") * cols, 128)
    nothing = jnp.zeros((CH, cols), jnp.bfloat16)
    for m in range(3):
        whole = embed_ref[m].astype(jnp.float32)
        average = jnp.sum(whole, axis=1, keepdims=True) * (1.0 / D)
        rows_ref[m] = embed_ref[m, :, pl.ds(row_start, rows)].astype(jnp.float32) - average
        direct = lax.dot_general(
            embed_ref[m, :, pl.ds(col_start, cols)],
            jnp.concatenate([unembed_ref[m], nothing], 0),
            CONTRACT_LAST,
            preferred_element_type=jnp.float32,
        )
        direct_ref[m] = jnp.where(f == 0, direct, 0.0)
        pair = jnp.concatenate(split_two(whole - average), 0)
        product = lax.dot_general(pair, pair, CONTRACT_LAST, preferred_element_type=jnp.float32)
        product = product[:CH] + product[CH:]
        gram = (product + pltpu.roll(product, CH, 1)) * (1.0 / D)
        gram_ref[m] = jnp.concatenate(split_three(block_diagonal(gram, gram)), 1)


def embed_products(embed, unembed, rows):
    return pl.pallas_call(
        embed_kernel,
        out_shape=[
            jax.ShapeDtypeStruct((3, 2 * CH, 6 * CH), jnp.bfloat16),
            jax.ShapeDtypeStruct((3, CH, rows), jnp.float32),
            jax.ShapeDtypeStruct((3, CH, 2 * CH), jnp.float32),
        ],
        in_specs=whole_specs(2),
        out_specs=whole_specs(3),
        compiler_params=vmem_params(),
        cost_estimate=pl.CostEstimate(
            flops=6 * 128 * 128 * D, bytes_accessed=6 * CH * D, transcendentals=0
        ),
        name="embed_products",
    )(embed, unembed)


def pair_ones():
    shape = (2 * CH, 2 * CH)
    lanes = lane_index(shape)
    subs = lax.broadcasted_iota(jnp.int32, shape, 0)
    ones = jnp.where((lanes < CH) == (subs < CH), 1.0, 0.0).astype(jnp.bfloat16)
    return jnp.concatenate([ones, ones], 0)


def inverse_deviation(u, by_gram, ones):
    squares = jnp.concatenate(split_two(by_gram * u), 1)
    spread = jnp.dot(squares, ones, preferred_element_type=jnp.float32)
    return lax.rsqrt(jnp.maximum(spread, 0.0) + EPS_NORM)


def columns(product, i):
    return product[:, i * 2 * CH : (i + 1) * 2 * CH]


def sample_latents(noise_ref, first_ref, second_ref):
    first, second = first_ref[...], second_ref[...]
    core = lax.axis_index("mp") % 2
    other = jnp.where(core == 0, first, second)
    other_renoise = jnp.where(core == 0, second, first)
    return jnp.concatenate([noise_ref[...].astype(jnp.bfloat16), other], 0), other_renoise


def noise_kernel(noise_ref, first_ref, second_ref, gram_ref, inverse_ref, normal_ref):
    noise, _ = sample_latents(noise_ref, first_ref, second_ref)
    product = jnp.dot(noise, gram_ref[0], preferred_element_type=jnp.float32)
    noise = noise.astype(jnp.float32)
    by_gram = columns(product, 0) + columns(product, 1) + columns(product, 2)
    inverse = inverse_deviation(noise, by_gram, pair_ones())
    inverse_ref[...] = inverse
    normal_ref[...] = (noise * inverse).astype(jnp.bfloat16)


def noise_statistics(noise, first, second, gram):
    shape = (2 * noise.shape[0], noise.shape[1])
    return pl.pallas_call(
        noise_kernel,
        out_shape=[
            jax.ShapeDtypeStruct(shape, jnp.float32),
            jax.ShapeDtypeStruct(shape, jnp.bfloat16),
        ],
        in_specs=whole_specs(4),
        out_specs=whole_specs(2),
        compiler_params=vmem_params(),
        name="noise_statistics",
    )(noise, first, second, gram)


def maps_kernel(kept_ref, got_ref, rows_ref, through_ref, direct_ref, maps_ref, mod_ref):
    rows = rows_ref.shape[2]
    packs = rows // PACK
    f = lax.axis_index("fsdp")
    kept, got = kept_ref[...], got_ref[...]
    shift = jnp.where(f == 0, kept, got)
    scale = jnp.where(f == 0, got, kept)
    offsets = []
    for m in range(3):
        pieces = []
        for j in range(packs):
            line = slice(m * packs + j, m * packs + j + 1)
            pieces.append(
                jnp.concatenate(
                    [
                        rows_ref[m, :, j * PACK : (j + 1) * PACK] * (1.0 + scale[line]),
                        shift[line],
                        jnp.zeros((7, PACK), jnp.float32),
                    ],
                    0,
                )
            )
        left = jnp.concatenate(pieces, 1).astype(jnp.bfloat16)
        through = jnp.concatenate([jnp.zeros((CH, rows), jnp.bfloat16), through_ref[m]], 0)
        product = lax.dot_general(
            left, through, CONTRACT_LAST, preferred_element_type=jnp.float32
        )
        maps_ref[m * CH : (m + 1) * CH] = product[:CH] + direct_ref[m]
        offsets.append(product[CH : CH + 1])
    maps_ref[3 * CH :] = jnp.concatenate(offsets + [jnp.zeros((5, PACK), jnp.float32)], 0)
    rest = jnp.zeros((mod_ref.shape[0] - 2 * packs, PACK), jnp.float32)
    mod_ref[...] = jnp.concatenate([shift[:packs], scale[:packs], rest], 0).astype(jnp.bfloat16)


def modulated_maps(kept, got, rows_part, through, direct):
    packs = rows_part.shape[2] // PACK
    return pl.pallas_call(
        maps_kernel,
        out_shape=[
            jax.ShapeDtypeStruct((3 * CH + 8, 2 * CH), jnp.float32),
            jax.ShapeDtypeStruct((-(-2 * packs // 16) * 16, PACK), jnp.bfloat16),
        ],
        in_specs=whole_specs(5),
        out_specs=whole_specs(2),
        compiler_params=vmem_params(),
        name="modulated_maps",
    )(kept, got, rows_part, through, direct)


MAP_ROWS = CH + 16


def token_kernel(
    level_ref,
    noise_ref,
    first_ref,
    second_ref,
    renoise_ref,
    inverse_ref,
    normal_ref,
    gram_ref,
    maps_a,
    maps_b,
    maps_c,
    maps_d,
    mod_ref,
    score_ref,
    payload_ref,
):
    half = renoise_ref.shape[0]
    level = level_ref[0]
    maps = [part[...].astype(jnp.float32) for part in (maps_a, maps_b, maps_c, maps_d)]
    maps = (maps[0] + maps[1]) + (maps[2] + maps[3])
    width = 2 * CH
    ones = pair_ones()

    def model_matrix(m):
        base = m * CH
        pair = maps[base : base + CH]
        turned = pltpu.roll(pair, CH, 1)
        direct = block_diagonal(pair, turned)
        modulated = block_diagonal(turned, pair)
        matrix = jnp.concatenate([direct, modulated], 1).astype(jnp.bfloat16)
        offset = maps[3 * CH + m : 3 * CH + m + 1]
        return matrix, offset + pltpu.roll(offset, CH, 1)

    def combine(product, inverse, offset):
        return columns(product, 0) + inverse * columns(product, 1) + offset

    noise, other_renoise = sample_latents(noise_ref, first_ref, second_ref)
    renoise = jnp.concatenate([renoise_ref[...], other_renoise.astype(jnp.float32)], 0)
    matrix, offset = model_matrix(0)
    product = jnp.dot(noise, matrix, preferred_element_type=jnp.float32)
    clean = combine(product, inverse_ref[...], offset)
    noisy = ((1.0 - level) * clean + level * renoise).astype(jnp.bfloat16)
    noisy_wide = noisy.astype(jnp.float32)

    def velocity(m):
        matrix, offset = model_matrix(m)
        matrix = jnp.concatenate([matrix, gram_ref[m]], 1)
        product = jnp.dot(noisy, matrix, preferred_element_type=jnp.float32)
        by_gram = columns(product, 2) + columns(product, 3) + columns(product, 4)
        return combine(product, inverse_deviation(noisy_wide, by_gram, ones), offset)

    real_v = velocity(1)
    fake_v = velocity(2)
    total = jnp.sum(jnp.abs(clean - renoise + real_v))
    gap_scale = level * total * (1.0 / (2 * half * width)) + EPS_GAP
    score = level * (real_v - fake_v) / gap_scale
    score_ref[...] = score[:half]
    tokens = 4 * half * lax.axis_size("dp")
    cotangent = (score * (1.0 / math.sqrt(tokens))).astype(jnp.bfloat16)
    pairs = lax.dot_general(
        normal_ref[...], cotangent, CONTRACT_FIRST, preferred_element_type=jnp.float32
    )
    outer = pairs[:CH] + pltpu.roll(pairs[CH:], CH, 1)
    sums = jnp.sum(cotangent.astype(jnp.float32), axis=0, keepdims=True)
    sums = sums + pltpu.roll(sums, CH, 1)
    rest = jnp.zeros((MAP_ROWS - CH - 1, width), jnp.float32)
    payload_ref[:MAP_ROWS] = jnp.concatenate([outer, sums, rest], 0).astype(jnp.bfloat16)
    payload_ref[MAP_ROWS:] = mod_ref[...]


def token_phase(level, noise, first, second, renoise, inverse, normal, gram, maps, mod):
    return pl.pallas_call(
        token_kernel,
        out_shape=[
            jax.ShapeDtypeStruct(renoise.shape, jnp.float32),
            jax.ShapeDtypeStruct((MAP_ROWS + mod.shape[0], 2 * CH), jnp.bfloat16),
        ],
        in_specs=[pl.BlockSpec(memory_space=pltpu.SMEM)] + whole_specs(12),
        out_specs=whole_specs(2),
        compiler_params=vmem_params(),
        name="tokens",
    )(level, noise, first, second, renoise, inverse, normal, gram, *maps, mod)


GRAD_PIECES = 6


def grad_kernel(
    block_a,
    block_b,
    block_c,
    block_d,
    rows_ref,
    unembed_ref,
    score_ref,
    grad_hbm,
    score_hbm,
    buffer,
    sems,
):
    score_copy = pltpu.make_async_copy(score_ref, score_hbm, sems.at[GRAD_PIECES])
    score_copy.start()
    rows = rows_ref.shape[2]
    packs = rows // PACK
    depth = rows // GRAD_PIECES
    blocks = [block[...] for block in (block_a, block_b, block_c, block_d)]
    left = jnp.concatenate([block[:MAP_ROWS, :CH] for block in blocks], 0)
    mods = [block[MAP_ROWS:].astype(jnp.float32) for block in blocks]
    unembed = unembed_ref[0]

    def piece(k):
        part = pl.ds(k * depth, depth)
        return pltpu.make_async_copy(buffer.at[part], grad_hbm.at[part], sems.at[k])

    tiles = []
    for j in range(packs):
        embed_tile = rows_ref[0, :, j * PACK : (j + 1) * PACK]
        column = []
        for mod in mods:
            column += [
                embed_tile * (1.0 + mod[packs + j : packs + j + 1]),
                mod[j : j + 1],
                jnp.zeros((MAP_ROWS - CH - 1, PACK), jnp.float32),
            ]
        tiles.append(jnp.concatenate(column, 0).astype(jnp.bfloat16))
    grad_map = lax.dot_general(
        left, jnp.concatenate(tiles, 1), CONTRACT_FIRST, preferred_element_type=jnp.float32
    ).astype(jnp.bfloat16)
    for k in range(GRAD_PIECES):
        part = slice(k * depth, (k + 1) * depth)
        buffer[part] = lax.dot_general(
            grad_map[:, part], unembed, CONTRACT_FIRST, preferred_element_type=jnp.float32
        )
        piece(k).start()
    for k in range(GRAD_PIECES):
        piece(k).wait()
    score_copy.wait()


def gradient(blocks, rows_part, unembed, score):
    rows = rows_part.shape[2]
    cols = unembed.shape[2]
    return pl.pallas_call(
        grad_kernel,
        out_shape=[
            jax.ShapeDtypeStruct((rows, cols), jnp.float32),
            jax.ShapeDtypeStruct(score.shape, jnp.float32),
        ],
        in_specs=whole_specs(7),
        out_specs=[pl.BlockSpec(memory_space=pl.ANY)] * 2,
        scratch_shapes=[
            pltpu.VMEM((rows, cols), jnp.float32),
            pltpu.SemaphoreType.DMA((GRAD_PIECES + 1,)),
        ],
        compiler_params=vmem_params(),
        name="gradient",
    )(*blocks, rows_part, unembed, score)


def body(
    gen_noise, renoise, gen_step, renoise_step, text_pooled, embed, mod_weight, proj_weight, unembed
):
    mine, latents, through = streamed_weights(
        gen_step,
        renoise_step,
        text_pooled,
        gen_noise[0],
        renoise[0],
        mod_weight,
        proj_weight,
        unembed,
    )
    f = lax.axis_index("fsdp")
    theirs = swap(mine, "mp", 1)
    own_half = lax.axis_index("mp") % 2 == f
    kept = jnp.where(own_half, mine, theirs)
    got = swap(jnp.where(own_half, theirs, mine), "fsdp", 1)
    first = swap(latents, "fsdp", 1)
    got, first = lax.optimization_barrier((got, first))
    second = swap(first, "mp", 1)
    gram, rows_part, direct = embed_products(embed, unembed, proj_weight.shape[1])
    maps, mod = modulated_maps(kept, got, rows_part, through, direct)
    maps = (maps + swap(maps, "mp", 1)).astype(jnp.bfloat16)
    inverse, normal = noise_statistics(gen_noise[0], first, second, gram)
    maps = chip_blocks(maps)
    level = renoise_step.astype(jnp.float32) / 1000.0
    score, payload = token_phase(
        level, gen_noise[0], first, second, renoise[0], inverse, normal, gram, maps, mod
    )
    blocks = gather_samples(payload)
    gen_grad, score_gap = gradient(blocks, rows_part, unembed, score)
    return (gen_grad, score_gap[None])


def fits_kernels(mesh):
    return mesh.shape["mp"] == 4 and mesh.shape["fsdp"] == 2 and mesh.shape["dp"] == 4


def solution(mesh):
    return jax.shard_map(
        body if fits_kernels(mesh) else plain_body,
        mesh=mesh,
        in_specs=(
            P("dp", "fsdp", None),
            P("dp", "fsdp", None),
            P("dp"),
            P("dp"),
            P("dp", None),
            P(),
            P(None, None, "fsdp"),
            P(None, "fsdp", "mp"),
            P(None, None, "mp"),
        ),
        out_specs=(P("fsdp", "mp"), P("dp", "fsdp", None)),
        check_vma=False,
    )
```

```python
import math

import jax
import jax.numpy as jnp
from jax import lax
from jax.experimental import pallas as pl
from jax.experimental.pallas import tpu as pltpu
from jax.sharding import PartitionSpec as P

D = 3072
CH = 64
TEMB = 256

GUIDANCE = 3.5
EPS_NORM = 1e-06
EPS_GAP = 1e-05
HI = lax.Precision.HIGHEST


def sinusoid(timesteps):
    half_size = TEMB // 2
    frequency = jnp.exp(-math.log(10000.0) * jnp.arange(half_size, dtype=jnp.float32) / half_size)
    angles = timesteps.astype(jnp.float32)[:, None] * frequency[None, :]
    return jnp.concatenate([jnp.cos(angles), jnp.sin(angles)], axis=1)


def condition(timesteps, pooled):
    joined = jnp.concatenate([sinusoid(timesteps), pooled.astype(jnp.float32)], axis=1)
    return jax.nn.silu(joined).astype(jnp.bfloat16)


def swap(x, axes, mask):
    count = lax.axis_size(axes)
    return lax.ppermute(x, axes, [(i, i ^ mask) for i in range(count)])


def plane_sum(x):
    if lax.axis_size("mp") != 4 or lax.axis_size("fsdp") != 2:
        return lax.psum(x, ("mp", "fsdp"))
    x = x + swap(x, "mp", 1)
    plane = ("mp", "fsdp")
    parts = [swap(x, plane, mask) for mask in (4, 1, 5)]
    return (x + parts[0]) + (parts[1] + parts[2])


def chip_blocks(x):
    pairs = []
    for m in range(4):
        for f in range(2):
            pairs.append((m * 2 + f, (m * 2 + f) ^ (4 if m % 2 == 0 else 1)))
    side = lax.ppermute(x, ("mp", "fsdp"), pairs)
    across = swap(x, ("mp", "fsdp"), 5)
    return [x, side, swap(side, "mp", 1), across]


def gather_samples(x):
    count = lax.axis_size("dp")
    if lax.axis_size("mp") != 4 or count != 4:
        blocks = lax.all_gather(x, "dp")
        return [blocks[i] for i in range(count)]
    pairs = []
    for m in range(4):
        for s in range(4):
            pairs.append((m * 4 + s, m * 4 + (s ^ (1 if m % 2 == 0 else 2))))
    near = lax.ppermute(x, ("mp", "dp"), pairs)
    far = swap(x, "dp", 3)
    return [x, near, swap(near, "mp", 1), far]


def exchange_modulation(local_mod, rows):
    if lax.axis_size("fsdp") == 2:
        f = lax.axis_index("fsdp")
        mine = lax.dynamic_slice_in_dim(local_mod, f * rows, rows, 1)
        theirs = swap(lax.dynamic_slice_in_dim(local_mod, (1 - f) * rows, rows, 1), "fsdp", 1)
        return jnp.where(f == 0, mine, theirs), jnp.where(f == 0, theirs, mine)
    whole = lax.all_gather(local_mod, "fsdp", axis=1, tiled=True)
    start = lax.axis_index("fsdp") * rows
    return (
        lax.dynamic_slice_in_dim(whole[:, :D], start, rows, 1),
        lax.dynamic_slice_in_dim(whole[:, D:], start, rows, 1),
    )


def dot(a, b, precision=HI):
    return jnp.dot(a, b, precision=precision, preferred_element_type=jnp.float32)


def both(x):
    zero = jnp.zeros_like(x)
    return jnp.concatenate(
        [jnp.concatenate([x, zero], 1), jnp.concatenate([zero, x], 1)], 0
    )


def plain_body(
    gen_noise, renoise, gen_step, renoise_step, text_pooled, embed, mod_weight, proj_weight, unembed
):
    rows, cols = proj_weight.shape[1], proj_weight.shape[2]
    f = lax.axis_index("fsdp")
    noise_all = lax.all_gather(gen_noise[0], "fsdp", axis=0, tiled=True)
    renoise_all = lax.all_gather(renoise[0], "fsdp", axis=0, tiled=True)

    blank_text = jnp.zeros_like(text_pooled)
    gen_vec = condition(gen_step, text_pooled)
    real_vec = jnp.concatenate(
        [condition(renoise_step, text_pooled), condition(renoise_step, blank_text)], 0
    )
    teacher_mod = jnp.dot(real_vec, mod_weight[1], preferred_element_type=jnp.float32)
    local_mod = jnp.concatenate(
        [
            jnp.dot(gen_vec, mod_weight[0], preferred_element_type=jnp.float32),
            GUIDANCE * teacher_mod[0:1] + (1.0 - GUIDANCE) * teacher_mod[1:2],
            jnp.dot(real_vec[0:1], mod_weight[2], preferred_element_type=jnp.float32),
        ],
        axis=0,
    )
    shift, scale = exchange_modulation(local_mod, rows)

    centred = embed.astype(jnp.float32)
    centred = centred - jnp.mean(centred, axis=2, keepdims=True)
    gram = [dot(centred[m], centred[m].T) / D for m in range(3)]
    centred_rows = lax.dynamic_slice_in_dim(centred, f * rows, rows, 2)
    embed_cols = lax.dynamic_slice_in_dim(embed, lax.axis_index("mp") * cols, cols, 2)

    pieces = []
    for m in range(3):
        through = lax.dot_general(
            proj_weight[m], unembed[m], (((1,), (1,)), ((), ())), preferred_element_type=jnp.float32
        )
        direct = lax.dot_general(
            embed_cols[m], unembed[m], (((1,), (1,)), ((), ())), preferred_element_type=jnp.float32
        )
        direct = jnp.where(f == 0, direct, 0.0)
        modulated = dot(centred_rows[m] * (1.0 + scale[m : m + 1]), through)
        offset = dot(shift[m : m + 1], through)
        offset = jnp.concatenate([offset, jnp.zeros((7, CH), jnp.float32)], 0)
        pieces.append(
            jnp.concatenate(
                [
                    jnp.concatenate([direct, modulated], 1),
                    jnp.concatenate([offset, jnp.zeros_like(offset)], 1),
                ],
                0,
            )
        )
    maps = plane_sum(jnp.concatenate(pieces, 0)).reshape(3, CH + 8, 2 * CH)
    direct = [both(maps[m, :CH, :CH]) for m in range(3)]
    modulated = [both(maps[m, :CH, CH:]) for m in range(3)]
    offset = [jnp.concatenate([maps[m, CH : CH + 1, :CH]] * 2, 1) for m in range(3)]

    ones = both(jnp.ones((CH, CH), jnp.float32))

    def normalized(u, m):
        spread = dot(dot(u, both(gram[m])) * u, ones)
        return u * lax.rsqrt(jnp.maximum(spread, 0.0) + EPS_NORM)

    def model(u, u_norm, m):
        return dot(u, direct[m]) + dot(u_norm, modulated[m]) + offset[m]

    noise = noise_all.astype(jnp.bfloat16).astype(jnp.float32)
    noise_norm = normalized(noise, 0)
    clean = model(noise, noise_norm, 0)
    level = renoise_step[0].astype(jnp.float32) / 1000.0
    noisy = (1.0 - level) * clean + level * renoise_all
    noisy = noisy.astype(jnp.bfloat16).astype(jnp.float32)
    real_v = model(noisy, normalized(noisy, 1), 1)
    fake_v = model(noisy, normalized(noisy, 2), 2)
    total = jnp.sum(jnp.abs(clean - renoise_all + real_v))
    gap_scale = level * total / (noise_all.shape[0] * 2 * CH) + EPS_GAP
    score = level * (real_v - fake_v) / gap_scale
    local_rows = gen_noise.shape[1]
    score_gap = lax.dynamic_slice_in_dim(score, f * local_rows, local_rows, 0)

    all_tokens = noise_all.shape[0] * 2 * lax.axis_size("dp")
    cotangent = (score / math.sqrt(all_tokens)).astype(jnp.bfloat16).astype(jnp.float32)
    pairs = dot(noise_norm.T, cotangent)
    outer = pairs[:CH, :CH] + pairs[CH:, CH:]
    sums = jnp.sum(cotangent, axis=0)
    sums = sums[:CH] + sums[CH:]
    payload = jnp.concatenate(
        [
            jnp.pad(outer, ((0, 0), (0, CH))),
            jnp.pad(sums[None], ((0, 7), (0, CH))),
            jnp.concatenate([shift[0], scale[0]]).reshape(-1, 2 * CH),
        ],
        0,
    )
    blocks = gather_samples(payload)
    grad_map = jnp.zeros((CH, rows), jnp.float32)
    for block in blocks:
        block_mod = block[CH + 8 :].reshape(2, rows)
        grad_map += dot(block[:CH, :CH].T, centred_rows[0]) * (1.0 + block_mod[1:2])
        grad_map += block[CH, :CH][:, None] * block_mod[0:1]
    gen_grad = lax.dot_general(
        grad_map.astype(jnp.bfloat16),
        unembed[0],
        (((0,), (0,)), ((), ())),
        preferred_element_type=jnp.float32,
    )
    return (gen_grad, score_gap[None])


def vmem_params():
    return pltpu.CompilerParams(vmem_limit_bytes=48 * 1024 * 1024)


def whole_specs(count):
    return [pl.BlockSpec(memory_space=pltpu.VMEM)] * count


def split_two(x):
    high = x.astype(jnp.bfloat16)
    return high, (x - high.astype(jnp.float32)).astype(jnp.bfloat16)


def split_three(x):
    high = x.astype(jnp.bfloat16)
    rest = x - high.astype(jnp.float32)
    middle = rest.astype(jnp.bfloat16)
    return high, middle, (rest - middle.astype(jnp.float32)).astype(jnp.bfloat16)


def lane_index(shape):
    return lax.broadcasted_iota(jnp.int32, shape, len(shape) - 1)


def block_diagonal(left_copy, right_copy):
    lanes = lane_index(left_copy.shape)
    top = jnp.where(lanes < CH, left_copy, 0.0)
    bottom = jnp.where(lanes >= CH, right_copy, 0.0)
    return jnp.concatenate([top, bottom], 0)


MOD_PIECES = 4
PROJ_PIECES = 3
IN_FLIGHT = 12
LATENTS_AFTER = 8
PACK = 128
CONTRACT_LAST = (((1,), (1,)), ((), ()))
CONTRACT_FIRST = (((0,), (0,)), ((), ()))


def stream_kernel(
    gen_step_ref,
    renoise_step_ref,
    text_hbm,
    noise_hbm,
    renoise_hbm,
    mod_hbm,
    proj_hbm,
    unembed_hbm,
    embed_hbm,
    mod_ref,
    latents_ref,
    through_ref,
    noise_ref,
    renoise_ref,
    unembed_ref,
    embed_ref,
    text_ref,
    mod_buffer,
    proj_buffer,
    mod_sems,
    proj_sems,
    small_sems,
):
    width = mod_buffer.shape[2]
    rows, cols = proj_buffer.shape[1:]
    mod_depth = mod_buffer.shape[1] // MOD_PIECES
    proj_depth = rows // PROJ_PIECES
    mod_start = pl.multiple_of((lax.axis_index("mp") % 2) * width, 128)

    def mod_piece(m, k):
        part = pl.ds(k * mod_depth, mod_depth)
        return pltpu.make_async_copy(
            mod_hbm.at[m, part, pl.ds(mod_start, width)], mod_buffer.at[m, part], mod_sems.at[m, k]
        )

    def proj_piece(m, k):
        part = pl.ds(k * proj_depth, proj_depth)
        return pltpu.make_async_copy(
            proj_hbm.at[m, part], proj_buffer.at[m, part], proj_sems.at[m, k]
        )

    small = [
        pltpu.make_async_copy(source, target, small_sems.at[k])
        for k, (source, target) in enumerate(
            (
                (text_hbm, text_ref),
                (unembed_hbm, unembed_ref),
                (noise_hbm, noise_ref),
                (renoise_hbm, renoise_ref),
                (embed_hbm, embed_ref),
            )
        )
    ]
    order = []
    for m in range(3):
        order += [proj_piece(m, k) for k in range(PROJ_PIECES)]
        order += [mod_piece(m, k) for k in range(MOD_PIECES)]
    order = small[:2] + order[:LATENTS_AFTER] + small[2:4] + order[LATENTS_AFTER:] + small[4:]
    for copy in order[:IN_FLIGHT]:
        copy.start()

    def take(position):
        order[position].wait()
        if position + IN_FLIGHT < len(order):
            order[position + IN_FLIGHT].start()

    take(0)
    half_size = TEMB // 2
    place = lane_index((8, half_size)).astype(jnp.float32)
    frequency = jnp.exp(place * (-math.log(10000.0) / half_size))
    level = lax.broadcasted_iota(jnp.int32, (8, half_size), 0)
    steps = jnp.where(level == 0, gen_step_ref[0], renoise_step_ref[0]).astype(jnp.float32)
    angles = steps * frequency
    text = jnp.broadcast_to(text_ref[...].astype(jnp.float32), (8, text_ref.shape[1]))
    text = jnp.where(lax.broadcasted_iota(jnp.int32, text.shape, 0) < 2, text, 0.0)
    joined = jnp.concatenate([jnp.cos(angles), jnp.sin(angles), text], 1)
    vectors = (joined / (1.0 + jnp.exp(-joined))).astype(jnp.bfloat16)
    packs = width // PACK
    mod_ref[...] = jnp.zeros_like(mod_ref)
    take(1)
    place = 2
    for m in range(3):
        total = jnp.zeros((8, width), jnp.float32)
        for k in range(PROJ_PIECES + MOD_PIECES):
            if place == LATENTS_AFTER + 2:
                take(place)
                take(place + 1)
                latents = jnp.where(lax.axis_index("mp") % 2 == 0, noise_ref[...], renoise_ref[...])
                latents_ref[...] = latents.astype(jnp.bfloat16)
                place += 2
            take(place)
            place += 1
            if k < PROJ_PIECES:
                part = slice(k * proj_depth, (k + 1) * proj_depth)
                through_ref[m, :, part] = lax.dot_general(
                    unembed_ref[m],
                    proj_buffer[m, part],
                    CONTRACT_LAST,
                    preferred_element_type=jnp.float32,
                ).astype(jnp.bfloat16)
            else:
                part = slice((k - PROJ_PIECES) * mod_depth, (k - PROJ_PIECES + 1) * mod_depth)
                total += jnp.dot(
                    vectors[:, part], mod_buffer[m, part], preferred_element_type=jnp.float32
                )
        if m == 0:
            line = total[0:1]
        elif m == 1:
            line = GUIDANCE * total[1:2] + (1.0 - GUIDANCE) * total[2:3]
        else:
            line = total[1:2]
        for j in range(packs):
            mod_ref[m * packs + j : m * packs + j + 1] = line[:, j * PACK : (j + 1) * PACK]
    take(len(order) - 1)


def streamed_weights(
    gen_step, renoise_step, text, noise, renoise, mod_weight, proj_weight, unembed, embed
):
    depth, width = mod_weight.shape[1], mod_weight.shape[2] // 2
    rows, cols = proj_weight.shape[1:]
    pack_rows = -(-3 * width // PACK // 8) * 8
    return pl.pallas_call(
        stream_kernel,
        out_shape=[
            jax.ShapeDtypeStruct((pack_rows, PACK), jnp.float32),
            jax.ShapeDtypeStruct(noise.shape, jnp.bfloat16),
            jax.ShapeDtypeStruct((3, CH, rows), jnp.bfloat16),
            jax.ShapeDtypeStruct(noise.shape, noise.dtype),
            jax.ShapeDtypeStruct(renoise.shape, renoise.dtype),
            jax.ShapeDtypeStruct(unembed.shape, unembed.dtype),
            jax.ShapeDtypeStruct(embed.shape, embed.dtype),
        ],
        in_specs=[pl.BlockSpec(memory_space=pltpu.SMEM)] * 2
        + [pl.BlockSpec(memory_space=pltpu.HBM)] * 7,
        out_specs=whole_specs(7),
        scratch_shapes=[
            pltpu.VMEM(text.shape, text.dtype),
            pltpu.VMEM((3, depth, width), jnp.bfloat16),
            pltpu.VMEM((3, rows, cols), jnp.bfloat16),
            pltpu.SemaphoreType.DMA((3, MOD_PIECES)),
            pltpu.SemaphoreType.DMA((3, PROJ_PIECES)),
            pltpu.SemaphoreType.DMA((5,)),
        ],
        compiler_params=vmem_params(),
        name="stream_weights",
    )(
        gen_step,
        renoise_step,
        *(
            pltpu.with_memory_space_constraint(x, pltpu.HBM)
            for x in (text, noise, renoise, mod_weight, proj_weight, unembed, embed)
        ),
    )


def embed_kernel(embed_ref, unembed_ref, gram_ref, rows_ref, direct_ref):
    rows, cols = rows_ref.shape[2], unembed_ref.shape[2]
    f = lax.axis_index("fsdp")
    row_start = pl.multiple_of(f * rows, 128)
    col_start = pl.multiple_of(lax.axis_index("mp") * cols, 128)
    nothing = jnp.zeros((CH, cols), jnp.bfloat16)
    for m in range(3):
        whole = embed_ref[m].astype(jnp.float32)
        average = jnp.sum(whole, axis=1, keepdims=True) * (1.0 / D)
        rows_ref[m] = embed_ref[m, :, pl.ds(row_start, rows)].astype(jnp.float32) - average
        direct = lax.dot_general(
            embed_ref[m, :, pl.ds(col_start, cols)],
            jnp.concatenate([unembed_ref[m], nothing], 0),
            CONTRACT_LAST,
            preferred_element_type=jnp.float32,
        )
        direct_ref[m] = jnp.where(f == 0, direct, 0.0)
        pair = jnp.concatenate(split_two(whole - average), 0)
        product = lax.dot_general(pair, pair, CONTRACT_LAST, preferred_element_type=jnp.float32)
        product = product[:CH] + product[CH:]
        gram = (product + pltpu.roll(product, CH, 1)) * (1.0 / D)
        gram_ref[m] = jnp.concatenate(split_three(block_diagonal(gram, gram)), 1)


def embed_products(embed, unembed, rows):
    return pl.pallas_call(
        embed_kernel,
        out_shape=[
            jax.ShapeDtypeStruct((3, 2 * CH, 6 * CH), jnp.bfloat16),
            jax.ShapeDtypeStruct((3, CH, rows), jnp.float32),
            jax.ShapeDtypeStruct((3, CH, 2 * CH), jnp.float32),
        ],
        in_specs=whole_specs(2),
        out_specs=whole_specs(3),
        compiler_params=vmem_params(),
        cost_estimate=pl.CostEstimate(
            flops=6 * 128 * 128 * D, bytes_accessed=6 * CH * D, transcendentals=0
        ),
        name="embed_products",
    )(embed, unembed)


def pair_ones():
    shape = (2 * CH, 2 * CH)
    lanes = lane_index(shape)
    subs = lax.broadcasted_iota(jnp.int32, shape, 0)
    ones = jnp.where((lanes < CH) == (subs < CH), 1.0, 0.0).astype(jnp.bfloat16)
    return jnp.concatenate([ones, ones], 0)


def inverse_deviation(u, by_gram, ones):
    squares = jnp.concatenate(split_two(by_gram * u), 1)
    spread = jnp.dot(squares, ones, preferred_element_type=jnp.float32)
    return lax.rsqrt(jnp.maximum(spread, 0.0) + EPS_NORM)


def columns(product, i):
    return product[:, i * 2 * CH : (i + 1) * 2 * CH]


def sample_latents(noise_ref, first_ref, second_ref):
    first, second = first_ref[...], second_ref[...]
    core = lax.axis_index("mp") % 2
    other = jnp.where(core == 0, first, second)
    other_renoise = jnp.where(core == 0, second, first)
    return jnp.concatenate([noise_ref[...].astype(jnp.bfloat16), other], 0), other_renoise


def noise_kernel(noise_ref, first_ref, second_ref, gram_ref, inverse_ref, normal_ref):
    noise, _ = sample_latents(noise_ref, first_ref, second_ref)
    product = jnp.dot(noise, gram_ref[0], preferred_element_type=jnp.float32)
    noise = noise.astype(jnp.float32)
    by_gram = columns(product, 0) + columns(product, 1) + columns(product, 2)
    inverse = inverse_deviation(noise, by_gram, pair_ones())
    inverse_ref[...] = inverse
    normal_ref[...] = (noise * inverse).astype(jnp.bfloat16)


def noise_statistics(noise, first, second, gram):
    shape = (2 * noise.shape[0], noise.shape[1])
    return pl.pallas_call(
        noise_kernel,
        out_shape=[
            jax.ShapeDtypeStruct(shape, jnp.float32),
            jax.ShapeDtypeStruct(shape, jnp.bfloat16),
        ],
        in_specs=whole_specs(4),
        out_specs=whole_specs(2),
        compiler_params=vmem_params(),
        name="noise_statistics",
    )(noise, first, second, gram)


def maps_kernel(kept_ref, got_ref, rows_ref, through_ref, direct_ref, maps_ref, mod_ref):
    rows = rows_ref.shape[2]
    packs = rows // PACK
    f = lax.axis_index("fsdp")
    kept, got = kept_ref[...], got_ref[...]
    shift = jnp.where(f == 0, kept, got)
    scale = jnp.where(f == 0, got, kept)
    offsets = []
    for m in range(3):
        pieces = []
        for j in range(packs):
            line = slice(m * packs + j, m * packs + j + 1)
            pieces.append(
                jnp.concatenate(
                    [
                        rows_ref[m, :, j * PACK : (j + 1) * PACK] * (1.0 + scale[line]),
                        shift[line],
                        jnp.zeros((7, PACK), jnp.float32),
                    ],
                    0,
                )
            )
        left = jnp.concatenate(pieces, 1).astype(jnp.bfloat16)
        through = jnp.concatenate([jnp.zeros((CH, rows), jnp.bfloat16), through_ref[m]], 0)
        product = lax.dot_general(
            left, through, CONTRACT_LAST, preferred_element_type=jnp.float32
        )
        maps_ref[m * CH : (m + 1) * CH] = product[:CH] + direct_ref[m]
        offsets.append(product[CH : CH + 1])
    maps_ref[3 * CH :] = jnp.concatenate(offsets + [jnp.zeros((5, PACK), jnp.float32)], 0)
    rest = jnp.zeros((mod_ref.shape[0] - 2 * packs, PACK), jnp.float32)
    mod_ref[...] = jnp.concatenate([shift[:packs], scale[:packs], rest], 0).astype(jnp.bfloat16)


def modulated_maps(kept, got, rows_part, through, direct):
    packs = rows_part.shape[2] // PACK
    return pl.pallas_call(
        maps_kernel,
        out_shape=[
            jax.ShapeDtypeStruct((3 * CH + 8, 2 * CH), jnp.float32),
            jax.ShapeDtypeStruct((-(-2 * packs // 16) * 16, PACK), jnp.bfloat16),
        ],
        in_specs=whole_specs(5),
        out_specs=whole_specs(2),
        compiler_params=vmem_params(),
        name="modulated_maps",
    )(kept, got, rows_part, through, direct)


MAP_ROWS = CH + 16


def token_kernel(
    level_ref,
    noise_ref,
    first_ref,
    second_ref,
    renoise_ref,
    inverse_ref,
    normal_ref,
    gram_ref,
    maps_a,
    maps_b,
    maps_c,
    maps_d,
    mod_ref,
    score_ref,
    payload_ref,
):
    half = renoise_ref.shape[0]
    level = level_ref[0]
    maps = [part[...].astype(jnp.float32) for part in (maps_a, maps_b, maps_c, maps_d)]
    maps = (maps[0] + maps[1]) + (maps[2] + maps[3])
    width = 2 * CH
    ones = pair_ones()

    def model_matrix(m):
        base = m * CH
        pair = maps[base : base + CH]
        turned = pltpu.roll(pair, CH, 1)
        direct = block_diagonal(pair, turned)
        modulated = block_diagonal(turned, pair)
        matrix = jnp.concatenate([direct, modulated], 1).astype(jnp.bfloat16)
        offset = maps[3 * CH + m : 3 * CH + m + 1]
        return matrix, offset + pltpu.roll(offset, CH, 1)

    def combine(product, inverse, offset):
        return columns(product, 0) + inverse * columns(product, 1) + offset

    noise, other_renoise = sample_latents(noise_ref, first_ref, second_ref)
    renoise = jnp.concatenate([renoise_ref[...], other_renoise.astype(jnp.float32)], 0)
    matrix, offset = model_matrix(0)
    product = jnp.dot(noise, matrix, preferred_element_type=jnp.float32)
    clean = combine(product, inverse_ref[...], offset)
    noisy = ((1.0 - level) * clean + level * renoise).astype(jnp.bfloat16)
    noisy_wide = noisy.astype(jnp.float32)

    def velocity(m):
        matrix, offset = model_matrix(m)
        matrix = jnp.concatenate([matrix, gram_ref[m]], 1)
        product = jnp.dot(noisy, matrix, preferred_element_type=jnp.float32)
        by_gram = columns(product, 2) + columns(product, 3) + columns(product, 4)
        return combine(product, inverse_deviation(noisy_wide, by_gram, ones), offset)

    real_v = velocity(1)
    fake_v = velocity(2)
    total = jnp.sum(jnp.abs(clean - renoise + real_v))
    gap_scale = level * total * (1.0 / (2 * half * width)) + EPS_GAP
    score = level * (real_v - fake_v) / gap_scale
    score_ref[...] = score[:half]
    tokens = 4 * half * lax.axis_size("dp")
    cotangent = (score * (1.0 / math.sqrt(tokens))).astype(jnp.bfloat16)
    pairs = lax.dot_general(
        normal_ref[...], cotangent, CONTRACT_FIRST, preferred_element_type=jnp.float32
    )
    outer = pairs[:CH] + pltpu.roll(pairs[CH:], CH, 1)
    sums = jnp.sum(cotangent.astype(jnp.float32), axis=0, keepdims=True)
    sums = sums + pltpu.roll(sums, CH, 1)
    rest = jnp.zeros((MAP_ROWS - CH - 1, width), jnp.float32)
    payload_ref[:MAP_ROWS] = jnp.concatenate([outer, sums, rest], 0).astype(jnp.bfloat16)
    payload_ref[MAP_ROWS:] = mod_ref[...]


def token_phase(level, noise, first, second, renoise, inverse, normal, gram, maps, mod):
    return pl.pallas_call(
        token_kernel,
        out_shape=[
            jax.ShapeDtypeStruct(renoise.shape, jnp.float32),
            jax.ShapeDtypeStruct((MAP_ROWS + mod.shape[0], 2 * CH), jnp.bfloat16),
        ],
        in_specs=[pl.BlockSpec(memory_space=pltpu.SMEM)] + whole_specs(12),
        out_specs=whole_specs(2),
        compiler_params=vmem_params(),
        name="tokens",
    )(level, noise, first, second, renoise, inverse, normal, gram, *maps, mod)


GRAD_PIECES = 6


def grad_kernel(
    block_a,
    block_b,
    block_c,
    block_d,
    rows_ref,
    unembed_ref,
    score_ref,
    grad_hbm,
    score_hbm,
    buffer,
    sems,
):
    score_copy = pltpu.make_async_copy(score_ref, score_hbm, sems.at[GRAD_PIECES])
    score_copy.start()
    rows = rows_ref.shape[2]
    packs = rows // PACK
    depth = rows // GRAD_PIECES
    blocks = [block[...] for block in (block_a, block_b, block_c, block_d)]
    left = jnp.concatenate([block[:MAP_ROWS, :CH] for block in blocks], 0)
    mods = [block[MAP_ROWS:].astype(jnp.float32) for block in blocks]
    unembed = unembed_ref[0]

    def piece(k):
        part = pl.ds(k * depth, depth)
        return pltpu.make_async_copy(buffer.at[part], grad_hbm.at[part], sems.at[k])

    tiles = []
    for j in range(packs):
        embed_tile = rows_ref[0, :, j * PACK : (j + 1) * PACK]
        column = []
        for mod in mods:
            column += [
                embed_tile * (1.0 + mod[packs + j : packs + j + 1]),
                mod[j : j + 1],
                jnp.zeros((MAP_ROWS - CH - 1, PACK), jnp.float32),
            ]
        tiles.append(jnp.concatenate(column, 0).astype(jnp.bfloat16))
    grad_map = lax.dot_general(
        left, jnp.concatenate(tiles, 1), CONTRACT_FIRST, preferred_element_type=jnp.float32
    ).astype(jnp.bfloat16)
    for k in range(GRAD_PIECES):
        part = slice(k * depth, (k + 1) * depth)
        buffer[part] = lax.dot_general(
            grad_map[:, part], unembed, CONTRACT_FIRST, preferred_element_type=jnp.float32
        )
        piece(k).start()
    for k in range(GRAD_PIECES):
        piece(k).wait()
    score_copy.wait()


def gradient(blocks, rows_part, unembed, score):
    rows = rows_part.shape[2]
    cols = unembed.shape[2]
    return pl.pallas_call(
        grad_kernel,
        out_shape=[
            jax.ShapeDtypeStruct((rows, cols), jnp.float32),
            jax.ShapeDtypeStruct(score.shape, jnp.float32),
        ],
        in_specs=whole_specs(7),
        out_specs=[pl.BlockSpec(memory_space=pl.ANY)] * 2,
        scratch_shapes=[
            pltpu.VMEM((rows, cols), jnp.float32),
            pltpu.SemaphoreType.DMA((GRAD_PIECES + 1,)),
        ],
        compiler_params=vmem_params(),
        name="gradient",
    )(*blocks, rows_part, unembed, score)


def body(
    gen_noise, renoise, gen_step, renoise_step, text_pooled, embed, mod_weight, proj_weight, unembed
):
    mine, latents, through, noise, renoise, unembed, embed = streamed_weights(
        gen_step,
        renoise_step,
        text_pooled,
        gen_noise[0],
        renoise[0],
        mod_weight,
        proj_weight,
        unembed,
        embed,
    )
    f = lax.axis_index("fsdp")
    theirs = swap(mine, "mp", 1)
    own_half = lax.axis_index("mp") % 2 == f
    kept = jnp.where(own_half, mine, theirs)
    got = swap(jnp.where(own_half, theirs, mine), "fsdp", 1)
    first = swap(latents, "fsdp", 1)
    got, first = lax.optimization_barrier((got, first))
    second = swap(first, "mp", 1)
    gram, rows_part, direct = embed_products(embed, unembed, proj_weight.shape[1])
    maps, mod = modulated_maps(kept, got, rows_part, through, direct)
    maps = (maps + swap(maps, "mp", 1)).astype(jnp.bfloat16)
    inverse, normal = noise_statistics(noise, first, second, gram)
    maps = chip_blocks(maps)
    level = renoise_step.astype(jnp.float32) / 1000.0
    score, payload = token_phase(
        level, noise, first, second, renoise, inverse, normal, gram, maps, mod
    )
    blocks = gather_samples(payload)
    gen_grad, score_gap = gradient(blocks, rows_part, unembed, score)
    return (gen_grad, score_gap[None])


def fits_kernels(mesh):
    return mesh.shape["mp"] == 4 and mesh.shape["fsdp"] == 2 and mesh.shape["dp"] == 4


def solution(mesh):
    return jax.shard_map(
        body if fits_kernels(mesh) else plain_body,
        mesh=mesh,
        in_specs=(
            P("dp", "fsdp", None),
            P("dp", "fsdp", None),
            P("dp"),
            P("dp"),
            P("dp", None),
            P(),
            P(None, None, "fsdp"),
            P(None, "fsdp", "mp"),
            P(None, None, "mp"),
        ),
        out_specs=(P("fsdp", "mp"), P("dp", "fsdp", None)),
        check_vma=False,
    )
```

```python
import math

import jax
import jax.numpy as jnp
from jax import lax
from jax.experimental import pallas as pl
from jax.experimental.pallas import tpu as pltpu
from jax.sharding import PartitionSpec as P

D = 3072
CH = 64
TEMB = 256

GUIDANCE = 3.5
EPS_NORM = 1e-06
EPS_GAP = 1e-05
HI = lax.Precision.HIGHEST


def sinusoid(timesteps):
    half_size = TEMB // 2
    frequency = jnp.exp(-math.log(10000.0) * jnp.arange(half_size, dtype=jnp.float32) / half_size)
    angles = timesteps.astype(jnp.float32)[:, None] * frequency[None, :]
    return jnp.concatenate([jnp.cos(angles), jnp.sin(angles)], axis=1)


def condition(timesteps, pooled):
    joined = jnp.concatenate([sinusoid(timesteps), pooled.astype(jnp.float32)], axis=1)
    return jax.nn.silu(joined).astype(jnp.bfloat16)


def swap(x, axes, mask):
    count = lax.axis_size(axes)
    return lax.ppermute(x, axes, [(i, i ^ mask) for i in range(count)])


def plane_sum(x):
    if lax.axis_size("mp") != 4 or lax.axis_size("fsdp") != 2:
        return lax.psum(x, ("mp", "fsdp"))
    x = x + swap(x, "mp", 1)
    plane = ("mp", "fsdp")
    parts = [swap(x, plane, mask) for mask in (4, 1, 5)]
    return (x + parts[0]) + (parts[1] + parts[2])


def chip_blocks(x):
    pairs = []
    for m in range(4):
        for f in range(2):
            pairs.append((m * 2 + f, (m * 2 + f) ^ (4 if m % 2 == 0 else 1)))
    side = lax.ppermute(x, ("mp", "fsdp"), pairs)
    across = swap(x, ("mp", "fsdp"), 5)
    return [x, side, swap(side, "mp", 1), across]


def gather_samples(x):
    count = lax.axis_size("dp")
    if lax.axis_size("mp") != 4 or count != 4:
        blocks = lax.all_gather(x, "dp")
        return [blocks[i] for i in range(count)]
    pairs = []
    for m in range(4):
        for s in range(4):
            pairs.append((m * 4 + s, m * 4 + (s ^ (1 if m % 2 == 0 else 2))))
    near = lax.ppermute(x, ("mp", "dp"), pairs)
    far = swap(x, "dp", 3)
    return [x, near, swap(near, "mp", 1), far]


def exchange_modulation(local_mod, rows):
    if lax.axis_size("fsdp") == 2:
        f = lax.axis_index("fsdp")
        mine = lax.dynamic_slice_in_dim(local_mod, f * rows, rows, 1)
        theirs = swap(lax.dynamic_slice_in_dim(local_mod, (1 - f) * rows, rows, 1), "fsdp", 1)
        return jnp.where(f == 0, mine, theirs), jnp.where(f == 0, theirs, mine)
    whole = lax.all_gather(local_mod, "fsdp", axis=1, tiled=True)
    start = lax.axis_index("fsdp") * rows
    return (
        lax.dynamic_slice_in_dim(whole[:, :D], start, rows, 1),
        lax.dynamic_slice_in_dim(whole[:, D:], start, rows, 1),
    )


def dot(a, b, precision=HI):
    return jnp.dot(a, b, precision=precision, preferred_element_type=jnp.float32)


def both(x):
    zero = jnp.zeros_like(x)
    return jnp.concatenate(
        [jnp.concatenate([x, zero], 1), jnp.concatenate([zero, x], 1)], 0
    )


def plain_body(
    gen_noise, renoise, gen_step, renoise_step, text_pooled, embed, mod_weight, proj_weight, unembed
):
    rows, cols = proj_weight.shape[1], proj_weight.shape[2]
    f = lax.axis_index("fsdp")
    noise_all = lax.all_gather(gen_noise[0], "fsdp", axis=0, tiled=True)
    renoise_all = lax.all_gather(renoise[0], "fsdp", axis=0, tiled=True)

    blank_text = jnp.zeros_like(text_pooled)
    gen_vec = condition(gen_step, text_pooled)
    real_vec = jnp.concatenate(
        [condition(renoise_step, text_pooled), condition(renoise_step, blank_text)], 0
    )
    teacher_mod = jnp.dot(real_vec, mod_weight[1], preferred_element_type=jnp.float32)
    local_mod = jnp.concatenate(
        [
            jnp.dot(gen_vec, mod_weight[0], preferred_element_type=jnp.float32),
            GUIDANCE * teacher_mod[0:1] + (1.0 - GUIDANCE) * teacher_mod[1:2],
            jnp.dot(real_vec[0:1], mod_weight[2], preferred_element_type=jnp.float32),
        ],
        axis=0,
    )
    shift, scale = exchange_modulation(local_mod, rows)

    centred = embed.astype(jnp.float32)
    centred = centred - jnp.mean(centred, axis=2, keepdims=True)
    gram = [dot(centred[m], centred[m].T) / D for m in range(3)]
    centred_rows = lax.dynamic_slice_in_dim(centred, f * rows, rows, 2)
    embed_cols = lax.dynamic_slice_in_dim(embed, lax.axis_index("mp") * cols, cols, 2)

    pieces = []
    for m in range(3):
        through = lax.dot_general(
            proj_weight[m], unembed[m], (((1,), (1,)), ((), ())), preferred_element_type=jnp.float32
        )
        direct = lax.dot_general(
            embed_cols[m], unembed[m], (((1,), (1,)), ((), ())), preferred_element_type=jnp.float32
        )
        direct = jnp.where(f == 0, direct, 0.0)
        modulated = dot(centred_rows[m] * (1.0 + scale[m : m + 1]), through)
        offset = dot(shift[m : m + 1], through)
        offset = jnp.concatenate([offset, jnp.zeros((7, CH), jnp.float32)], 0)
        pieces.append(
            jnp.concatenate(
                [
                    jnp.concatenate([direct, modulated], 1),
                    jnp.concatenate([offset, jnp.zeros_like(offset)], 1),
                ],
                0,
            )
        )
    maps = plane_sum(jnp.concatenate(pieces, 0)).reshape(3, CH + 8, 2 * CH)
    direct = [both(maps[m, :CH, :CH]) for m in range(3)]
    modulated = [both(maps[m, :CH, CH:]) for m in range(3)]
    offset = [jnp.concatenate([maps[m, CH : CH + 1, :CH]] * 2, 1) for m in range(3)]

    ones = both(jnp.ones((CH, CH), jnp.float32))

    def normalized(u, m):
        spread = dot(dot(u, both(gram[m])) * u, ones)
        return u * lax.rsqrt(jnp.maximum(spread, 0.0) + EPS_NORM)

    def model(u, u_norm, m):
        return dot(u, direct[m]) + dot(u_norm, modulated[m]) + offset[m]

    noise = noise_all.astype(jnp.bfloat16).astype(jnp.float32)
    noise_norm = normalized(noise, 0)
    clean = model(noise, noise_norm, 0)
    level = renoise_step[0].astype(jnp.float32) / 1000.0
    noisy = (1.0 - level) * clean + level * renoise_all
    noisy = noisy.astype(jnp.bfloat16).astype(jnp.float32)
    real_v = model(noisy, normalized(noisy, 1), 1)
    fake_v = model(noisy, normalized(noisy, 2), 2)
    total = jnp.sum(jnp.abs(clean - renoise_all + real_v))
    gap_scale = level * total / (noise_all.shape[0] * 2 * CH) + EPS_GAP
    score = level * (real_v - fake_v) / gap_scale
    local_rows = gen_noise.shape[1]
    score_gap = lax.dynamic_slice_in_dim(score, f * local_rows, local_rows, 0)

    all_tokens = noise_all.shape[0] * 2 * lax.axis_size("dp")
    cotangent = (score / math.sqrt(all_tokens)).astype(jnp.bfloat16).astype(jnp.float32)
    pairs = dot(noise_norm.T, cotangent)
    outer = pairs[:CH, :CH] + pairs[CH:, CH:]
    sums = jnp.sum(cotangent, axis=0)
    sums = sums[:CH] + sums[CH:]
    payload = jnp.concatenate(
        [
            jnp.pad(outer, ((0, 0), (0, CH))),
            jnp.pad(sums[None], ((0, 7), (0, CH))),
            jnp.concatenate([shift[0], scale[0]]).reshape(-1, 2 * CH),
        ],
        0,
    )
    blocks = gather_samples(payload)
    grad_map = jnp.zeros((CH, rows), jnp.float32)
    for block in blocks:
        block_mod = block[CH + 8 :].reshape(2, rows)
        grad_map += dot(block[:CH, :CH].T, centred_rows[0]) * (1.0 + block_mod[1:2])
        grad_map += block[CH, :CH][:, None] * block_mod[0:1]
    gen_grad = lax.dot_general(
        grad_map.astype(jnp.bfloat16),
        unembed[0],
        (((0,), (0,)), ((), ())),
        preferred_element_type=jnp.float32,
    )
    return (gen_grad, score_gap[None])


def vmem_params():
    return pltpu.CompilerParams(vmem_limit_bytes=48 * 1024 * 1024)


def whole_specs(count):
    return [pl.BlockSpec(memory_space=pltpu.VMEM)] * count


def split_two(x):
    high = x.astype(jnp.bfloat16)
    return high, (x - high.astype(jnp.float32)).astype(jnp.bfloat16)


def split_three(x):
    high = x.astype(jnp.bfloat16)
    rest = x - high.astype(jnp.float32)
    middle = rest.astype(jnp.bfloat16)
    return high, middle, (rest - middle.astype(jnp.float32)).astype(jnp.bfloat16)


def lane_index(shape):
    return lax.broadcasted_iota(jnp.int32, shape, len(shape) - 1)


def block_diagonal(left_copy, right_copy):
    lanes = lane_index(left_copy.shape)
    top = jnp.where(lanes < CH, left_copy, 0.0)
    bottom = jnp.where(lanes >= CH, right_copy, 0.0)
    return jnp.concatenate([top, bottom], 0)


MOD_PIECES = 4
PROJ_PIECES = 3
IN_FLIGHT = 12
LATENTS_AFTER = 8
PACK = 128
CONTRACT_LAST = (((1,), (1,)), ((), ()))
CONTRACT_FIRST = (((0,), (0,)), ((), ()))


def stream_kernel(
    gen_step_ref,
    renoise_step_ref,
    text_hbm,
    noise_hbm,
    renoise_hbm,
    mod_hbm,
    proj_hbm,
    unembed_hbm,
    embed_hbm,
    mod_ref,
    latents_ref,
    through_ref,
    noise_ref,
    renoise_ref,
    unembed_ref,
    embed_ref,
    text_ref,
    mod_buffer,
    proj_buffer,
    mod_sems,
    proj_sems,
    small_sems,
):
    width = mod_buffer.shape[2]
    rows, cols = proj_buffer.shape[1:]
    mod_depth = mod_buffer.shape[1] // MOD_PIECES
    proj_depth = rows // PROJ_PIECES
    mod_start = pl.multiple_of((lax.axis_index("mp") % 2) * width, 128)

    def mod_piece(m, k):
        part = pl.ds(k * mod_depth, mod_depth)
        return pltpu.make_async_copy(
            mod_hbm.at[m, part, pl.ds(mod_start, width)], mod_buffer.at[m, part], mod_sems.at[m, k]
        )

    def proj_piece(m, k):
        part = pl.ds(k * proj_depth, proj_depth)
        return pltpu.make_async_copy(
            proj_hbm.at[m, part], proj_buffer.at[m, part], proj_sems.at[m, k]
        )

    small = [
        pltpu.make_async_copy(source, target, small_sems.at[k])
        for k, (source, target) in enumerate(
            (
                (text_hbm, text_ref),
                (unembed_hbm, unembed_ref),
                (noise_hbm, noise_ref),
                (renoise_hbm, renoise_ref),
                (embed_hbm, embed_ref),
            )
        )
    ]
    order = []
    for m in range(3):
        order += [proj_piece(m, k) for k in range(PROJ_PIECES)]
        order += [mod_piece(m, k) for k in range(MOD_PIECES)]
    order = small[:2] + order[:LATENTS_AFTER] + small[2:4] + order[LATENTS_AFTER:] + small[4:]
    for copy in order[:IN_FLIGHT]:
        copy.start()

    def take(position):
        order[position].wait()
        if position + IN_FLIGHT < len(order):
            order[position + IN_FLIGHT].start()

    take(0)
    half_size = TEMB // 2
    place = lane_index((8, half_size)).astype(jnp.float32)
    frequency = jnp.exp(place * (-math.log(10000.0) / half_size))
    level = lax.broadcasted_iota(jnp.int32, (8, half_size), 0)
    steps = jnp.where(level == 0, gen_step_ref[0], renoise_step_ref[0]).astype(jnp.float32)
    angles = steps * frequency
    text = jnp.broadcast_to(text_ref[...].astype(jnp.float32), (8, text_ref.shape[1]))
    text = jnp.where(lax.broadcasted_iota(jnp.int32, text.shape, 0) < 2, text, 0.0)
    joined = jnp.concatenate([jnp.cos(angles), jnp.sin(angles), text], 1)
    vectors = (joined / (1.0 + jnp.exp(-joined))).astype(jnp.bfloat16)
    packs = width // PACK
    mod_ref[...] = jnp.zeros_like(mod_ref)
    take(1)
    place = 2
    for m in range(3):
        total = jnp.zeros((8, width), jnp.float32)
        for k in range(PROJ_PIECES + MOD_PIECES):
            if place == LATENTS_AFTER + 2:
                take(place)
                take(place + 1)
                half = noise_ref.shape[0]
                latents_ref[:half] = noise_ref[...].astype(jnp.bfloat16)
                latents_ref[half:] = renoise_ref[...].astype(jnp.bfloat16)
                place += 2
            take(place)
            place += 1
            if k < PROJ_PIECES:
                part = slice(k * proj_depth, (k + 1) * proj_depth)
                through_ref[m, :, part] = lax.dot_general(
                    unembed_ref[m],
                    proj_buffer[m, part],
                    CONTRACT_LAST,
                    preferred_element_type=jnp.float32,
                ).astype(jnp.bfloat16)
            else:
                part = slice((k - PROJ_PIECES) * mod_depth, (k - PROJ_PIECES + 1) * mod_depth)
                total += jnp.dot(
                    vectors[:, part], mod_buffer[m, part], preferred_element_type=jnp.float32
                )
        if m == 0:
            line = total[0:1]
        elif m == 1:
            line = GUIDANCE * total[1:2] + (1.0 - GUIDANCE) * total[2:3]
        else:
            line = total[1:2]
        for j in range(packs):
            mod_ref[m * packs + j : m * packs + j + 1] = line[:, j * PACK : (j + 1) * PACK]
    take(len(order) - 1)


def streamed_weights(
    gen_step, renoise_step, text, noise, renoise, mod_weight, proj_weight, unembed, embed
):
    depth, width = mod_weight.shape[1], mod_weight.shape[2] // 2
    rows, cols = proj_weight.shape[1:]
    pack_rows = -(-3 * width // PACK // 8) * 8
    return pl.pallas_call(
        stream_kernel,
        out_shape=[
            jax.ShapeDtypeStruct((pack_rows, PACK), jnp.float32),
            jax.ShapeDtypeStruct((2 * noise.shape[0], noise.shape[1]), jnp.bfloat16),
            jax.ShapeDtypeStruct((3, CH, rows), jnp.bfloat16),
            jax.ShapeDtypeStruct(noise.shape, noise.dtype),
            jax.ShapeDtypeStruct(renoise.shape, renoise.dtype),
            jax.ShapeDtypeStruct(unembed.shape, unembed.dtype),
            jax.ShapeDtypeStruct(embed.shape, embed.dtype),
        ],
        in_specs=[pl.BlockSpec(memory_space=pltpu.SMEM)] * 2
        + [pl.BlockSpec(memory_space=pltpu.HBM)] * 7,
        out_specs=whole_specs(7),
        scratch_shapes=[
            pltpu.VMEM(text.shape, text.dtype),
            pltpu.VMEM((3, depth, width), jnp.bfloat16),
            pltpu.VMEM((3, rows, cols), jnp.bfloat16),
            pltpu.SemaphoreType.DMA((3, MOD_PIECES)),
            pltpu.SemaphoreType.DMA((3, PROJ_PIECES)),
            pltpu.SemaphoreType.DMA((5,)),
        ],
        compiler_params=vmem_params(),
        name="stream_weights",
    )(
        gen_step,
        renoise_step,
        *(
            pltpu.with_memory_space_constraint(x, pltpu.HBM)
            for x in (text, noise, renoise, mod_weight, proj_weight, unembed, embed)
        ),
    )


def embed_kernel(embed_ref, unembed_ref, gram_ref, rows_ref, direct_ref):
    rows, cols = rows_ref.shape[2], unembed_ref.shape[2]
    f = lax.axis_index("fsdp")
    row_start = pl.multiple_of(f * rows, 128)
    col_start = pl.multiple_of(lax.axis_index("mp") * cols, 128)
    nothing = jnp.zeros((CH, cols), jnp.bfloat16)
    for m in range(3):
        whole = embed_ref[m].astype(jnp.float32)
        average = jnp.sum(whole, axis=1, keepdims=True) * (1.0 / D)
        rows_ref[m] = embed_ref[m, :, pl.ds(row_start, rows)].astype(jnp.float32) - average
        direct = lax.dot_general(
            embed_ref[m, :, pl.ds(col_start, cols)],
            jnp.concatenate([unembed_ref[m], nothing], 0),
            CONTRACT_LAST,
            preferred_element_type=jnp.float32,
        )
        direct_ref[m] = jnp.where(f == 0, direct, 0.0)
        pair = jnp.concatenate(split_two(whole - average), 0)
        product = lax.dot_general(pair, pair, CONTRACT_LAST, preferred_element_type=jnp.float32)
        product = product[:CH] + product[CH:]
        gram = (product + pltpu.roll(product, CH, 1)) * (1.0 / D)
        gram_ref[m] = jnp.concatenate(split_three(block_diagonal(gram, gram)), 1)


def embed_products(embed, unembed, rows):
    return pl.pallas_call(
        embed_kernel,
        out_shape=[
            jax.ShapeDtypeStruct((3, 2 * CH, 6 * CH), jnp.bfloat16),
            jax.ShapeDtypeStruct((3, CH, rows), jnp.float32),
            jax.ShapeDtypeStruct((3, CH, 2 * CH), jnp.float32),
        ],
        in_specs=whole_specs(2),
        out_specs=whole_specs(3),
        compiler_params=vmem_params(),
        cost_estimate=pl.CostEstimate(
            flops=6 * 128 * 128 * D, bytes_accessed=6 * CH * D, transcendentals=0
        ),
        name="embed_products",
    )(embed, unembed)


def pair_ones():
    shape = (2 * CH, 2 * CH)
    lanes = lane_index(shape)
    subs = lax.broadcasted_iota(jnp.int32, shape, 0)
    ones = jnp.where((lanes < CH) == (subs < CH), 1.0, 0.0).astype(jnp.bfloat16)
    return jnp.concatenate([ones, ones], 0)


def inverse_deviation(u, by_gram, ones):
    squares = jnp.concatenate(split_two(by_gram * u), 1)
    spread = jnp.dot(squares, ones, preferred_element_type=jnp.float32)
    return lax.rsqrt(jnp.maximum(spread, 0.0) + EPS_NORM)


def columns(product, i):
    return product[:, i * 2 * CH : (i + 1) * 2 * CH]


def sample_latents(noise_ref, other_ref):
    half = noise_ref.shape[0]
    noise = jnp.concatenate([noise_ref[...].astype(jnp.bfloat16), other_ref[:half]], 0)
    return noise, other_ref[half:]


def noise_kernel(noise_ref, other_ref, gram_ref, inverse_ref, normal_ref):
    noise, _ = sample_latents(noise_ref, other_ref)
    product = jnp.dot(noise, gram_ref[0], preferred_element_type=jnp.float32)
    noise = noise.astype(jnp.float32)
    by_gram = columns(product, 0) + columns(product, 1) + columns(product, 2)
    inverse = inverse_deviation(noise, by_gram, pair_ones())
    inverse_ref[...] = inverse
    normal_ref[...] = (noise * inverse).astype(jnp.bfloat16)


def noise_statistics(noise, other, gram):
    shape = (2 * noise.shape[0], noise.shape[1])
    return pl.pallas_call(
        noise_kernel,
        out_shape=[
            jax.ShapeDtypeStruct(shape, jnp.float32),
            jax.ShapeDtypeStruct(shape, jnp.bfloat16),
        ],
        in_specs=whole_specs(3),
        out_specs=whole_specs(2),
        compiler_params=vmem_params(),
        name="noise_statistics",
    )(noise, other, gram)


def maps_kernel(kept_ref, got_ref, rows_ref, through_ref, direct_ref, maps_ref, mod_ref):
    rows = rows_ref.shape[2]
    packs = rows // PACK
    f = lax.axis_index("fsdp")
    kept, got = kept_ref[...], got_ref[...]
    shift = jnp.where(f == 0, kept, got)
    scale = jnp.where(f == 0, got, kept)
    offsets = []
    for m in range(3):
        pieces = []
        for j in range(packs):
            line = slice(m * packs + j, m * packs + j + 1)
            pieces.append(
                jnp.concatenate(
                    [
                        rows_ref[m, :, j * PACK : (j + 1) * PACK] * (1.0 + scale[line]),
                        shift[line],
                        jnp.zeros((7, PACK), jnp.float32),
                    ],
                    0,
                )
            )
        left = jnp.concatenate(pieces, 1).astype(jnp.bfloat16)
        through = jnp.concatenate([jnp.zeros((CH, rows), jnp.bfloat16), through_ref[m]], 0)
        product = lax.dot_general(
            left, through, CONTRACT_LAST, preferred_element_type=jnp.float32
        )
        maps_ref[m * CH : (m + 1) * CH] = (product[:CH] + direct_ref[m]).astype(jnp.bfloat16)
        offsets.append(product[CH : CH + 1])
    maps_ref[3 * CH :] = jnp.concatenate(
        offsets + [jnp.zeros((5, PACK), jnp.float32)], 0
    ).astype(jnp.bfloat16)
    rest = jnp.zeros((mod_ref.shape[0] - 2 * packs, PACK), jnp.float32)
    mod_ref[...] = jnp.concatenate([shift[:packs], scale[:packs], rest], 0).astype(jnp.bfloat16)


def modulated_maps(kept, got, rows_part, through, direct):
    packs = rows_part.shape[2] // PACK
    return pl.pallas_call(
        maps_kernel,
        out_shape=[
            jax.ShapeDtypeStruct((3 * CH + 8, 2 * CH), jnp.bfloat16),
            jax.ShapeDtypeStruct((-(-2 * packs // 16) * 16, PACK), jnp.bfloat16),
        ],
        in_specs=whole_specs(5),
        out_specs=whole_specs(2),
        compiler_params=vmem_params(),
        name="modulated_maps",
    )(kept, got, rows_part, through, direct)


MAP_ROWS = CH + 16


def token_kernel(
    level_ref,
    noise_ref,
    other_ref,
    renoise_ref,
    inverse_ref,
    normal_ref,
    gram_ref,
    maps_a,
    maps_b,
    maps_c,
    maps_d,
    mod_ref,
    score_ref,
    payload_ref,
):
    half = renoise_ref.shape[0]
    level = level_ref[0]
    maps = [part[...].astype(jnp.float32) for part in (maps_a, maps_b, maps_c, maps_d)]
    maps = (maps[0] + maps[1]) + (maps[2] + maps[3])
    width = 2 * CH
    ones = pair_ones()

    def model_matrix(m):
        base = m * CH
        pair = maps[base : base + CH]
        turned = pltpu.roll(pair, CH, 1)
        direct = block_diagonal(pair, turned)
        modulated = block_diagonal(turned, pair)
        matrix = jnp.concatenate([direct, modulated], 1).astype(jnp.bfloat16)
        offset = maps[3 * CH + m : 3 * CH + m + 1]
        return matrix, offset + pltpu.roll(offset, CH, 1)

    def combine(product, inverse, offset):
        return columns(product, 0) + inverse * columns(product, 1) + offset

    noise, other_renoise = sample_latents(noise_ref, other_ref)
    renoise = jnp.concatenate([renoise_ref[...], other_renoise.astype(jnp.float32)], 0)
    matrix, offset = model_matrix(0)
    product = jnp.dot(noise, matrix, preferred_element_type=jnp.float32)
    clean = combine(product, inverse_ref[...], offset)
    noisy = ((1.0 - level) * clean + level * renoise).astype(jnp.bfloat16)
    noisy_wide = noisy.astype(jnp.float32)

    def velocity(m):
        matrix, offset = model_matrix(m)
        matrix = jnp.concatenate([matrix, gram_ref[m]], 1)
        product = jnp.dot(noisy, matrix, preferred_element_type=jnp.float32)
        by_gram = columns(product, 2) + columns(product, 3) + columns(product, 4)
        return combine(product, inverse_deviation(noisy_wide, by_gram, ones), offset)

    real_v = velocity(1)
    fake_v = velocity(2)
    total = jnp.sum(jnp.abs(clean - renoise + real_v))
    gap_scale = level * total * (1.0 / (2 * half * width)) + EPS_GAP
    score = level * (real_v - fake_v) / gap_scale
    score_ref[...] = score[:half]
    tokens = 4 * half * lax.axis_size("dp")
    cotangent = (score * (1.0 / math.sqrt(tokens))).astype(jnp.bfloat16)
    pairs = lax.dot_general(
        normal_ref[...], cotangent, CONTRACT_FIRST, preferred_element_type=jnp.float32
    )
    outer = pairs[:CH] + pltpu.roll(pairs[CH:], CH, 1)
    sums = jnp.sum(cotangent.astype(jnp.float32), axis=0, keepdims=True)
    sums = sums + pltpu.roll(sums, CH, 1)
    rest = jnp.zeros((MAP_ROWS - CH - 1, width), jnp.float32)
    payload_ref[:MAP_ROWS] = jnp.concatenate([outer, sums, rest], 0).astype(jnp.bfloat16)
    payload_ref[MAP_ROWS:] = mod_ref[...]


def token_phase(level, noise, other, renoise, inverse, normal, gram, maps, mod):
    return pl.pallas_call(
        token_kernel,
        out_shape=[
            jax.ShapeDtypeStruct(renoise.shape, jnp.float32),
            jax.ShapeDtypeStruct((MAP_ROWS + mod.shape[0], 2 * CH), jnp.bfloat16),
        ],
        in_specs=[pl.BlockSpec(memory_space=pltpu.SMEM)] + whole_specs(11),
        out_specs=whole_specs(2),
        compiler_params=vmem_params(),
        name="tokens",
    )(level, noise, other, renoise, inverse, normal, gram, *maps, mod)


GRAD_PIECES = 6


def grad_kernel(
    block_a,
    block_b,
    block_c,
    block_d,
    rows_ref,
    unembed_ref,
    score_ref,
    grad_hbm,
    score_hbm,
    buffer,
    sems,
):
    score_copy = pltpu.make_async_copy(score_ref, score_hbm, sems.at[GRAD_PIECES])
    score_copy.start()
    rows = rows_ref.shape[2]
    packs = rows // PACK
    depth = rows // GRAD_PIECES
    blocks = [block[...] for block in (block_a, block_b, block_c, block_d)]
    left = jnp.concatenate([block[:MAP_ROWS, :CH] for block in blocks], 0)
    mods = [block[MAP_ROWS:].astype(jnp.float32) for block in blocks]
    unembed = unembed_ref[0]

    def piece(k):
        part = pl.ds(k * depth, depth)
        return pltpu.make_async_copy(buffer.at[part], grad_hbm.at[part], sems.at[k])

    tiles = []
    for j in range(packs):
        embed_tile = rows_ref[0, :, j * PACK : (j + 1) * PACK]
        column = []
        for mod in mods:
            column += [
                embed_tile * (1.0 + mod[packs + j : packs + j + 1]),
                mod[j : j + 1],
                jnp.zeros((MAP_ROWS - CH - 1, PACK), jnp.float32),
            ]
        tiles.append(jnp.concatenate(column, 0).astype(jnp.bfloat16))
    grad_map = lax.dot_general(
        left, jnp.concatenate(tiles, 1), CONTRACT_FIRST, preferred_element_type=jnp.float32
    ).astype(jnp.bfloat16)
    for k in range(GRAD_PIECES):
        part = slice(k * depth, (k + 1) * depth)
        buffer[part] = lax.dot_general(
            grad_map[:, part], unembed, CONTRACT_FIRST, preferred_element_type=jnp.float32
        )
        piece(k).start()
    for k in range(GRAD_PIECES):
        piece(k).wait()
    score_copy.wait()


def gradient(blocks, rows_part, unembed, score):
    rows = rows_part.shape[2]
    cols = unembed.shape[2]
    return pl.pallas_call(
        grad_kernel,
        out_shape=[
            jax.ShapeDtypeStruct((rows, cols), jnp.float32),
            jax.ShapeDtypeStruct(score.shape, jnp.float32),
        ],
        in_specs=whole_specs(7),
        out_specs=[pl.BlockSpec(memory_space=pl.ANY)] * 2,
        scratch_shapes=[
            pltpu.VMEM((rows, cols), jnp.float32),
            pltpu.SemaphoreType.DMA((GRAD_PIECES + 1,)),
        ],
        compiler_params=vmem_params(),
        name="gradient",
    )(*blocks, rows_part, unembed, score)


def body(
    gen_noise, renoise, gen_step, renoise_step, text_pooled, embed, mod_weight, proj_weight, unembed
):
    mine, latents, through, noise, renoise, unembed, embed = streamed_weights(
        gen_step,
        renoise_step,
        text_pooled,
        gen_noise[0],
        renoise[0],
        mod_weight,
        proj_weight,
        unembed,
        embed,
    )
    f = lax.axis_index("fsdp")
    theirs = swap(mine, "mp", 1)
    own_half = lax.axis_index("mp") % 2 == f
    kept = jnp.where(own_half, mine, theirs)
    sent = jnp.where(own_half, theirs, mine)
    sent, latents = lax.optimization_barrier((sent, latents))
    got = swap(sent, "fsdp", 1)
    other = swap(latents, "fsdp", 1)
    gram, rows_part, direct = embed_products(embed, unembed, proj_weight.shape[1])
    maps, mod = modulated_maps(kept, got, rows_part, through, direct)
    maps = maps.astype(jnp.float32) + swap(maps, "mp", 1).astype(jnp.float32)
    maps = maps.astype(jnp.bfloat16)
    maps = chip_blocks(maps)
    inverse, normal = noise_statistics(noise, other, gram)
    level = renoise_step.astype(jnp.float32) / 1000.0
    score, payload = token_phase(
        level, noise, other, renoise, inverse, normal, gram, maps, mod
    )
    blocks = gather_samples(payload)
    gen_grad, score_gap = gradient(blocks, rows_part, unembed, score)
    return (gen_grad, score_gap[None])


def fits_kernels(mesh):
    return mesh.shape["mp"] == 4 and mesh.shape["fsdp"] == 2 and mesh.shape["dp"] == 4


def solution(mesh):
    return jax.shard_map(
        body if fits_kernels(mesh) else plain_body,
        mesh=mesh,
        in_specs=(
            P("dp", "fsdp", None),
            P("dp", "fsdp", None),
            P("dp"),
            P("dp"),
            P("dp", None),
            P(),
            P(None, None, "fsdp"),
            P(None, "fsdp", "mp"),
            P(None, None, "mp"),
        ),
        out_specs=(P("fsdp", "mp"), P("dp", "fsdp", None)),
        check_vma=False,
    )
```

```python
import math

import jax
import jax.numpy as jnp
from jax import lax
from jax.experimental import pallas as pl
from jax.experimental.pallas import tpu as pltpu
from jax.sharding import PartitionSpec as P

D = 3072
CH = 64
TEMB = 256

GUIDANCE = 3.5
EPS_NORM = 1e-06
EPS_GAP = 1e-05
HI = lax.Precision.HIGHEST


def sinusoid(timesteps):
    half_size = TEMB // 2
    frequency = jnp.exp(-math.log(10000.0) * jnp.arange(half_size, dtype=jnp.float32) / half_size)
    angles = timesteps.astype(jnp.float32)[:, None] * frequency[None, :]
    return jnp.concatenate([jnp.cos(angles), jnp.sin(angles)], axis=1)


def condition(timesteps, pooled):
    joined = jnp.concatenate([sinusoid(timesteps), pooled.astype(jnp.float32)], axis=1)
    return jax.nn.silu(joined).astype(jnp.bfloat16)


def swap(x, axes, mask):
    count = lax.axis_size(axes)
    return lax.ppermute(x, axes, [(i, i ^ mask) for i in range(count)])


def plane_sum(x):
    if lax.axis_size("mp") != 4 or lax.axis_size("fsdp") != 2:
        return lax.psum(x, ("mp", "fsdp"))
    x = x + swap(x, "mp", 1)
    plane = ("mp", "fsdp")
    parts = [swap(x, plane, mask) for mask in (4, 1, 5)]
    return (x + parts[0]) + (parts[1] + parts[2])


def chip_blocks(x):
    pairs = []
    for m in range(4):
        for f in range(2):
            pairs.append((m * 2 + f, (m * 2 + f) ^ (4 if m % 2 == 0 else 1)))
    side = lax.ppermute(x, ("mp", "fsdp"), pairs)
    across = swap(x, ("mp", "fsdp"), 5)
    return [x, side, swap(side, "mp", 1), across]


def gather_samples(x):
    count = lax.axis_size("dp")
    if lax.axis_size("mp") != 4 or count != 4:
        blocks = lax.all_gather(x, "dp")
        return [blocks[i] for i in range(count)]
    pairs = []
    for m in range(4):
        for s in range(4):
            pairs.append((m * 4 + s, m * 4 + (s ^ (1 if m % 2 == 0 else 2))))
    near = lax.ppermute(x, ("mp", "dp"), pairs)
    far = swap(x, "dp", 3)
    return [x, near, swap(near, "mp", 1), far]


def exchange_modulation(local_mod, rows):
    if lax.axis_size("fsdp") == 2:
        f = lax.axis_index("fsdp")
        mine = lax.dynamic_slice_in_dim(local_mod, f * rows, rows, 1)
        theirs = swap(lax.dynamic_slice_in_dim(local_mod, (1 - f) * rows, rows, 1), "fsdp", 1)
        return jnp.where(f == 0, mine, theirs), jnp.where(f == 0, theirs, mine)
    whole = lax.all_gather(local_mod, "fsdp", axis=1, tiled=True)
    start = lax.axis_index("fsdp") * rows
    return (
        lax.dynamic_slice_in_dim(whole[:, :D], start, rows, 1),
        lax.dynamic_slice_in_dim(whole[:, D:], start, rows, 1),
    )


def dot(a, b, precision=HI):
    return jnp.dot(a, b, precision=precision, preferred_element_type=jnp.float32)


def both(x):
    zero = jnp.zeros_like(x)
    return jnp.concatenate(
        [jnp.concatenate([x, zero], 1), jnp.concatenate([zero, x], 1)], 0
    )


def plain_body(
    gen_noise, renoise, gen_step, renoise_step, text_pooled, embed, mod_weight, proj_weight, unembed
):
    rows, cols = proj_weight.shape[1], proj_weight.shape[2]
    f = lax.axis_index("fsdp")
    noise_all = lax.all_gather(gen_noise[0], "fsdp", axis=0, tiled=True)
    renoise_all = lax.all_gather(renoise[0], "fsdp", axis=0, tiled=True)

    blank_text = jnp.zeros_like(text_pooled)
    gen_vec = condition(gen_step, text_pooled)
    real_vec = jnp.concatenate(
        [condition(renoise_step, text_pooled), condition(renoise_step, blank_text)], 0
    )
    teacher_mod = jnp.dot(real_vec, mod_weight[1], preferred_element_type=jnp.float32)
    local_mod = jnp.concatenate(
        [
            jnp.dot(gen_vec, mod_weight[0], preferred_element_type=jnp.float32),
            GUIDANCE * teacher_mod[0:1] + (1.0 - GUIDANCE) * teacher_mod[1:2],
            jnp.dot(real_vec[0:1], mod_weight[2], preferred_element_type=jnp.float32),
        ],
        axis=0,
    )
    shift, scale = exchange_modulation(local_mod, rows)

    centred = embed.astype(jnp.float32)
    centred = centred - jnp.mean(centred, axis=2, keepdims=True)
    gram = [dot(centred[m], centred[m].T) / D for m in range(3)]
    centred_rows = lax.dynamic_slice_in_dim(centred, f * rows, rows, 2)
    embed_cols = lax.dynamic_slice_in_dim(embed, lax.axis_index("mp") * cols, cols, 2)

    pieces = []
    for m in range(3):
        through = lax.dot_general(
            proj_weight[m], unembed[m], (((1,), (1,)), ((), ())), preferred_element_type=jnp.float32
        )
        direct = lax.dot_general(
            embed_cols[m], unembed[m], (((1,), (1,)), ((), ())), preferred_element_type=jnp.float32
        )
        direct = jnp.where(f == 0, direct, 0.0)
        modulated = dot(centred_rows[m] * (1.0 + scale[m : m + 1]), through)
        offset = dot(shift[m : m + 1], through)
        offset = jnp.concatenate([offset, jnp.zeros((7, CH), jnp.float32)], 0)
        pieces.append(
            jnp.concatenate(
                [
                    jnp.concatenate([direct, modulated], 1),
                    jnp.concatenate([offset, jnp.zeros_like(offset)], 1),
                ],
                0,
            )
        )
    maps = plane_sum(jnp.concatenate(pieces, 0)).reshape(3, CH + 8, 2 * CH)
    direct = [both(maps[m, :CH, :CH]) for m in range(3)]
    modulated = [both(maps[m, :CH, CH:]) for m in range(3)]
    offset = [jnp.concatenate([maps[m, CH : CH + 1, :CH]] * 2, 1) for m in range(3)]

    ones = both(jnp.ones((CH, CH), jnp.float32))

    def normalized(u, m):
        spread = dot(dot(u, both(gram[m])) * u, ones)
        return u * lax.rsqrt(jnp.maximum(spread, 0.0) + EPS_NORM)

    def model(u, u_norm, m):
        return dot(u, direct[m]) + dot(u_norm, modulated[m]) + offset[m]

    noise = noise_all.astype(jnp.bfloat16).astype(jnp.float32)
    noise_norm = normalized(noise, 0)
    clean = model(noise, noise_norm, 0)
    level = renoise_step[0].astype(jnp.float32) / 1000.0
    noisy = (1.0 - level) * clean + level * renoise_all
    noisy = noisy.astype(jnp.bfloat16).astype(jnp.float32)
    real_v = model(noisy, normalized(noisy, 1), 1)
    fake_v = model(noisy, normalized(noisy, 2), 2)
    total = jnp.sum(jnp.abs(clean - renoise_all + real_v))
    gap_scale = level * total / (noise_all.shape[0] * 2 * CH) + EPS_GAP
    score = level * (real_v - fake_v) / gap_scale
    local_rows = gen_noise.shape[1]
    score_gap = lax.dynamic_slice_in_dim(score, f * local_rows, local_rows, 0)

    all_tokens = noise_all.shape[0] * 2 * lax.axis_size("dp")
    cotangent = (score / math.sqrt(all_tokens)).astype(jnp.bfloat16).astype(jnp.float32)
    pairs = dot(noise_norm.T, cotangent)
    outer = pairs[:CH, :CH] + pairs[CH:, CH:]
    sums = jnp.sum(cotangent, axis=0)
    sums = sums[:CH] + sums[CH:]
    payload = jnp.concatenate(
        [
            jnp.pad(outer, ((0, 0), (0, CH))),
            jnp.pad(sums[None], ((0, 7), (0, CH))),
            jnp.concatenate([shift[0], scale[0]]).reshape(-1, 2 * CH),
        ],
        0,
    )
    blocks = gather_samples(payload)
    grad_map = jnp.zeros((CH, rows), jnp.float32)
    for block in blocks:
        block_mod = block[CH + 8 :].reshape(2, rows)
        grad_map += dot(block[:CH, :CH].T, centred_rows[0]) * (1.0 + block_mod[1:2])
        grad_map += block[CH, :CH][:, None] * block_mod[0:1]
    gen_grad = lax.dot_general(
        grad_map.astype(jnp.bfloat16),
        unembed[0],
        (((0,), (0,)), ((), ())),
        preferred_element_type=jnp.float32,
    )
    return (gen_grad, score_gap[None])


def vmem_params():
    return pltpu.CompilerParams(vmem_limit_bytes=48 * 1024 * 1024)


def whole_specs(count):
    return [pl.BlockSpec(memory_space=pltpu.VMEM)] * count


def split_two(x):
    high = x.astype(jnp.bfloat16)
    return high, (x - high.astype(jnp.float32)).astype(jnp.bfloat16)


def split_three(x):
    high = x.astype(jnp.bfloat16)
    rest = x - high.astype(jnp.float32)
    middle = rest.astype(jnp.bfloat16)
    return high, middle, (rest - middle.astype(jnp.float32)).astype(jnp.bfloat16)


def lane_index(shape):
    return lax.broadcasted_iota(jnp.int32, shape, len(shape) - 1)


def block_diagonal(left_copy, right_copy):
    lanes = lane_index(left_copy.shape)
    top = jnp.where(lanes < CH, left_copy, 0.0)
    bottom = jnp.where(lanes >= CH, right_copy, 0.0)
    return jnp.concatenate([top, bottom], 0)


MOD_PIECES = 4
PROJ_PIECES = 3
IN_FLIGHT = 12
LATENTS_AFTER = 8
PACK = 128
CONTRACT_LAST = (((1,), (1,)), ((), ()))
CONTRACT_FIRST = (((0,), (0,)), ((), ()))


def stream_kernel(
    gen_step_ref,
    renoise_step_ref,
    text_hbm,
    noise_hbm,
    renoise_hbm,
    mod_hbm,
    proj_hbm,
    unembed_hbm,
    embed_hbm,
    mod_ref,
    latents_ref,
    through_ref,
    noise_ref,
    renoise_ref,
    unembed_ref,
    embed_ref,
    text_ref,
    mod_buffer,
    proj_buffer,
    mod_sems,
    proj_sems,
    small_sems,
):
    width = mod_buffer.shape[2]
    rows, cols = proj_buffer.shape[1:]
    mod_depth = mod_buffer.shape[1] // MOD_PIECES
    proj_depth = rows // PROJ_PIECES
    mod_start = pl.multiple_of((lax.axis_index("mp") % 2) * width, 128)

    def mod_piece(m, k):
        part = pl.ds(k * mod_depth, mod_depth)
        return pltpu.make_async_copy(
            mod_hbm.at[m, part, pl.ds(mod_start, width)], mod_buffer.at[m, part], mod_sems.at[m, k]
        )

    def proj_piece(m, k):
        part = pl.ds(k * proj_depth, proj_depth)
        return pltpu.make_async_copy(
            proj_hbm.at[m, part], proj_buffer.at[m, part], proj_sems.at[m, k]
        )

    small = [
        pltpu.make_async_copy(source, target, small_sems.at[k])
        for k, (source, target) in enumerate(
            (
                (text_hbm, text_ref),
                (unembed_hbm, unembed_ref),
                (noise_hbm, noise_ref),
                (renoise_hbm, renoise_ref),
                (embed_hbm, embed_ref),
            )
        )
    ]
    order = []
    for m in range(3):
        order += [proj_piece(m, k) for k in range(PROJ_PIECES)]
        order += [mod_piece(m, k) for k in range(MOD_PIECES)]
    order = small[:2] + order[:LATENTS_AFTER] + small[2:4] + order[LATENTS_AFTER:] + small[4:]
    for copy in order[:IN_FLIGHT]:
        copy.start()

    def take(position):
        order[position].wait()
        if position + IN_FLIGHT < len(order):
            order[position + IN_FLIGHT].start()

    take(0)
    half_size = TEMB // 2
    place = lane_index((8, half_size)).astype(jnp.float32)
    frequency = jnp.exp(place * (-math.log(10000.0) / half_size))
    level = lax.broadcasted_iota(jnp.int32, (8, half_size), 0)
    steps = jnp.where(level == 0, gen_step_ref[0], renoise_step_ref[0]).astype(jnp.float32)
    angles = steps * frequency
    text = jnp.broadcast_to(text_ref[...].astype(jnp.float32), (8, text_ref.shape[1]))
    text = jnp.where(lax.broadcasted_iota(jnp.int32, text.shape, 0) < 2, text, 0.0)
    joined = jnp.concatenate([jnp.cos(angles), jnp.sin(angles), text], 1)
    vectors = (joined / (1.0 + jnp.exp(-joined))).astype(jnp.bfloat16)
    packs = width // PACK
    mod_ref[...] = jnp.zeros_like(mod_ref)
    take(1)
    place = 2
    for m in range(3):
        total = jnp.zeros((8, width), jnp.float32)
        for k in range(PROJ_PIECES + MOD_PIECES):
            if place == LATENTS_AFTER + 2:
                take(place)
                take(place + 1)
                half = noise_ref.shape[0]
                latents_ref[:half] = noise_ref[...].astype(jnp.bfloat16)
                latents_ref[half:] = renoise_ref[...].astype(jnp.bfloat16)
                place += 2
            take(place)
            place += 1
            if k < PROJ_PIECES:
                part = slice(k * proj_depth, (k + 1) * proj_depth)
                through_ref[m, :, part] = lax.dot_general(
                    unembed_ref[m],
                    proj_buffer[m, part],
                    CONTRACT_LAST,
                    preferred_element_type=jnp.float32,
                ).astype(jnp.bfloat16)
            else:
                part = slice((k - PROJ_PIECES) * mod_depth, (k - PROJ_PIECES + 1) * mod_depth)
                total += jnp.dot(
                    vectors[:, part], mod_buffer[m, part], preferred_element_type=jnp.float32
                )
        if m == 0:
            line = total[0:1]
        elif m == 1:
            line = GUIDANCE * total[1:2] + (1.0 - GUIDANCE) * total[2:3]
        else:
            line = total[1:2]
        for j in range(packs):
            mod_ref[m * packs + j : m * packs + j + 1] = line[:, j * PACK : (j + 1) * PACK]
    take(len(order) - 1)


def streamed_weights(
    gen_step, renoise_step, text, noise, renoise, mod_weight, proj_weight, unembed, embed
):
    depth, width = mod_weight.shape[1], mod_weight.shape[2] // 2
    rows, cols = proj_weight.shape[1:]
    pack_rows = -(-3 * width // PACK // 8) * 8
    return pl.pallas_call(
        stream_kernel,
        out_shape=[
            jax.ShapeDtypeStruct((pack_rows, PACK), jnp.float32),
            jax.ShapeDtypeStruct((2 * noise.shape[0], noise.shape[1]), jnp.bfloat16),
            jax.ShapeDtypeStruct((3, CH, rows), jnp.bfloat16),
            jax.ShapeDtypeStruct(noise.shape, noise.dtype),
            jax.ShapeDtypeStruct(renoise.shape, renoise.dtype),
            jax.ShapeDtypeStruct(unembed.shape, unembed.dtype),
            jax.ShapeDtypeStruct(embed.shape, embed.dtype),
        ],
        in_specs=[pl.BlockSpec(memory_space=pltpu.SMEM)] * 2
        + [pl.BlockSpec(memory_space=pltpu.HBM)] * 7,
        out_specs=whole_specs(7),
        scratch_shapes=[
            pltpu.VMEM(text.shape, text.dtype),
            pltpu.VMEM((3, depth, width), jnp.bfloat16),
            pltpu.VMEM((3, rows, cols), jnp.bfloat16),
            pltpu.SemaphoreType.DMA((3, MOD_PIECES)),
            pltpu.SemaphoreType.DMA((3, PROJ_PIECES)),
            pltpu.SemaphoreType.DMA((5,)),
        ],
        compiler_params=vmem_params(),
        name="stream_weights",
    )(
        gen_step,
        renoise_step,
        *(
            pltpu.with_memory_space_constraint(x, pltpu.HBM)
            for x in (text, noise, renoise, mod_weight, proj_weight, unembed, embed)
        ),
    )


def embed_kernel(embed_ref, unembed_ref, gram_ref, rows_ref, direct_ref):
    rows, cols = rows_ref.shape[2], unembed_ref.shape[2]
    f = lax.axis_index("fsdp")
    row_start = pl.multiple_of(f * rows, 128)
    col_start = pl.multiple_of(lax.axis_index("mp") * cols, 128)
    nothing = jnp.zeros((CH, cols), jnp.bfloat16)
    for m in range(3):
        whole = embed_ref[m].astype(jnp.float32)
        average = jnp.sum(whole, axis=1, keepdims=True) * (1.0 / D)
        rows_ref[m] = embed_ref[m, :, pl.ds(row_start, rows)].astype(jnp.float32) - average
        direct = lax.dot_general(
            embed_ref[m, :, pl.ds(col_start, cols)],
            jnp.concatenate([unembed_ref[m], nothing], 0),
            CONTRACT_LAST,
            preferred_element_type=jnp.float32,
        )
        direct_ref[m] = jnp.where(f == 0, direct, 0.0)
        pair = jnp.concatenate(split_two(whole - average), 0)
        product = lax.dot_general(pair, pair, CONTRACT_LAST, preferred_element_type=jnp.float32)
        product = product[:CH] + product[CH:]
        gram = (product + pltpu.roll(product, CH, 1)) * (1.0 / D)
        gram_ref[m] = jnp.concatenate(split_three(block_diagonal(gram, gram)), 1)


def embed_products(embed, unembed, rows):
    return pl.pallas_call(
        embed_kernel,
        out_shape=[
            jax.ShapeDtypeStruct((3, 2 * CH, 6 * CH), jnp.bfloat16),
            jax.ShapeDtypeStruct((3, CH, rows), jnp.float32),
            jax.ShapeDtypeStruct((3, CH, 2 * CH), jnp.float32),
        ],
        in_specs=whole_specs(2),
        out_specs=whole_specs(3),
        compiler_params=vmem_params(),
        cost_estimate=pl.CostEstimate(
            flops=6 * 128 * 128 * D, bytes_accessed=6 * CH * D, transcendentals=0
        ),
        name="embed_products",
    )(embed, unembed)


def pair_ones():
    shape = (2 * CH, 2 * CH)
    lanes = lane_index(shape)
    subs = lax.broadcasted_iota(jnp.int32, shape, 0)
    ones = jnp.where((lanes < CH) == (subs < CH), 1.0, 0.0).astype(jnp.bfloat16)
    return jnp.concatenate([ones, ones], 0)


def inverse_deviation(u, by_gram, ones):
    squares = jnp.concatenate(split_two(by_gram * u), 1)
    spread = jnp.dot(squares, ones, preferred_element_type=jnp.float32)
    return lax.rsqrt(jnp.maximum(spread, 0.0) + EPS_NORM)


def columns(product, i):
    return product[:, i * 2 * CH : (i + 1) * 2 * CH]


def sample_latents(noise_ref, other_ref):
    half = noise_ref.shape[0]
    noise = jnp.concatenate([noise_ref[...].astype(jnp.bfloat16), other_ref[:half]], 0)
    return noise, other_ref[half:]


def noise_kernel(noise_ref, other_ref, gram_ref, inverse_ref, normal_ref):
    noise, _ = sample_latents(noise_ref, other_ref)
    product = jnp.dot(noise, gram_ref[0], preferred_element_type=jnp.float32)
    noise = noise.astype(jnp.float32)
    by_gram = columns(product, 0) + columns(product, 1) + columns(product, 2)
    inverse = inverse_deviation(noise, by_gram, pair_ones())
    inverse_ref[...] = inverse
    normal_ref[...] = (noise * inverse).astype(jnp.bfloat16)


def noise_statistics(noise, other, gram):
    shape = (2 * noise.shape[0], noise.shape[1])
    return pl.pallas_call(
        noise_kernel,
        out_shape=[
            jax.ShapeDtypeStruct(shape, jnp.float32),
            jax.ShapeDtypeStruct(shape, jnp.bfloat16),
        ],
        in_specs=whole_specs(3),
        out_specs=whole_specs(2),
        compiler_params=vmem_params(),
        name="noise_statistics",
    )(noise, other, gram)


def maps_kernel(kept_ref, got_ref, rows_ref, through_ref, direct_ref, maps_ref, mod_ref):
    rows = rows_ref.shape[2]
    packs = rows // PACK
    f = lax.axis_index("fsdp")
    kept, got = kept_ref[...], got_ref[...]
    shift = jnp.where(f == 0, kept, got)
    scale = jnp.where(f == 0, got, kept)
    offsets = []
    for m in range(3):
        pieces = []
        for j in range(packs):
            line = slice(m * packs + j, m * packs + j + 1)
            pieces.append(
                jnp.concatenate(
                    [
                        rows_ref[m, :, j * PACK : (j + 1) * PACK] * (1.0 + scale[line]),
                        shift[line],
                        jnp.zeros((7, PACK), jnp.float32),
                    ],
                    0,
                )
            )
        left = jnp.concatenate(pieces, 1).astype(jnp.bfloat16)
        through = jnp.concatenate([jnp.zeros((CH, rows), jnp.bfloat16), through_ref[m]], 0)
        product = lax.dot_general(
            left, through, CONTRACT_LAST, preferred_element_type=jnp.float32
        )
        maps_ref[m * CH : (m + 1) * CH] = (product[:CH] + direct_ref[m]).astype(jnp.bfloat16)
        offsets.append(product[CH : CH + 1])
    maps_ref[3 * CH :] = jnp.concatenate(
        offsets + [jnp.zeros((5, PACK), jnp.float32)], 0
    ).astype(jnp.bfloat16)
    rest = jnp.zeros((mod_ref.shape[0] - 2 * packs, PACK), jnp.float32)
    mod_ref[...] = jnp.concatenate([shift[:packs], scale[:packs], rest], 0).astype(jnp.bfloat16)


def modulated_maps(kept, got, rows_part, through, direct):
    packs = rows_part.shape[2] // PACK
    return pl.pallas_call(
        maps_kernel,
        out_shape=[
            jax.ShapeDtypeStruct((3 * CH + 8, 2 * CH), jnp.bfloat16),
            jax.ShapeDtypeStruct((-(-2 * packs // 16) * 16, PACK), jnp.bfloat16),
        ],
        in_specs=whole_specs(5),
        out_specs=whole_specs(2),
        compiler_params=vmem_params(),
        name="modulated_maps",
    )(kept, got, rows_part, through, direct)


MAP_ROWS = CH + 16


def token_kernel(
    level_ref,
    noise_ref,
    other_ref,
    renoise_ref,
    inverse_ref,
    normal_ref,
    gram_ref,
    maps_a,
    maps_b,
    maps_c,
    maps_d,
    mod_ref,
    score_ref,
    payload_ref,
):
    half = renoise_ref.shape[0]
    level = level_ref[0]
    maps = [part[...].astype(jnp.float32) for part in (maps_a, maps_b, maps_c, maps_d)]
    maps = (maps[0] + maps[1]) + (maps[2] + maps[3])
    width = 2 * CH
    ones = pair_ones()

    def model_matrix(m):
        base = m * CH
        pair = maps[base : base + CH]
        turned = pltpu.roll(pair, CH, 1)
        direct = block_diagonal(pair, turned)
        modulated = block_diagonal(turned, pair)
        matrix = jnp.concatenate([direct, modulated], 1).astype(jnp.bfloat16)
        offset = maps[3 * CH + m : 3 * CH + m + 1]
        return matrix, offset + pltpu.roll(offset, CH, 1)

    def combine(product, inverse, offset):
        return columns(product, 0) + inverse * columns(product, 1) + offset

    noise, other_renoise = sample_latents(noise_ref, other_ref)
    renoise = jnp.concatenate([renoise_ref[...], other_renoise.astype(jnp.float32)], 0)
    matrix, offset = model_matrix(0)
    product = jnp.dot(noise, matrix, preferred_element_type=jnp.float32)
    clean = combine(product, inverse_ref[...], offset)
    noisy = ((1.0 - level) * clean + level * renoise).astype(jnp.bfloat16)
    noisy_wide = noisy.astype(jnp.float32)

    def velocity(m):
        matrix, offset = model_matrix(m)
        matrix = jnp.concatenate([matrix, gram_ref[m]], 1)
        product = jnp.dot(noisy, matrix, preferred_element_type=jnp.float32)
        by_gram = columns(product, 2) + columns(product, 3) + columns(product, 4)
        return combine(product, inverse_deviation(noisy_wide, by_gram, ones), offset)

    real_v = velocity(1)
    fake_v = velocity(2)
    total = jnp.sum(jnp.abs(clean - renoise + real_v))
    gap_scale = level * total * (1.0 / (2 * half * width)) + EPS_GAP
    score = level * (real_v - fake_v) / gap_scale
    score_ref[...] = score[:half]
    tokens = 4 * half * lax.axis_size("dp")
    cotangent = (score * (1.0 / math.sqrt(tokens))).astype(jnp.bfloat16)
    pairs = lax.dot_general(
        normal_ref[...], cotangent, CONTRACT_FIRST, preferred_element_type=jnp.float32
    )
    outer = pairs[:CH] + pltpu.roll(pairs[CH:], CH, 1)
    sums = jnp.sum(cotangent.astype(jnp.float32), axis=0, keepdims=True)
    sums = sums + pltpu.roll(sums, CH, 1)
    rest = jnp.zeros((MAP_ROWS - CH - 1, width), jnp.float32)
    payload_ref[:MAP_ROWS] = jnp.concatenate([outer, sums, rest], 0).astype(jnp.bfloat16)
    payload_ref[MAP_ROWS:] = mod_ref[...]


def token_phase(level, noise, other, renoise, inverse, normal, gram, maps, mod):
    return pl.pallas_call(
        token_kernel,
        out_shape=[
            jax.ShapeDtypeStruct(renoise.shape, jnp.float32),
            jax.ShapeDtypeStruct((MAP_ROWS + mod.shape[0], 2 * CH), jnp.bfloat16),
        ],
        in_specs=[pl.BlockSpec(memory_space=pltpu.SMEM)] + whole_specs(11),
        out_specs=whole_specs(2),
        compiler_params=vmem_params(),
        name="tokens",
    )(level, noise, other, renoise, inverse, normal, gram, *maps, mod)


GRAD_PIECES = 6


def grad_kernel(
    block_a,
    block_b,
    block_c,
    block_d,
    rows_ref,
    unembed_ref,
    score_ref,
    grad_hbm,
    score_hbm,
    buffer,
    sems,
):
    score_copy = pltpu.make_async_copy(score_ref, score_hbm, sems.at[GRAD_PIECES])
    score_copy.start()
    rows = rows_ref.shape[2]
    packs = rows // PACK
    depth = rows // GRAD_PIECES
    blocks = [block[...] for block in (block_a, block_b, block_c, block_d)]
    left = jnp.concatenate([block[:MAP_ROWS, :CH] for block in blocks], 0)
    mods = [block[MAP_ROWS:].astype(jnp.float32) for block in blocks]
    unembed = unembed_ref[0]

    def piece(k):
        part = pl.ds(k * depth, depth)
        return pltpu.make_async_copy(buffer.at[part], grad_hbm.at[part], sems.at[k])

    tiles = []
    for j in range(packs):
        embed_tile = rows_ref[0, :, j * PACK : (j + 1) * PACK]
        column = []
        for mod in mods:
            column += [
                embed_tile * (1.0 + mod[packs + j : packs + j + 1]),
                mod[j : j + 1],
                jnp.zeros((MAP_ROWS - CH - 1, PACK), jnp.float32),
            ]
        tiles.append(jnp.concatenate(column, 0).astype(jnp.bfloat16))
    grad_map = lax.dot_general(
        left, jnp.concatenate(tiles, 1), CONTRACT_FIRST, preferred_element_type=jnp.float32
    ).astype(jnp.bfloat16)
    for k in range(GRAD_PIECES):
        part = slice(k * depth, (k + 1) * depth)
        buffer[part] = lax.dot_general(
            grad_map[:, part], unembed, CONTRACT_FIRST, preferred_element_type=jnp.float32
        )
        piece(k).start()
    for k in range(GRAD_PIECES):
        piece(k).wait()
    score_copy.wait()


def gradient(blocks, rows_part, unembed, score):
    rows = rows_part.shape[2]
    cols = unembed.shape[2]
    return pl.pallas_call(
        grad_kernel,
        out_shape=[
            jax.ShapeDtypeStruct((rows, cols), jnp.float32),
            jax.ShapeDtypeStruct(score.shape, jnp.float32),
        ],
        in_specs=whole_specs(7),
        out_specs=[pl.BlockSpec(memory_space=pl.ANY)] * 2,
        scratch_shapes=[
            pltpu.VMEM((rows, cols), jnp.float32),
            pltpu.SemaphoreType.DMA((GRAD_PIECES + 1,)),
        ],
        compiler_params=vmem_params(),
        name="gradient",
    )(*blocks, rows_part, unembed, score)


def body(
    gen_noise, renoise, gen_step, renoise_step, text_pooled, embed, mod_weight, proj_weight, unembed
):
    mine, latents, through, noise, renoise, unembed, embed = streamed_weights(
        gen_step,
        renoise_step,
        text_pooled,
        gen_noise[0],
        renoise[0],
        mod_weight,
        proj_weight,
        unembed,
        embed,
    )
    f = lax.axis_index("fsdp")
    theirs = swap(mine, "mp", 1)
    own_half = lax.axis_index("mp") % 2 == f
    kept = jnp.where(own_half, mine, theirs)
    straight = swap(mine, "fsdp", 1)
    cross = swap(mine, ("mp", "fsdp"), 3)
    got = jnp.where(own_half, straight, cross)
    got, latents = lax.optimization_barrier((got, latents))
    other = swap(latents, "fsdp", 1)
    gram, rows_part, direct = embed_products(embed, unembed, proj_weight.shape[1])
    maps, mod = modulated_maps(kept, got, rows_part, through, direct)
    maps = maps.astype(jnp.float32) + swap(maps, "mp", 1).astype(jnp.float32)
    maps = maps.astype(jnp.bfloat16)
    maps = chip_blocks(maps)
    inverse, normal = noise_statistics(noise, other, gram)
    level = renoise_step.astype(jnp.float32) / 1000.0
    score, payload = token_phase(
        level, noise, other, renoise, inverse, normal, gram, maps, mod
    )
    blocks = gather_samples(payload)
    gen_grad, score_gap = gradient(blocks, rows_part, unembed, score)
    return (gen_grad, score_gap[None])


def fits_kernels(mesh):
    return mesh.shape["mp"] == 4 and mesh.shape["fsdp"] == 2 and mesh.shape["dp"] == 4


def solution(mesh):
    return jax.shard_map(
        body if fits_kernels(mesh) else plain_body,
        mesh=mesh,
        in_specs=(
            P("dp", "fsdp", None),
            P("dp", "fsdp", None),
            P("dp"),
            P("dp"),
            P("dp", None),
            P(),
            P(None, None, "fsdp"),
            P(None, "fsdp", "mp"),
            P(None, None, "mp"),
        ),
        out_specs=(P("fsdp", "mp"), P("dp", "fsdp", None)),
        check_vma=False,
    )
```

```python
import math

import jax
import jax.numpy as jnp
from jax import lax
from jax.experimental import pallas as pl
from jax.experimental.pallas import tpu as pltpu
from jax.sharding import PartitionSpec as P

D = 3072
CH = 64
TEMB = 256

GUIDANCE = 3.5
EPS_NORM = 1e-06
EPS_GAP = 1e-05
HI = lax.Precision.HIGHEST


def sinusoid(timesteps):
    half_size = TEMB // 2
    frequency = jnp.exp(-math.log(10000.0) * jnp.arange(half_size, dtype=jnp.float32) / half_size)
    angles = timesteps.astype(jnp.float32)[:, None] * frequency[None, :]
    return jnp.concatenate([jnp.cos(angles), jnp.sin(angles)], axis=1)


def condition(timesteps, pooled):
    joined = jnp.concatenate([sinusoid(timesteps), pooled.astype(jnp.float32)], axis=1)
    return jax.nn.silu(joined).astype(jnp.bfloat16)


def swap(x, axes, mask):
    count = lax.axis_size(axes)
    return lax.ppermute(x, axes, [(i, i ^ mask) for i in range(count)])


def plane_sum(x):
    if lax.axis_size("mp") != 4 or lax.axis_size("fsdp") != 2:
        return lax.psum(x, ("mp", "fsdp"))
    x = x + swap(x, "mp", 1)
    plane = ("mp", "fsdp")
    parts = [swap(x, plane, mask) for mask in (4, 1, 5)]
    return (x + parts[0]) + (parts[1] + parts[2])


def chip_blocks(x):
    pairs = []
    for m in range(4):
        for f in range(2):
            pairs.append((m * 2 + f, (m * 2 + f) ^ (4 if m % 2 == 0 else 1)))
    side = lax.ppermute(x, ("mp", "fsdp"), pairs)
    across = swap(x, ("mp", "fsdp"), 5)
    return [x, side, swap(side, "mp", 1), across]


def gather_samples(x):
    count = lax.axis_size("dp")
    if lax.axis_size("mp") != 4 or count != 4:
        blocks = lax.all_gather(x, "dp")
        return [blocks[i] for i in range(count)]
    pairs = []
    for m in range(4):
        for s in range(4):
            pairs.append((m * 4 + s, m * 4 + (s ^ (1 if m % 2 == 0 else 2))))
    near = lax.ppermute(x, ("mp", "dp"), pairs)
    far = swap(x, "dp", 3)
    return [x, near, swap(near, "mp", 1), far]


def exchange_modulation(local_mod, rows):
    if lax.axis_size("fsdp") == 2:
        f = lax.axis_index("fsdp")
        mine = lax.dynamic_slice_in_dim(local_mod, f * rows, rows, 1)
        theirs = swap(lax.dynamic_slice_in_dim(local_mod, (1 - f) * rows, rows, 1), "fsdp", 1)
        return jnp.where(f == 0, mine, theirs), jnp.where(f == 0, theirs, mine)
    whole = lax.all_gather(local_mod, "fsdp", axis=1, tiled=True)
    start = lax.axis_index("fsdp") * rows
    return (
        lax.dynamic_slice_in_dim(whole[:, :D], start, rows, 1),
        lax.dynamic_slice_in_dim(whole[:, D:], start, rows, 1),
    )


def dot(a, b, precision=HI):
    return jnp.dot(a, b, precision=precision, preferred_element_type=jnp.float32)


def both(x):
    zero = jnp.zeros_like(x)
    return jnp.concatenate(
        [jnp.concatenate([x, zero], 1), jnp.concatenate([zero, x], 1)], 0
    )


def plain_body(
    gen_noise, renoise, gen_step, renoise_step, text_pooled, embed, mod_weight, proj_weight, unembed
):
    rows, cols = proj_weight.shape[1], proj_weight.shape[2]
    f = lax.axis_index("fsdp")
    noise_all = lax.all_gather(gen_noise[0], "fsdp", axis=0, tiled=True)
    renoise_all = lax.all_gather(renoise[0], "fsdp", axis=0, tiled=True)

    blank_text = jnp.zeros_like(text_pooled)
    gen_vec = condition(gen_step, text_pooled)
    real_vec = jnp.concatenate(
        [condition(renoise_step, text_pooled), condition(renoise_step, blank_text)], 0
    )
    teacher_mod = jnp.dot(real_vec, mod_weight[1], preferred_element_type=jnp.float32)
    local_mod = jnp.concatenate(
        [
            jnp.dot(gen_vec, mod_weight[0], preferred_element_type=jnp.float32),
            GUIDANCE * teacher_mod[0:1] + (1.0 - GUIDANCE) * teacher_mod[1:2],
            jnp.dot(real_vec[0:1], mod_weight[2], preferred_element_type=jnp.float32),
        ],
        axis=0,
    )
    shift, scale = exchange_modulation(local_mod, rows)

    centred = embed.astype(jnp.float32)
    centred = centred - jnp.mean(centred, axis=2, keepdims=True)
    gram = [dot(centred[m], centred[m].T) / D for m in range(3)]
    centred_rows = lax.dynamic_slice_in_dim(centred, f * rows, rows, 2)
    embed_cols = lax.dynamic_slice_in_dim(embed, lax.axis_index("mp") * cols, cols, 2)

    pieces = []
    for m in range(3):
        through = lax.dot_general(
            proj_weight[m], unembed[m], (((1,), (1,)), ((), ())), preferred_element_type=jnp.float32
        )
        direct = lax.dot_general(
            embed_cols[m], unembed[m], (((1,), (1,)), ((), ())), preferred_element_type=jnp.float32
        )
        direct = jnp.where(f == 0, direct, 0.0)
        modulated = dot(centred_rows[m] * (1.0 + scale[m : m + 1]), through)
        offset = dot(shift[m : m + 1], through)
        offset = jnp.concatenate([offset, jnp.zeros((7, CH), jnp.float32)], 0)
        pieces.append(
            jnp.concatenate(
                [
                    jnp.concatenate([direct, modulated], 1),
                    jnp.concatenate([offset, jnp.zeros_like(offset)], 1),
                ],
                0,
            )
        )
    maps = plane_sum(jnp.concatenate(pieces, 0)).reshape(3, CH + 8, 2 * CH)
    direct = [both(maps[m, :CH, :CH]) for m in range(3)]
    modulated = [both(maps[m, :CH, CH:]) for m in range(3)]
    offset = [jnp.concatenate([maps[m, CH : CH + 1, :CH]] * 2, 1) for m in range(3)]

    ones = both(jnp.ones((CH, CH), jnp.float32))

    def normalized(u, m):
        spread = dot(dot(u, both(gram[m])) * u, ones)
        return u * lax.rsqrt(jnp.maximum(spread, 0.0) + EPS_NORM)

    def model(u, u_norm, m):
        return dot(u, direct[m]) + dot(u_norm, modulated[m]) + offset[m]

    noise = noise_all.astype(jnp.bfloat16).astype(jnp.float32)
    noise_norm = normalized(noise, 0)
    clean = model(noise, noise_norm, 0)
    level = renoise_step[0].astype(jnp.float32) / 1000.0
    noisy = (1.0 - level) * clean + level * renoise_all
    noisy = noisy.astype(jnp.bfloat16).astype(jnp.float32)
    real_v = model(noisy, normalized(noisy, 1), 1)
    fake_v = model(noisy, normalized(noisy, 2), 2)
    total = jnp.sum(jnp.abs(clean - renoise_all + real_v))
    gap_scale = level * total / (noise_all.shape[0] * 2 * CH) + EPS_GAP
    score = level * (real_v - fake_v) / gap_scale
    local_rows = gen_noise.shape[1]
    score_gap = lax.dynamic_slice_in_dim(score, f * local_rows, local_rows, 0)

    all_tokens = noise_all.shape[0] * 2 * lax.axis_size("dp")
    cotangent = (score / math.sqrt(all_tokens)).astype(jnp.bfloat16).astype(jnp.float32)
    pairs = dot(noise_norm.T, cotangent)
    outer = pairs[:CH, :CH] + pairs[CH:, CH:]
    sums = jnp.sum(cotangent, axis=0)
    sums = sums[:CH] + sums[CH:]
    payload = jnp.concatenate(
        [
            jnp.pad(outer, ((0, 0), (0, CH))),
            jnp.pad(sums[None], ((0, 7), (0, CH))),
            jnp.concatenate([shift[0], scale[0]]).reshape(-1, 2 * CH),
        ],
        0,
    )
    blocks = gather_samples(payload)
    grad_map = jnp.zeros((CH, rows), jnp.float32)
    for block in blocks:
        block_mod = block[CH + 8 :].reshape(2, rows)
        grad_map += dot(block[:CH, :CH].T, centred_rows[0]) * (1.0 + block_mod[1:2])
        grad_map += block[CH, :CH][:, None] * block_mod[0:1]
    gen_grad = lax.dot_general(
        grad_map.astype(jnp.bfloat16),
        unembed[0],
        (((0,), (0,)), ((), ())),
        preferred_element_type=jnp.float32,
    )
    return (gen_grad, score_gap[None])


def vmem_params():
    return pltpu.CompilerParams(vmem_limit_bytes=48 * 1024 * 1024)


def whole_specs(count):
    return [pl.BlockSpec(memory_space=pltpu.VMEM)] * count


def split_two(x):
    high = x.astype(jnp.bfloat16)
    return high, (x - high.astype(jnp.float32)).astype(jnp.bfloat16)


def split_three(x):
    high = x.astype(jnp.bfloat16)
    rest = x - high.astype(jnp.float32)
    middle = rest.astype(jnp.bfloat16)
    return high, middle, (rest - middle.astype(jnp.float32)).astype(jnp.bfloat16)


def lane_index(shape):
    return lax.broadcasted_iota(jnp.int32, shape, len(shape) - 1)


def block_diagonal(left_copy, right_copy):
    lanes = lane_index(left_copy.shape)
    top = jnp.where(lanes < CH, left_copy, 0.0)
    bottom = jnp.where(lanes >= CH, right_copy, 0.0)
    return jnp.concatenate([top, bottom], 0)


MOD_PIECES = 4
PROJ_PIECES = 3
IN_FLIGHT = 12
LATENTS_AFTER = 4
PACK = 128
CONTRACT_LAST = (((1,), (1,)), ((), ()))
CONTRACT_FIRST = (((0,), (0,)), ((), ()))


def stream_kernel(
    gen_step_ref,
    renoise_step_ref,
    text_hbm,
    noise_hbm,
    renoise_hbm,
    mod_hbm,
    proj_hbm,
    unembed_hbm,
    embed_hbm,
    mod_ref,
    latents_ref,
    through_ref,
    noise_ref,
    renoise_ref,
    unembed_ref,
    embed_ref,
    text_ref,
    mod_buffer,
    proj_buffer,
    mod_sems,
    proj_sems,
    small_sems,
):
    width = mod_buffer.shape[2]
    rows, cols = proj_buffer.shape[1:]
    mod_depth = mod_buffer.shape[1] // MOD_PIECES
    proj_depth = rows // PROJ_PIECES
    mod_start = pl.multiple_of((lax.axis_index("mp") % 2) * width, 128)

    def mod_piece(m, k):
        part = pl.ds(k * mod_depth, mod_depth)
        return pltpu.make_async_copy(
            mod_hbm.at[m, part, pl.ds(mod_start, width)], mod_buffer.at[m, part], mod_sems.at[m, k]
        )

    def proj_piece(m, k):
        part = pl.ds(k * proj_depth, proj_depth)
        return pltpu.make_async_copy(
            proj_hbm.at[m, part], proj_buffer.at[m, part], proj_sems.at[m, k]
        )

    small = [
        pltpu.make_async_copy(source, target, small_sems.at[k])
        for k, (source, target) in enumerate(
            (
                (text_hbm, text_ref),
                (unembed_hbm, unembed_ref),
                (noise_hbm, noise_ref),
                (renoise_hbm, renoise_ref),
                (embed_hbm, embed_ref),
            )
        )
    ]
    order = []
    for m in range(3):
        order += [proj_piece(m, k) for k in range(PROJ_PIECES)]
        order += [mod_piece(m, k) for k in range(MOD_PIECES)]
    order = small[:2] + order[:LATENTS_AFTER] + small[2:4] + order[LATENTS_AFTER:] + small[4:]
    for copy in order[:IN_FLIGHT]:
        copy.start()

    def take(position):
        order[position].wait()
        if position + IN_FLIGHT < len(order):
            order[position + IN_FLIGHT].start()

    take(0)
    half_size = TEMB // 2
    place = lane_index((8, half_size)).astype(jnp.float32)
    frequency = jnp.exp(place * (-math.log(10000.0) / half_size))
    level = lax.broadcasted_iota(jnp.int32, (8, half_size), 0)
    steps = jnp.where(level == 0, gen_step_ref[0], renoise_step_ref[0]).astype(jnp.float32)
    angles = steps * frequency
    text = jnp.broadcast_to(text_ref[...].astype(jnp.float32), (8, text_ref.shape[1]))
    text = jnp.where(lax.broadcasted_iota(jnp.int32, text.shape, 0) < 2, text, 0.0)
    joined = jnp.concatenate([jnp.cos(angles), jnp.sin(angles), text], 1)
    vectors = (joined / (1.0 + jnp.exp(-joined))).astype(jnp.bfloat16)
    packs = width // PACK
    mod_ref[...] = jnp.zeros_like(mod_ref)
    take(1)
    place = 2
    for m in range(3):
        total = jnp.zeros((8, width), jnp.float32)
        for k in range(PROJ_PIECES + MOD_PIECES):
            if place == LATENTS_AFTER + 2:
                take(place)
                take(place + 1)
                half = noise_ref.shape[0]
                latents_ref[:half] = noise_ref[...].astype(jnp.bfloat16)
                latents_ref[half:] = renoise_ref[...].astype(jnp.bfloat16)
                place += 2
            take(place)
            place += 1
            if k < PROJ_PIECES:
                part = slice(k * proj_depth, (k + 1) * proj_depth)
                through_ref[m, :, part] = lax.dot_general(
                    unembed_ref[m],
                    proj_buffer[m, part],
                    CONTRACT_LAST,
                    preferred_element_type=jnp.float32,
                ).astype(jnp.bfloat16)
            else:
                part = slice((k - PROJ_PIECES) * mod_depth, (k - PROJ_PIECES + 1) * mod_depth)
                total += jnp.dot(
                    vectors[:, part], mod_buffer[m, part], preferred_element_type=jnp.float32
                )
        if m == 0:
            line = total[0:1]
        elif m == 1:
            line = GUIDANCE * total[1:2] + (1.0 - GUIDANCE) * total[2:3]
        else:
            line = total[1:2]
        for j in range(packs):
            mod_ref[m * packs + j : m * packs + j + 1] = line[:, j * PACK : (j + 1) * PACK]
    take(len(order) - 1)


def streamed_weights(
    gen_step, renoise_step, text, noise, renoise, mod_weight, proj_weight, unembed, embed
):
    depth, width = mod_weight.shape[1], mod_weight.shape[2] // 2
    rows, cols = proj_weight.shape[1:]
    pack_rows = -(-3 * width // PACK // 8) * 8
    return pl.pallas_call(
        stream_kernel,
        out_shape=[
            jax.ShapeDtypeStruct((pack_rows, PACK), jnp.float32),
            jax.ShapeDtypeStruct((2 * noise.shape[0], noise.shape[1]), jnp.bfloat16),
            jax.ShapeDtypeStruct((3, CH, rows), jnp.bfloat16),
            jax.ShapeDtypeStruct(noise.shape, noise.dtype),
            jax.ShapeDtypeStruct(renoise.shape, renoise.dtype),
            jax.ShapeDtypeStruct(unembed.shape, unembed.dtype),
            jax.ShapeDtypeStruct(embed.shape, embed.dtype),
        ],
        in_specs=[pl.BlockSpec(memory_space=pltpu.SMEM)] * 2
        + [pl.BlockSpec(memory_space=pltpu.HBM)] * 7,
        out_specs=whole_specs(7),
        scratch_shapes=[
            pltpu.VMEM(text.shape, text.dtype),
            pltpu.VMEM((3, depth, width), jnp.bfloat16),
            pltpu.VMEM((3, rows, cols), jnp.bfloat16),
            pltpu.SemaphoreType.DMA((3, MOD_PIECES)),
            pltpu.SemaphoreType.DMA((3, PROJ_PIECES)),
            pltpu.SemaphoreType.DMA((5,)),
        ],
        compiler_params=vmem_params(),
        name="stream_weights",
    )(
        gen_step,
        renoise_step,
        *(
            pltpu.with_memory_space_constraint(x, pltpu.HBM)
            for x in (text, noise, renoise, mod_weight, proj_weight, unembed, embed)
        ),
    )


def embed_kernel(embed_ref, unembed_ref, gram_ref, rows_ref, direct_ref):
    rows, cols = rows_ref.shape[2], unembed_ref.shape[2]
    f = lax.axis_index("fsdp")
    row_start = pl.multiple_of(f * rows, 128)
    col_start = pl.multiple_of(lax.axis_index("mp") * cols, 128)
    nothing = jnp.zeros((CH, cols), jnp.bfloat16)
    for m in range(3):
        whole = embed_ref[m].astype(jnp.float32)
        average = jnp.sum(whole, axis=1, keepdims=True) * (1.0 / D)
        rows_ref[m] = embed_ref[m, :, pl.ds(row_start, rows)].astype(jnp.float32) - average
        direct = lax.dot_general(
            embed_ref[m, :, pl.ds(col_start, cols)],
            jnp.concatenate([unembed_ref[m], nothing], 0),
            CONTRACT_LAST,
            preferred_element_type=jnp.float32,
        )
        direct_ref[m] = jnp.where(f == 0, direct, 0.0)
        pair = jnp.concatenate(split_two(whole - average), 0)
        product = lax.dot_general(pair, pair, CONTRACT_LAST, preferred_element_type=jnp.float32)
        product = product[:CH] + product[CH:]
        gram = (product + pltpu.roll(product, CH, 1)) * (1.0 / D)
        gram_ref[m] = jnp.concatenate(split_three(block_diagonal(gram, gram)), 1)


def embed_products(embed, unembed, rows):
    return pl.pallas_call(
        embed_kernel,
        out_shape=[
            jax.ShapeDtypeStruct((3, 2 * CH, 6 * CH), jnp.bfloat16),
            jax.ShapeDtypeStruct((3, CH, rows), jnp.float32),
            jax.ShapeDtypeStruct((3, CH, 2 * CH), jnp.float32),
        ],
        in_specs=whole_specs(2),
        out_specs=whole_specs(3),
        compiler_params=vmem_params(),
        cost_estimate=pl.CostEstimate(
            flops=6 * 128 * 128 * D, bytes_accessed=6 * CH * D, transcendentals=0
        ),
        name="embed_products",
    )(embed, unembed)


def pair_ones():
    shape = (2 * CH, 2 * CH)
    lanes = lane_index(shape)
    subs = lax.broadcasted_iota(jnp.int32, shape, 0)
    ones = jnp.where((lanes < CH) == (subs < CH), 1.0, 0.0).astype(jnp.bfloat16)
    return jnp.concatenate([ones, ones], 0)


def inverse_deviation(u, by_gram, ones):
    squares = jnp.concatenate(split_two(by_gram * u), 1)
    spread = jnp.dot(squares, ones, preferred_element_type=jnp.float32)
    return lax.rsqrt(jnp.maximum(spread, 0.0) + EPS_NORM)


def columns(product, i):
    return product[:, i * 2 * CH : (i + 1) * 2 * CH]


def sample_latents(noise_ref, other_ref):
    half = noise_ref.shape[0]
    noise = jnp.concatenate([noise_ref[...].astype(jnp.bfloat16), other_ref[:half]], 0)
    return noise, other_ref[half:]


def noise_kernel(noise_ref, other_ref, gram_ref, inverse_ref, normal_ref):
    noise, _ = sample_latents(noise_ref, other_ref)
    product = jnp.dot(noise, gram_ref[0], preferred_element_type=jnp.float32)
    noise = noise.astype(jnp.float32)
    by_gram = columns(product, 0) + columns(product, 1) + columns(product, 2)
    inverse = inverse_deviation(noise, by_gram, pair_ones())
    inverse_ref[...] = inverse
    normal_ref[...] = (noise * inverse).astype(jnp.bfloat16)


def noise_statistics(noise, other, gram):
    shape = (2 * noise.shape[0], noise.shape[1])
    return pl.pallas_call(
        noise_kernel,
        out_shape=[
            jax.ShapeDtypeStruct(shape, jnp.float32),
            jax.ShapeDtypeStruct(shape, jnp.bfloat16),
        ],
        in_specs=whole_specs(3),
        out_specs=whole_specs(2),
        compiler_params=vmem_params(),
        name="noise_statistics",
    )(noise, other, gram)


def maps_kernel(kept_ref, got_ref, rows_ref, through_ref, direct_ref, maps_ref, mod_ref):
    rows = rows_ref.shape[2]
    packs = rows // PACK
    f = lax.axis_index("fsdp")
    kept, got = kept_ref[...], got_ref[...]
    shift = jnp.where(f == 0, kept, got)
    scale = jnp.where(f == 0, got, kept)
    offsets = []
    for m in range(3):
        pieces = []
        for j in range(packs):
            line = slice(m * packs + j, m * packs + j + 1)
            pieces.append(
                jnp.concatenate(
                    [
                        rows_ref[m, :, j * PACK : (j + 1) * PACK] * (1.0 + scale[line]),
                        shift[line],
                        jnp.zeros((7, PACK), jnp.float32),
                    ],
                    0,
                )
            )
        left = jnp.concatenate(pieces, 1).astype(jnp.bfloat16)
        through = jnp.concatenate([jnp.zeros((CH, rows), jnp.bfloat16), through_ref[m]], 0)
        product = lax.dot_general(
            left, through, CONTRACT_LAST, preferred_element_type=jnp.float32
        )
        maps_ref[m * CH : (m + 1) * CH] = (product[:CH] + direct_ref[m]).astype(jnp.bfloat16)
        offsets.append(product[CH : CH + 1])
    maps_ref[3 * CH :] = jnp.concatenate(
        offsets + [jnp.zeros((5, PACK), jnp.float32)], 0
    ).astype(jnp.bfloat16)
    rest = jnp.zeros((mod_ref.shape[0] - 2 * packs, PACK), jnp.float32)
    mod_ref[...] = jnp.concatenate([shift[:packs], scale[:packs], rest], 0).astype(jnp.bfloat16)


def modulated_maps(kept, got, rows_part, through, direct):
    packs = rows_part.shape[2] // PACK
    return pl.pallas_call(
        maps_kernel,
        out_shape=[
            jax.ShapeDtypeStruct((3 * CH + 8, 2 * CH), jnp.bfloat16),
            jax.ShapeDtypeStruct((-(-2 * packs // 16) * 16, PACK), jnp.bfloat16),
        ],
        in_specs=whole_specs(5),
        out_specs=whole_specs(2),
        compiler_params=vmem_params(),
        name="modulated_maps",
    )(kept, got, rows_part, through, direct)


MAP_ROWS = CH + 16


def token_kernel(
    level_ref,
    noise_ref,
    other_ref,
    renoise_ref,
    inverse_ref,
    normal_ref,
    gram_ref,
    maps_a,
    maps_b,
    maps_c,
    maps_d,
    mod_ref,
    score_ref,
    payload_ref,
):
    half = renoise_ref.shape[0]
    level = level_ref[0]
    maps = [part[...].astype(jnp.float32) for part in (maps_a, maps_b, maps_c, maps_d)]
    maps = (maps[0] + maps[1]) + (maps[2] + maps[3])
    width = 2 * CH
    ones = pair_ones()

    def model_matrix(m):
        base = m * CH
        pair = maps[base : base + CH]
        turned = pltpu.roll(pair, CH, 1)
        direct = block_diagonal(pair, turned)
        modulated = block_diagonal(turned, pair)
        matrix = jnp.concatenate([direct, modulated], 1).astype(jnp.bfloat16)
        offset = maps[3 * CH + m : 3 * CH + m + 1]
        return matrix, offset + pltpu.roll(offset, CH, 1)

    def combine(product, inverse, offset):
        return columns(product, 0) + inverse * columns(product, 1) + offset

    noise, other_renoise = sample_latents(noise_ref, other_ref)
    renoise = jnp.concatenate([renoise_ref[...], other_renoise.astype(jnp.float32)], 0)
    matrix, offset = model_matrix(0)
    product = jnp.dot(noise, matrix, preferred_element_type=jnp.float32)
    clean = combine(product, inverse_ref[...], offset)
    noisy = ((1.0 - level) * clean + level * renoise).astype(jnp.bfloat16)
    noisy_wide = noisy.astype(jnp.float32)

    def velocity(m):
        matrix, offset = model_matrix(m)
        matrix = jnp.concatenate([matrix, gram_ref[m]], 1)
        product = jnp.dot(noisy, matrix, preferred_element_type=jnp.float32)
        by_gram = columns(product, 2) + columns(product, 3) + columns(product, 4)
        return combine(product, inverse_deviation(noisy_wide, by_gram, ones), offset)

    real_v = velocity(1)
    fake_v = velocity(2)
    total = jnp.sum(jnp.abs(clean - renoise + real_v))
    gap_scale = level * total * (1.0 / (2 * half * width)) + EPS_GAP
    score = level * (real_v - fake_v) / gap_scale
    score_ref[...] = score[:half]
    tokens = 4 * half * lax.axis_size("dp")
    cotangent = (score * (1.0 / math.sqrt(tokens))).astype(jnp.bfloat16)
    pairs = lax.dot_general(
        normal_ref[...], cotangent, CONTRACT_FIRST, preferred_element_type=jnp.float32
    )
    outer = pairs[:CH] + pltpu.roll(pairs[CH:], CH, 1)
    sums = jnp.sum(cotangent.astype(jnp.float32), axis=0, keepdims=True)
    sums = sums + pltpu.roll(sums, CH, 1)
    rest = jnp.zeros((MAP_ROWS - CH - 1, width), jnp.float32)
    payload_ref[:MAP_ROWS] = jnp.concatenate([outer, sums, rest], 0).astype(jnp.bfloat16)
    payload_ref[MAP_ROWS:] = mod_ref[...]


def token_phase(level, noise, other, renoise, inverse, normal, gram, maps, mod):
    return pl.pallas_call(
        token_kernel,
        out_shape=[
            jax.ShapeDtypeStruct(renoise.shape, jnp.float32),
            jax.ShapeDtypeStruct((MAP_ROWS + mod.shape[0], 2 * CH), jnp.bfloat16),
        ],
        in_specs=[pl.BlockSpec(memory_space=pltpu.SMEM)] + whole_specs(11),
        out_specs=whole_specs(2),
        compiler_params=vmem_params(),
        name="tokens",
    )(level, noise, other, renoise, inverse, normal, gram, *maps, mod)


GRAD_PIECES = 6


def grad_kernel(
    block_a,
    block_b,
    block_c,
    block_d,
    rows_ref,
    unembed_ref,
    score_ref,
    grad_hbm,
    score_hbm,
    buffer,
    sems,
):
    score_copy = pltpu.make_async_copy(score_ref, score_hbm, sems.at[GRAD_PIECES])
    score_copy.start()
    rows = rows_ref.shape[2]
    packs = rows // PACK
    depth = rows // GRAD_PIECES
    blocks = [block[...] for block in (block_a, block_b, block_c, block_d)]
    left = jnp.concatenate([block[:MAP_ROWS, :CH] for block in blocks], 0)
    mods = [block[MAP_ROWS:].astype(jnp.float32) for block in blocks]
    unembed = unembed_ref[0]

    def piece(k):
        part = pl.ds(k * depth, depth)
        return pltpu.make_async_copy(buffer.at[part], grad_hbm.at[part], sems.at[k])

    tiles = []
    for j in range(packs):
        embed_tile = rows_ref[0, :, j * PACK : (j + 1) * PACK]
        column = []
        for mod in mods:
            column += [
                embed_tile * (1.0 + mod[packs + j : packs + j + 1]),
                mod[j : j + 1],
                jnp.zeros((MAP_ROWS - CH - 1, PACK), jnp.float32),
            ]
        tiles.append(jnp.concatenate(column, 0).astype(jnp.bfloat16))
    grad_map = lax.dot_general(
        left, jnp.concatenate(tiles, 1), CONTRACT_FIRST, preferred_element_type=jnp.float32
    ).astype(jnp.bfloat16)
    for k in range(GRAD_PIECES):
        part = slice(k * depth, (k + 1) * depth)
        buffer[part] = lax.dot_general(
            grad_map[:, part], unembed, CONTRACT_FIRST, preferred_element_type=jnp.float32
        )
        piece(k).start()
    for k in range(GRAD_PIECES):
        piece(k).wait()
    score_copy.wait()


def gradient(blocks, rows_part, unembed, score):
    rows = rows_part.shape[2]
    cols = unembed.shape[2]
    return pl.pallas_call(
        grad_kernel,
        out_shape=[
            jax.ShapeDtypeStruct((rows, cols), jnp.float32),
            jax.ShapeDtypeStruct(score.shape, jnp.float32),
        ],
        in_specs=whole_specs(7),
        out_specs=[pl.BlockSpec(memory_space=pl.ANY)] * 2,
        scratch_shapes=[
            pltpu.VMEM((rows, cols), jnp.float32),
            pltpu.SemaphoreType.DMA((GRAD_PIECES + 1,)),
        ],
        compiler_params=vmem_params(),
        name="gradient",
    )(*blocks, rows_part, unembed, score)


def body(
    gen_noise, renoise, gen_step, renoise_step, text_pooled, embed, mod_weight, proj_weight, unembed
):
    mine, latents, through, noise, renoise, unembed, embed = streamed_weights(
        gen_step,
        renoise_step,
        text_pooled,
        gen_noise[0],
        renoise[0],
        mod_weight,
        proj_weight,
        unembed,
        embed,
    )
    f = lax.axis_index("fsdp")
    theirs = swap(mine, "mp", 1)
    own_half = lax.axis_index("mp") % 2 == f
    kept = jnp.where(own_half, mine, theirs)
    sent = jnp.where(own_half, theirs, mine)
    sent, latents = lax.optimization_barrier((sent, latents))
    got = swap(sent, "fsdp", 1)
    other = swap(latents, "fsdp", 1)
    gram, rows_part, direct = embed_products(embed, unembed, proj_weight.shape[1])
    maps, mod = modulated_maps(kept, got, rows_part, through, direct)
    maps = maps.astype(jnp.float32) + swap(maps, "mp", 1).astype(jnp.float32)
    maps = maps.astype(jnp.bfloat16)
    maps = chip_blocks(maps)
    inverse, normal = noise_statistics(noise, other, gram)
    level = renoise_step.astype(jnp.float32) / 1000.0
    score, payload = token_phase(
        level, noise, other, renoise, inverse, normal, gram, maps, mod
    )
    blocks = gather_samples(payload)
    gen_grad, score_gap = gradient(blocks, rows_part, unembed, score)
    return (gen_grad, score_gap[None])


def fits_kernels(mesh):
    return mesh.shape["mp"] == 4 and mesh.shape["fsdp"] == 2 and mesh.shape["dp"] == 4


def solution(mesh):
    return jax.shard_map(
        body if fits_kernels(mesh) else plain_body,
        mesh=mesh,
        in_specs=(
            P("dp", "fsdp", None),
            P("dp", "fsdp", None),
            P("dp"),
            P("dp"),
            P("dp", None),
            P(),
            P(None, None, "fsdp"),
            P(None, "fsdp", "mp"),
            P(None, None, "mp"),
        ),
        out_specs=(P("fsdp", "mp"), P("dp", "fsdp", None)),
        check_vma=False,
    )
```
